32 devices in a mesh: dp: 8 (over z, y), mp: 4 (over x, core).
Axes of the slice: x: 2, y: 2, z: 4, core: 2. Of those that a mesh axis runs over, the one named last changes fastest.
Arguments:
- tokens: bfloat16 [16384, 1024], P('dp'), may hold values from -96 to 96
- doc_ids: int32 [16384], P('dp'), may hold values from 0 to 255, as said below
- ln_gain: float32 [1024], replicated, may hold values from 0.1 to 1.9
- w_query: bfloat16 [1024, 1024], P(None, 'mp'), may hold values from -16 to 16
- w_key: bfloat16 [1024, 1024], P(None, 'mp'), may hold values from -0.5 to 0.5
- w_value: bfloat16 [1024, 1024], P(None, 'mp'), may hold values from -0.1875 to 0.1875
- w_out: bfloat16 [1024, 1024], P('mp'), may hold values from -0.1875 to 0.1875
- centroids: float32 [8192, 1024], P('dp', 'mp'), may hold values from -6 to 6
- cluster_mass: float32 [8192], P('dp'), may hold values from 0.5 to 4
- assigned: int32 [256], P('dp'), may hold values from 0 to 8191, as said below
Outputs:
- doc_vectors: float32 [256, 1024], P('dp', 'mp')
- new_centroids: float32 [8192, 1024], P('dp', 'mp')
The draws below stay inside these ranges and needn't reach their ends.
Inputs may be any that keep to these rules, and one draw needn't show every extreme that they name: `doc_ids`: never falls along the positions. The documents that begin in row r (positions r * 2048 onward) have the ids r * 32 upward without gaps, from 24 to 32 of them, and some row has 32; ids of slots that no document takes never occur. A row begins with its own first document or with the rest of the last document begun in the row before, and row 0 begins with document 0; every document lies within the row where it begins and the next one. `assigned`: centroid c belongs to dp index c // 1024. Among the 32 slots of one row at most 5 name centroids of one dp index; in every row exactly 5 slots that hold documents name centroids of one dp index common to all rows.
All inputs are finite; a program needn't handle non-finite values.
Results may differ from the reference program's by a relative error of at most 0.0024.
Values sent between devices are 32-bit elements; how exact they have to be, the bound alone decides.
No kernel may reach another device: no remote copies, remote signals or barrier semaphores. Data moves between devices by JAX's collectives and lax.ppermute only.
A program may use at most 128 MiB of HBM per device.

```python
import math
import jax
import jax.numpy as jnp
from jax import lax

D = 1024
HEADS = 16
HEAD_DIM = 64
ROW_LEN = 2048
DOCS_ROW = 32
CENT_DEV = 1024
TOKENS = 16384
NDOCS = 256
CENTROIDS = 8192
CAP = 5


def draw_tokens(key, part):
    key_base, key_column, key_row = jax.random.split(jax.random.fold_in(key, 5), 3)
    base = jax.random.truncated_normal(key_base, -4.0, 4.0, (TOKENS, D), jnp.float32)
    row_scale = jnp.exp(jax.random.uniform(key_row, (TOKENS, 1), jnp.float32, math.log(0.5), math.log(2.0)))
    rising = jnp.exp(math.log(10.0) * jnp.arange(D, dtype=jnp.float32) / D)
    jiggle = jnp.exp(jax.random.uniform(key_column, (D,), jnp.float32, -0.35, 0.35))
    column_scale = 0.3 * rising * jiggle
    return (base * column_scale[None, :] * row_scale).astype(jnp.bfloat16)


def projection_pair(key):
    key_first, key_second = jax.random.split(jax.random.fold_in(key, 7), 2)
    w_key = jax.random.truncated_normal(key_first, -6.0, 6.0, (D, D), jnp.float32) / math.sqrt(D)
    w_key = jnp.clip(w_key, -0.5, 0.5)
    noise = jax.random.truncated_normal(key_second, -6.0, 6.0, (D, D), jnp.float32) / math.sqrt(D)
    w_query = noise
    w_query = jnp.clip(w_query, -16.0, 16.0)
    return (w_query, w_key)


def draw_w_query(key, part):
    return projection_pair(key)[0].astype(jnp.bfloat16)


def draw_w_key(key, part):
    return projection_pair(key)[1].astype(jnp.bfloat16)


def draw_doc_ids(key, part):
    row_count = TOKENS // ROW_LEN
    key_used, key_carry, key_jitter = jax.random.split(jax.random.fold_in(key, 11), 3)
    used_docs = jax.random.randint(key_used, (row_count,), 3 * DOCS_ROW // 4, DOCS_ROW + 1).at[0].set(DOCS_ROW)
    carry_len = jax.random.randint(key_carry, (row_count,), 0, ROW_LEN // 4).at[0].set(0)
    stride = (ROW_LEN - carry_len) // used_docs
    slot_index = jnp.arange(DOCS_ROW, dtype=jnp.int32)
    jitter = jax.random.randint(key_jitter, (row_count, DOCS_ROW), 0, jnp.maximum(stride // 2, 1)[:, None])
    jitter = jnp.where(slot_index[None, :] == 0, 0, jitter)
    starts = carry_len[:, None] + slot_index[None, :] * stride[:, None] + jitter
    starts = jnp.where(slot_index[None, :] < used_docs[:, None], starts, ROW_LEN)
    position = jnp.arange(ROW_LEN, dtype=jnp.int32)
    started = jnp.sum((position[None, :, None] >= starts[:, None, :]).astype(jnp.int32), axis=2)
    row_index = jnp.arange(row_count, dtype=jnp.int32)
    own_ids = row_index[:, None] * DOCS_ROW + started - 1
    prior_used = jnp.concatenate([used_docs[:1], used_docs[:-1]])
    previous = (row_index - 1) * DOCS_ROW + prior_used - 1
    ids_all = jnp.where(position[None, :] < carry_len[:, None], previous[:, None], own_ids)
    return ids_all.reshape(-1).astype(jnp.int32)


def draw_assigned(key, part):
    row_count = NDOCS // DOCS_ROW
    key_hot, key_order, key_offset, key_pick = jax.random.split(jax.random.fold_in(key, 23), 4)
    hot_owner = jax.random.randint(key_hot, (), 0, row_count)
    front = 3 * DOCS_ROW // 4
    order_keys = jax.random.split(key_order, row_count)
    orders = jax.vmap(lambda single: jax.random.permutation(single, front))(order_keys)
    slot_index = jnp.arange(DOCS_ROW, dtype=jnp.int32)
    chosen = jnp.sum((orders[:, :CAP][:, :, None] == slot_index[None, None, :]).astype(jnp.int32), axis=1) > 0
    others = jnp.cumsum(1 - chosen.astype(jnp.int32), axis=1) - 1
    offsets = jax.random.randint(key_offset, (row_count, 1), 0, row_count - 1)
    spread_owner = (hot_owner + 1 + (offsets + others) % (row_count - 1)) % row_count
    owners = jnp.where(chosen, hot_owner, spread_owner)
    picks = jax.random.randint(key_pick, (row_count, DOCS_ROW), 0, CENT_DEV)
    return (owners * CENT_DEV + picks).reshape(-1).astype(jnp.int32)


def block_levels(own_key, dims, cuts, least, top_value):
    def one(dim, parts):
        steps = jax.random.uniform(jax.random.fold_in(jax.random.fold_in(own_key, 6), dim), (parts,), jnp.float32, least / len(cuts), top_value / len(cuts))
        return jnp.repeat(jnp.exp(steps), dims[dim] // parts).reshape((-1,) + (1,) * (len(dims) - dim - 1))

    factor_of = one(*cuts[0])
    for cut in cuts[1:]:
        factor_of = factor_of * one(*cut)
    return factor_of


def bell_draw(own_key, extent, width, reach, pieces=(), held_as=jnp.bfloat16):
    drawn = jax.random.normal(own_key, extent, jnp.float32) * width
    if len(pieces) > 0:
        drawn = block_levels(own_key, extent, pieces, -0.22, 0.18) * drawn
    return jnp.clip(drawn, min=-reach, max=reach).astype(held_as)


def setup_inputs(seed: int = 0) -> dict:
    arg_keys = jax.random.split(jax.random.key(seed), 11)
    return {
        "tokens": draw_tokens(jax.random.fold_in(arg_keys[10], 71), 0),
        "doc_ids": draw_doc_ids(jax.random.fold_in(arg_keys[10], 71), 0),
        "ln_gain": jnp.clip(1.0 + 0.18 * jax.random.normal(arg_keys[2], (D,), jnp.float32), 0.1, 1.9),
        "w_query": draw_w_query(jax.random.fold_in(arg_keys[10], 71), 0),
        "w_key": draw_w_key(jax.random.fold_in(arg_keys[10], 71), 0),
        "w_value": bell_draw(arg_keys[5], (D, D), D ** -0.5, 0.1875, ((1, 4),)),
        "w_out": bell_draw(arg_keys[6], (D, D), D ** -0.5, 0.1875, ((0, 4),)),
        "centroids": bell_draw(arg_keys[7], (CENTROIDS, D), 1.0, 6.0, ((0, 8), (1, 4)), jnp.float32),
        "cluster_mass": jnp.clip(jnp.exp(math.log(4.0) - 2.0794415 * jax.random.uniform(arg_keys[8], (CENTROIDS,), jnp.float32) ** block_levels(arg_keys[8], (CENTROIDS,), ((0, 8),), -0.2, 0.2)), 0.5, 4.0),
        "assigned": draw_assigned(jax.random.fold_in(arg_keys[10], 71), 0),
    }


def layer_norm(tokens, ln_gain):
    widened = tokens.astype(jnp.float32)
    average = lax.optimization_barrier(jnp.mean(widened, axis=-1, keepdims=True))
    centered = widened - average
    variance = lax.optimization_barrier(jnp.mean(centered * centered, axis=-1, keepdims=True))
    return (centered * lax.rsqrt(variance + 1e-05) * ln_gain).astype(jnp.bfloat16)

def attend_block(queries, keys_all, values_all, query_ids, row_ids):
    scores = jnp.einsum('qhd,khd->hqk', queries.astype(jnp.float32), keys_all.astype(jnp.float32)) * (1.0 / math.sqrt(HEAD_DIM))
    same_doc = query_ids[:, None] == row_ids[None, :]
    scores = jnp.where(same_doc[None], scores, -1e+30)
    top_score = lax.optimization_barrier(jnp.max(scores, axis=-1, keepdims=True))
    raised = jnp.exp(scores - top_score)
    weights = (raised / lax.optimization_barrier(jnp.sum(raised, axis=-1, keepdims=True))).astype(jnp.bfloat16)
    return jnp.einsum('hqk,khd->qhd', weights.astype(jnp.float32), values_all.astype(jnp.float32)).astype(jnp.bfloat16)

def self_attention(normed, w_query, w_key, w_value, row_ids):
    length = normed.shape[0]

    def project(weight):
        return jnp.dot(normed, weight, preferred_element_type=jnp.float32).astype(jnp.bfloat16).reshape(length, HEADS, HEAD_DIM)
    queries = project(w_query)
    keys_all = project(w_key)
    values_all = project(w_value)
    block_rows = min(512, length)
    query_blocks = queries.reshape(length // block_rows, block_rows, HEADS, HEAD_DIM)
    id_blocks = row_ids.reshape(length // block_rows, block_rows)
    context = lax.map(lambda pair: attend_block(pair[0], keys_all, values_all, pair[1], row_ids), (query_blocks, id_blocks))
    return context.reshape(length, HEADS * HEAD_DIM)

def reference(tokens, doc_ids, ln_gain, w_query, w_key, w_value, w_out, centroids, cluster_mass, assigned):
    row_count = TOKENS // ROW_LEN
    token_rows = tokens.reshape(row_count, ROW_LEN, D)
    id_rows = doc_ids.reshape(row_count, ROW_LEN)

    def add_row(doc_sums, pair):
        row_tokens, row_ids = pair
        normed = layer_norm(row_tokens, ln_gain)
        context = self_attention(normed, w_query, w_key, w_value, row_ids)
        mixed = row_tokens.astype(jnp.float32) + jnp.dot(context, w_out, preferred_element_type=jnp.float32)
        return (doc_sums + jax.ops.segment_sum(mixed, row_ids, num_segments=NDOCS), jnp.float32(0.0))
    doc_sums, ignored = lax.scan(add_row, jnp.zeros((NDOCS, D), jnp.float32), (token_rows, id_rows))
    doc_counts = jax.ops.segment_sum(jnp.ones((TOKENS,), jnp.float32), doc_ids, num_segments=NDOCS)
    averages = doc_sums / jnp.maximum(doc_counts, 1.0)[:, None]
    doc_vectors = averages * lax.rsqrt(lax.optimization_barrier(jnp.mean(averages * averages, axis=1)) + 1e-06)[:, None]
    is_used = (doc_counts > 0).astype(jnp.float32)
    gained = jax.ops.segment_sum(doc_vectors * is_used[:, None], assigned, num_segments=CENTROIDS)
    members = jax.ops.segment_sum(is_used, assigned, num_segments=CENTROIDS)
    blended = cluster_mass[:, None] * centroids + gained
    scaled = blended * lax.rsqrt(lax.optimization_barrier(jnp.mean(blended * blended, axis=1)) + 1e-06)[:, None]
    new_centroids = jnp.where((members > 0)[:, None], scaled, centroids)
    return (doc_vectors, new_centroids)
```

```python
import functools
import math

import jax
import jax.numpy as jnp
from jax import lax
from jax.experimental import pallas as pl
from jax.experimental.pallas import tpu as pltpu
from jax.sharding import PartitionSpec as P

D = 1024
HEAD_DIM = 64
QB = 128
GROUP = 4
SLOTS = 48
LANES = 128
BF = jnp.bfloat16
F32 = jnp.float32

NN = (((1,), (0,)), ((), ()))
NT = (((1,), (1,)), ((), ()))
TN = (((0,), (0,)), ((), ()))


def dot(a, b, dims=NN, precision=None):
    return lax.dot_general(a, b, dims, preferred_element_type=F32, precision=precision)


def iota(shape, dim):
    return lax.broadcasted_iota(jnp.int32, shape, dim)


def thirds(x):
    first = x.astype(BF)
    rest = x - first.astype(F32)
    second = rest.astype(BF)
    third = (rest - second.astype(F32)).astype(BF)
    return first, second, third


def pick_rows(one_hot, x, dims=NN):
    first, second, third = thirds(x)
    return dot(one_hot, first, dims) + (dot(one_hot, second, dims) + dot(one_hot, third, dims))


def round_up(n, by):
    return (n + by - 1) // by * by


def row_kernel(
    sizes, ids_hbm, assigned_hbm, gain_hbm, x_hbm, wq_hbm, wk_hbm, wv_hbm, wo_hbm, out_ref,
    ids_ref, ids_sm, assigned_sm, gain_ref, x_ref, w_ref, wo_ref, normed_ref, q_ref, k_ref, v_ref,
    slot_ref, slot_rows_ref, windows_sm, place_ref, meta_ref, acc_ref, part_ref, small_sems, x_sems, w_sems,
):
    length, tile, slots, capacity, block_rows, dp, mp, width, cents = sizes
    tiles = length // tile
    blocks_all = length // QB
    rows = dp * block_rows
    row = lax.axis_index("dp")
    column = lax.axis_index("mp")
    pairs = width // LANES

    small_copies = [
        pltpu.make_async_copy(ids_hbm, ids_ref, small_sems.at[0]),
        pltpu.make_async_copy(ids_hbm, ids_sm, small_sems.at[1]),
        pltpu.make_async_copy(assigned_hbm, assigned_sm, small_sems.at[2]),
        pltpu.make_async_copy(gain_hbm, gain_ref, small_sems.at[3]),
    ]
    x_copies = [
        pltpu.make_async_copy(x_hbm.at[pl.ds(i * tile, tile), :], x_ref.at[pl.ds(i * tile, tile), :], x_sems.at[i])
        for i in range(tiles)
    ]
    w_copies = [
        pltpu.make_async_copy(w_hbm, w_ref.at[:, pl.ds(i * width, width)], w_sems.at[i])
        for i, w_hbm in enumerate((wq_hbm, wk_hbm, wv_hbm))
    ] + [pltpu.make_async_copy(wo_hbm, wo_ref, w_sems.at[3])]
    for copy in small_copies + x_copies[:1] + w_copies[:3] + x_copies[1:] + w_copies[3:]:
        copy.start()
    for copy in small_copies:
        copy.wait()

    ids = ids_ref[...]
    local = ids - row * slots
    slot_rows = jnp.where(local < 0, slots, local).astype(F32)
    slot_rows_ref[...] = slot_rows
    on_diagonal = iota((LANES, LANES), 0) == iota((LANES, LANES), 1)
    ones = jnp.ones((LANES, LANES), BF)
    counts = jnp.zeros((8, LANES), F32)
    for block in range(blocks_all):
        slot = slot_rows[block:block + 1, :]
        diagonal = jnp.where(on_diagonal, slot, 0.0).astype(BF)
        slot_ref[block * LANES:(block + 1) * LANES, :] = dot(diagonal, ones)
        member = (iota((LANES, LANES), 0).astype(F32) == slot).astype(F32).astype(BF)
        counts += dot(ones[:8], member, NT)

    for block in range(blocks_all):
        first = ids_sm[block, 0]
        last = ids_sm[block, QB - 1]
        begin = jnp.sum((ids < first).astype(F32)).astype(jnp.int32)
        end = jnp.sum((ids <= last).astype(F32)).astype(jnp.int32)
        windows_sm[0, block] = (begin // 16) * 16
        windows_sm[1, block] = end

    lane = iota((1, LANES), 1)
    named = jnp.full((1, LANES), -1, jnp.int32)
    owner = jnp.full((1, LANES), -1, jnp.int32)
    for j in range(slots):
        name = assigned_sm[0, j]
        named = jnp.where(lane == j, name, named)
        owner = jnp.where(lane == j, name // cents, owner)
    wide = jnp.broadcast_to(owner.astype(F32), (LANES, LANES))
    earlier = (wide.T == wide) & (iota((LANES, LANES), 0) < iota((LANES, LANES), 1))
    rank = jnp.sum(earlier.astype(F32), axis=0, keepdims=True)
    goes_to = jnp.where(lane < slots, owner.astype(F32) * block_rows + rank, -1.0)
    row_of = iota((rows, LANES), 0)
    place = (row_of.astype(F32) == goes_to) | (
        (row_of % block_rows == capacity) & (iota((rows, LANES), 1) == slots)
    )
    place_ref[...] = place.astype(F32).astype(BF)
    last_slot = ids_sm[blocks_all - 1, QB - 1] - row * slots
    speaks = (column == 0).astype(F32)
    meta_ref[0:1, :LANES] = goes_to * speaks
    meta_ref[0:1, LANES:] = counts[:1] * speaks
    meta_ref[1:2, :LANES] = named.astype(F32) * speaks
    meta_ref[1:2, LANES:] = (lane == last_slot).astype(F32) * speaks
    part_ref[...] = jnp.zeros_like(part_ref)
    acc_ref[...] = jnp.zeros_like(acc_ref)

    own = pl.ds(pl.multiple_of(column * width, width), width)
    gain = gain_ref[...]
    piece_rows = 32

    def normalise(i):
        x_copies[i].wait()
        for piece in range(tile // piece_rows):
            at = i * tile + piece * piece_rows
            widened = x_ref[at:at + piece_rows, :].astype(F32)
            centered = widened - jnp.mean(widened, axis=1, keepdims=True)
            variance = jnp.mean(centered * centered, axis=1, keepdims=True)
            scaled = (centered * lax.rsqrt(variance + 1e-05) * gain).astype(BF)
            normed_ref[i % 2, piece * piece_rows:(piece + 1) * piece_rows, :] = scaled

    def project(i):
        here = slice(i * tile, (i + 1) * tile)
        both = dot(normed_ref[i % 2], w_ref[...])
        q_ref[here, :] = (both[:, :width] * (1.0 / math.sqrt(HEAD_DIM))).astype(BF)
        k_ref[here, :] = both[:, width:2 * width].astype(BF)
        v_ref[here, :] = both[:, 2 * width:].astype(BF)
        slot = jnp.concatenate(
            [slot_rows_ref[b:b + 1, :] for b in range(i * tile // LANES, (i + 1) * tile // LANES)], axis=1
        )
        member = (iota((SLOTS, tile), 0).astype(F32) == slot).astype(F32).astype(BF)
        return dot(member, x_ref[here, own])

    tokens_sum = jnp.zeros((SLOTS, width), F32)
    normalise(0)
    for copy in w_copies[:3]:
        copy.wait()
    for i in range(1, tiles):
        normalise(i)
        tokens_sum += project(i - 1)
    tokens_sum += project(tiles - 1)
    part_ref[:SLOTS, own] = tokens_sum

    low_head = iota((QB, LANES), 1) < HEAD_DIM

    def two_heads(block, pair):
        both = q_ref[pl.ds(pl.multiple_of(block * QB, QB), QB), pair * LANES:(pair + 1) * LANES]
        zero = jnp.zeros_like(both)
        return jnp.concatenate(
            [jnp.where(low_head, both, zero), jnp.where(low_head, zero, both)], axis=0
        )

    def query_slots(block):
        return slot_rows_ref[pl.ds(block, 1), :]

    def masked_scores(block, pair, at, extent):
        keys = k_ref[pl.ds(at, extent), pair * LANES:(pair + 1) * LANES]
        scores = dot(keys, two_heads(block, pair), NT)
        same = slot_ref[pl.ds(at, extent), :] == query_slots(block)
        same = jnp.concatenate([same, same], axis=1)
        return jnp.where(same, scores, -1e30)

    def pooled_shares(block, raised, inverse):
        member = iota((SLOTS, QB), 0).astype(F32) == query_slots(block)
        zero = jnp.zeros((SLOTS, QB), F32)
        left = jnp.concatenate([jnp.where(member, inverse[:, :QB], 0.0), zero], axis=1)
        right = jnp.concatenate([zero, jnp.where(member, inverse[:, QB:], 0.0)], axis=1)
        shares = jnp.concatenate([left, right], axis=0).astype(BF)
        return dot(shares, raised.astype(BF), NT).astype(BF)

    def values_at(pair, at, extent):
        return v_ref[pl.ds(at, extent), pair * LANES:(pair + 1) * LANES]

    def straight(blocks, begins, extent):
        ats = [pl.multiple_of(jnp.minimum(begin, length - extent), 16) for begin in begins]
        for pair in range(pairs):
            chains = list(zip(blocks, ats))
            scores = [masked_scores(block, pair, at, extent) for block, at in chains]
            raised = [jnp.exp(s - jnp.max(s, axis=0, keepdims=True)) for s in scores]
            inverse = [1.0 / jnp.sum(r, axis=0, keepdims=True) for r in raised]
            shares = [pooled_shares(block, r, v) for block, r, v in zip(blocks, raised, inverse)]
            total = [dot(share, values_at(pair, at, extent)) for share, at in zip(shares, ats)]
            acc_ref[pair] += functools.reduce(jnp.add, total)

    def any_length(block):
        chunk = 256
        first_chunk = windows_sm[0, block] // chunk
        end_chunk = (windows_sm[1, block] + chunk - 1) // chunk
        for pair in range(pairs):

            def scores_at(index):
                at = pl.multiple_of(index * chunk, chunk)
                return at, masked_scores(block, pair, at, chunk)

            def forward(index, carry):
                top, total = carry
                _, scores = scores_at(index)
                higher = jnp.maximum(top, jnp.max(scores, axis=0, keepdims=True))
                raised = jnp.sum(jnp.exp(scores - higher), axis=0, keepdims=True)
                return higher, total * jnp.exp(top - higher) + raised

            top, total = lax.fori_loop(
                first_chunk, end_chunk, forward,
                (jnp.full((1, 2 * QB), -1e30, F32), jnp.zeros((1, 2 * QB), F32)),
            )
            inverse = 1.0 / total

            def again(index, nothing):
                at, scores = scores_at(index)
                raised = jnp.exp(scores - top)
                acc_ref[pair] += dot(pooled_shares(block, raised, inverse), values_at(pair, at, chunk))
                return nothing

            lax.fori_loop(first_chunk, end_chunk, again, 0)

    def group_step(group, nothing):
        blocks = [group * GROUP + i for i in range(GROUP)]
        begins = [windows_sm[0, block] for block in blocks]
        widest = functools.reduce(
            jnp.maximum, [windows_sm[1, block] - begin for block, begin in zip(blocks, begins)]
        )
        done = jnp.int32(0)
        for extent in (256, 384, 640):
            if extent > length:
                break

            @pl.when((widest > done) & (widest <= extent))
            def run(extent=extent):
                straight(blocks, begins, extent)

            done = jnp.int32(extent)

        @pl.when(widest > done)
        def slow():
            def one(index, nothing):
                any_length(group * GROUP + index)
                return nothing

            lax.fori_loop(0, GROUP, one, 0)

        return nothing

    lax.fori_loop(0, blocks_all // GROUP, group_step, 0)

    low = iota((SLOTS, LANES), 1) < HEAD_DIM
    context = jnp.concatenate(
        [jnp.where(low, acc_ref[pair, :SLOTS], acc_ref[pair, SLOTS:]) for pair in range(pairs)], axis=1
    )
    upper = context.astype(BF)
    lower = (context - upper.astype(F32)).astype(BF)
    w_copies[3].wait()
    part_ref[:SLOTS, :] += dot(upper, wo_ref[...]) + dot(lower, wo_ref[...])
    sent = pick_rows(place_ref[...], part_ref[...])
    row_wide = iota((rows, 2 * LANES), 0) % block_rows
    for target in range(mp):
        piece = sent[:, target * width:(target + 1) * width]
        piece = jnp.where(row_wide == capacity + 1, meta_ref[0:1, :], piece)
        out_ref[target] = jnp.where(row_wide == capacity + 2, meta_ref[1:2, :], piece)


def row_sums(doc_ids, assigned, tokens, ln_gain, w_query, w_key, w_value, w_out, sizes):
    length, tile, slots, capacity, block_rows, dp, mp, width, cents = sizes
    rows = dp * block_rows
    return pl.pallas_call(
        functools.partial(row_kernel, sizes),
        in_specs=[pl.BlockSpec(memory_space=pltpu.HBM)] * 8,
        out_shape=jax.ShapeDtypeStruct((mp, rows, width), F32),
        scratch_shapes=[
            pltpu.VMEM((length // LANES, LANES), jnp.int32),
            pltpu.SMEM((length // LANES, LANES), jnp.int32),
            pltpu.SMEM((1, slots), jnp.int32),
            pltpu.VMEM((1, D), F32),
            pltpu.VMEM((length, D), BF),
            pltpu.VMEM((D, 3 * width), BF),
            pltpu.VMEM((width, D), BF),
            pltpu.VMEM((2, tile, D), BF),
            pltpu.VMEM((length, width), BF),
            pltpu.VMEM((length, width), BF),
            pltpu.VMEM((length, width), BF),
            pltpu.VMEM((length, LANES), F32),
            pltpu.VMEM((length // LANES, LANES), F32),
            pltpu.SMEM((2, length // QB), jnp.int32),
            pltpu.VMEM((rows, LANES), BF),
            pltpu.VMEM((8, 2 * LANES), F32),
            pltpu.VMEM((width // LANES, 2 * SLOTS, LANES), F32),
            pltpu.VMEM((LANES, D), F32),
            pltpu.SemaphoreType.DMA((4,)),
            pltpu.SemaphoreType.DMA((length // tile,)),
            pltpu.SemaphoreType.DMA((4,)),
        ],
        compiler_params=pltpu.CompilerParams(vmem_limit_bytes=48 * 1024 * 1024),
        name="row_sums",
    )(
        doc_ids.reshape(length // LANES, LANES), assigned.reshape(1, slots), ln_gain.reshape(1, D),
        tokens, w_query, w_key, w_value, w_out,
    )


def products_kernel(
    sizes, here_ref, own_ref, cent_ref, mass_ref, pay_ref, docs_ref, near_ref, info_ref, own_out_ref
):
    length, tile, slots, capacity, block_rows, dp, mp, width, cents = sizes
    me = lax.axis_index("dp")
    rows = dp * block_rows
    lane = iota((1, LANES), 1)

    def rows_of(meta, first_row, count):
        goes_to, counts = meta[0:1, :LANES], meta[0:1, LANES:]
        named, is_last = meta[1:2, :LANES], meta[1:2, LANES:]
        held = (goes_to == (iota((count, LANES), 0) + first_row).astype(F32)).astype(F32)

        def column(values):
            return jnp.sum(held * values, axis=1, keepdims=True)

        return column(named), column(counts), column(is_last), column(jnp.ones((1, LANES), F32))

    def carry_of(source):
        block = here_ref[pl.ds(pl.multiple_of(source * block_rows, 8), block_rows), :]
        counts = block[capacity + 1:capacity + 2, LANES:]
        count = jnp.sum(jnp.where(lane == slots, counts, 0.0), axis=1, keepdims=True)
        return block[capacity:capacity + 1, :], count

    columns = []
    for source in range(dp):
        base = source * block_rows
        block = here_ref[base:base + block_rows, :]
        meta = block[capacity + 1:capacity + 3, :]
        named, counts, is_last, held = rows_of(meta, me * block_rows, block_rows)
        sums = jnp.where(held > 0, block, 0.0)
        if source < dp - 1:
            carry, carry_count = carry_of(source + 1)
            sums = sums + is_last * carry
            counts = counts + is_last * carry_count
        docs_ref[base:base + block_rows, :] = sums
        columns.append((named - (me * cents).astype(F32), counts, held))
    local = jnp.concatenate([c[0] for c in columns], axis=0)
    counts = jnp.concatenate([c[1] for c in columns], axis=0)
    held = jnp.concatenate([c[2] for c in columns], axis=0)
    valid = ((held > 0) & (counts > 0)).astype(F32)

    docs = docs_ref[...]
    names = (iota((rows, cents), 1).astype(F32) == local) & (valid > 0)
    names = names.astype(F32)
    mass = jnp.sum(names * mass_ref[...], axis=1, keepdims=True)
    near = pick_rows(names.astype(BF), cent_ref[...])
    near_ref[...] = near

    own = own_ref[...]
    _, own_counts, own_last, _ = rows_of(own_ref[capacity + 1:capacity + 3, :], 0, rows)
    following = jnp.minimum(me + 1, dp - 1)
    more = (me < dp - 1).astype(F32)
    carry, carry_count = carry_of(following)
    own = own + own_last * (carry * more)
    own_counts = own_counts + own_last * (carry_count * more)
    own_out_ref[...] = own

    gram = dot(docs, docs, NT, precision=lax.Precision.HIGHEST)
    spot = iota((rows, LANES), 1)
    cross = jnp.sum(near * docs, axis=1, keepdims=True)
    square = jnp.sum(near * near, axis=1, keepdims=True)
    own_square = jnp.sum(own * own, axis=1, keepdims=True)
    doc_square = jnp.sum(docs * docs, axis=1, keepdims=True)
    for target in range(mp):
        pay_ref[target] = jnp.zeros(pay_ref.shape[1:], F32)
        pay_ref[target, :, :rows] = gram
        for i, sums in enumerate((cross, square, own_square, doc_square)):
            pay_ref[target, :, rows + i:rows + i + 1] = sums
    info_ref[...] = jnp.where(
        spot == 0, local, jnp.where(spot == 1, counts, jnp.where(spot == 2, valid, jnp.where(spot == 3, mass, own_counts)))
    )


def update_kernel(
    sizes, pay_ref, docs_ref, near_ref, info_ref, own_ref, meta_ref, cent_ref, vec_ref, new_ref
):
    length, tile, slots, capacity, block_rows, dp, mp, width, cents = sizes
    rows = dp * block_rows
    info = info_ref[...]
    local, counts, valid, mass, own_counts = (info[:, i:i + 1] for i in range(5))
    pay = functools.reduce(jnp.add, [pay_ref[i] for i in range(mp)])
    cross, square, own_square, doc_square = (pay[:, rows + i:rows + i + 1] for i in range(4))

    def scale(sums, count):
        inverse = 1.0 / jnp.maximum(count, 1.0)
        return inverse * lax.rsqrt(sums * inverse * inverse * (1.0 / D) + 1e-06)

    vectors = own_ref[...] * scale(own_square, own_counts)
    goes_to = meta_ref[capacity + 1:capacity + 2, :LANES]
    place = ((iota((rows, LANES), 0).astype(F32) == goes_to).astype(F32)).T
    vec_ref[...] = pick_rows(place[:slots].astype(BF), vectors)

    share = scale(doc_square, counts) * valid
    across = jnp.where(valid > 0, local, -1.0)
    flat = jnp.broadcast_to(across, (rows, LANES)).T[:1]
    share_flat = jnp.broadcast_to(share, (rows, LANES)).T[:1]
    cross_flat = jnp.broadcast_to(cross, (rows, LANES)).T[:1]
    same = (across == flat) & (valid > 0)
    mixed = jnp.where(same, share_flat, 0.0)
    gained = dot(mixed, docs_ref[...], precision=lax.Precision.HIGHEST)
    twice = dot(mixed, pay[:, :rows], precision=lax.Precision.HIGHEST)
    norm = (
        mass * mass * square
        + 2.0 * mass * jnp.sum(mixed * cross_flat, axis=1, keepdims=True)
        + jnp.sum(twice * mixed, axis=1, keepdims=True)
    )
    blended = mass * near_ref[...] + gained
    scaled = blended * lax.rsqrt(norm * (1.0 / D) + 1e-06)
    before = same & (iota((rows, rows), 0) < iota((rows, rows), 1))
    repeated = jnp.sum(before.astype(F32), axis=0, keepdims=True)
    target = jnp.where((flat >= 0) & (repeated < 0.5), flat, -1.0)
    hits = (iota((cents, rows), 0).astype(F32) == target).astype(F32)
    updated = pick_rows(hits.astype(BF), scaled)
    hit = jnp.sum(hits, axis=1, keepdims=True)
    new_ref[...] = jnp.where(hit > 0, updated, cent_ref[...])


def shards(
    tokens, doc_ids, ln_gain, w_query, w_key, w_value, w_out, centroids, cluster_mass, assigned
):
    length = tokens.shape[0]
    slots = assigned.shape[0]
    width = w_out.shape[0]
    cents = centroids.shape[0]
    dp = lax.axis_size("dp")
    mp = lax.axis_size("mp")
    capacity = max(2, (slots + dp - 2) // (dp - 1))
    block_rows = round_up(capacity + 3, 8)
    rows = dp * block_rows
    sizes = (length, min(256, length), slots, capacity, block_rows, dp, mp, width, cents)
    limit = pltpu.CompilerParams(vmem_limit_bytes=48 * 1024 * 1024)

    partial = row_sums(doc_ids, assigned, tokens, ln_gain, w_query, w_key, w_value, w_out, sizes)
    shared = lax.all_to_all(partial, "mp", split_axis=0, concat_axis=0, tiled=True)
    own = jnp.sum(shared, axis=0)
    here = lax.all_to_all(own, "dp", split_axis=0, concat_axis=0, tiled=True)

    pay, docs, near, info, own_sums = pl.pallas_call(
        functools.partial(products_kernel, sizes),
        out_shape=(
            jax.ShapeDtypeStruct((mp, rows, round_up(rows + 4, LANES)), F32),
            jax.ShapeDtypeStruct((rows, width), F32),
            jax.ShapeDtypeStruct((rows, width), F32),
            jax.ShapeDtypeStruct((rows, LANES), F32),
            jax.ShapeDtypeStruct((rows, width), F32),
        ),
        compiler_params=limit,
        name="products",
    )(here, own, centroids, cluster_mass.reshape(1, cents))
    pay = lax.all_to_all(pay, "mp", split_axis=0, concat_axis=0, tiled=True)
    return pl.pallas_call(
        functools.partial(update_kernel, sizes),
        out_shape=(
            jax.ShapeDtypeStruct((slots, width), F32),
            jax.ShapeDtypeStruct((cents, width), F32),
        ),
        compiler_params=limit,
        name="update",
    )(pay, docs, near, info, own_sums, own, centroids)


def solution(mesh):
    placed = (
        P("dp", None),
        P("dp"),
        P(),
        P(None, "mp"),
        P(None, "mp"),
        P(None, "mp"),
        P("mp", None),
        P("dp", "mp"),
        P("dp"),
        P("dp"),
    )
    return jax.shard_map(
        shards,
        mesh=mesh,
        in_specs=placed,
        out_specs=(P("dp", "mp"), P("dp", "mp")),
        check_vma=False,
    )
```

```python
import functools
import math

import jax
import jax.numpy as jnp
from jax import lax
from jax.experimental import pallas as pl
from jax.experimental.pallas import tpu as pltpu
from jax.sharding import PartitionSpec as P

D = 1024
HEAD_DIM = 64
QB = 128
GROUP = 4
SLOTS = 48
LANES = 128
BF = jnp.bfloat16
F32 = jnp.float32

NN = (((1,), (0,)), ((), ()))
NT = (((1,), (1,)), ((), ()))
TN = (((0,), (0,)), ((), ()))


def dot(a, b, dims=NN, precision=None):
    return lax.dot_general(a, b, dims, preferred_element_type=F32, precision=precision)


def iota(shape, dim):
    return lax.broadcasted_iota(jnp.int32, shape, dim)


def thirds(x):
    first = x.astype(BF)
    rest = x - first.astype(F32)
    second = rest.astype(BF)
    third = (rest - second.astype(F32)).astype(BF)
    return first, second, third


def pick_rows(one_hot, x, dims=NN):
    first, second, third = thirds(x)
    return dot(one_hot, first, dims) + (dot(one_hot, second, dims) + dot(one_hot, third, dims))


def round_up(n, by):
    return (n + by - 1) // by * by


def row_kernel(
    sizes, ids_hbm, assigned_hbm, gain_hbm, x_hbm, wq_hbm, wk_hbm, wv_hbm, wo_hbm, out_ref,
    ids_ref, ids_sm, assigned_sm, gain_ref, x_ref, w_ref, wo_ref, normed_ref, q_ref, k_ref, v_ref,
    slot_ref, slot_rows_ref, windows_sm, place_ref, meta_ref, acc_ref, part_ref, small_sems, x_sems, w_sems,
):
    length, tile, slots, capacity, block_rows, dp, mp, width, cents = sizes
    tiles = length // tile
    blocks_all = length // QB
    rows = dp * block_rows
    row = lax.axis_index("dp")
    column = lax.axis_index("mp")
    pairs = width // LANES

    small_copies = [
        pltpu.make_async_copy(ids_hbm, ids_ref, small_sems.at[0]),
        pltpu.make_async_copy(ids_hbm, ids_sm, small_sems.at[1]),
        pltpu.make_async_copy(assigned_hbm, assigned_sm, small_sems.at[2]),
        pltpu.make_async_copy(gain_hbm, gain_ref, small_sems.at[3]),
    ]
    x_copies = [
        pltpu.make_async_copy(x_hbm.at[pl.ds(i * tile, tile), :], x_ref.at[pl.ds(i * tile, tile), :], x_sems.at[i])
        for i in range(tiles)
    ]
    w_copies = [
        pltpu.make_async_copy(w_hbm, w_ref.at[:, pl.ds(i * width, width)], w_sems.at[i])
        for i, w_hbm in enumerate((wq_hbm, wk_hbm, wv_hbm))
    ] + [pltpu.make_async_copy(wo_hbm, wo_ref, w_sems.at[3])]
    for copy in small_copies + x_copies[:1] + w_copies[:3] + x_copies[1:] + w_copies[3:]:
        copy.start()
    for copy in small_copies:
        copy.wait()

    ids = ids_ref[...]
    local = ids - row * slots
    slot_rows = jnp.where(local < 0, slots, local).astype(F32)
    slot_rows_ref[...] = slot_rows
    on_diagonal = iota((LANES, LANES), 0) == iota((LANES, LANES), 1)
    ones = jnp.ones((LANES, LANES), BF)
    counts = jnp.zeros((8, LANES), F32)
    for block in range(blocks_all):
        slot = slot_rows[block:block + 1, :]
        diagonal = jnp.where(on_diagonal, slot, 0.0).astype(BF)
        slot_ref[block * LANES:(block + 1) * LANES, :] = dot(diagonal, ones)
        member = (iota((LANES, LANES), 0).astype(F32) == slot).astype(F32).astype(BF)
        counts += dot(ones[:8], member, NT)

    for block in range(blocks_all):
        first = ids_sm[block, 0]
        last = ids_sm[block, QB - 1]
        begin = jnp.sum((ids < first).astype(F32)).astype(jnp.int32)
        end = jnp.sum((ids <= last).astype(F32)).astype(jnp.int32)
        windows_sm[0, block] = (begin // 16) * 16
        windows_sm[1, block] = end

    lane = iota((1, LANES), 1)
    named = jnp.full((1, LANES), -1, jnp.int32)
    owner = jnp.full((1, LANES), -1, jnp.int32)
    for j in range(slots):
        name = assigned_sm[0, j]
        named = jnp.where(lane == j, name, named)
        owner = jnp.where(lane == j, name // cents, owner)
    wide = jnp.broadcast_to(owner.astype(F32), (LANES, LANES))
    earlier = (wide.T == wide) & (iota((LANES, LANES), 0) < iota((LANES, LANES), 1))
    rank = jnp.sum(earlier.astype(F32), axis=0, keepdims=True)
    goes_to = jnp.where(lane < slots, owner.astype(F32) * block_rows + rank, -1.0)
    row_of = iota((rows, LANES), 0)
    place = (row_of.astype(F32) == goes_to) | (
        (row_of % block_rows == capacity) & (iota((rows, LANES), 1) == slots)
    )
    place_ref[...] = place.astype(F32).astype(BF)
    last_slot = ids_sm[blocks_all - 1, QB - 1] - row * slots
    speaks = (column == 0).astype(F32)
    meta_ref[0:1, :LANES] = goes_to * speaks
    meta_ref[0:1, LANES:] = counts[:1] * speaks
    meta_ref[1:2, :LANES] = named.astype(F32) * speaks
    meta_ref[1:2, LANES:] = (lane == last_slot).astype(F32) * speaks
    part_ref[...] = jnp.zeros_like(part_ref)
    acc_ref[...] = jnp.zeros_like(acc_ref)

    own = pl.ds(pl.multiple_of(column * width, width), width)
    gain = gain_ref[...]
    piece_rows = 32

    def normalise(i):
        x_copies[i].wait()
        for piece in range(tile // piece_rows):
            at = i * tile + piece * piece_rows
            widened = x_ref[at:at + piece_rows, :].astype(F32)
            centered = widened - jnp.mean(widened, axis=1, keepdims=True)
            variance = jnp.mean(centered * centered, axis=1, keepdims=True)
            scaled = (centered * lax.rsqrt(variance + 1e-05) * gain).astype(BF)
            normed_ref[i % 2, piece * piece_rows:(piece + 1) * piece_rows, :] = scaled

    def project(i):
        here = slice(i * tile, (i + 1) * tile)
        both = dot(normed_ref[i % 2], w_ref[...])
        q_ref[here, :] = (both[:, :width] * (1.0 / math.sqrt(HEAD_DIM))).astype(BF)
        k_ref[here, :] = both[:, width:2 * width].astype(BF)
        v_ref[here, :] = both[:, 2 * width:].astype(BF)
        slot = jnp.concatenate(
            [slot_rows_ref[b:b + 1, :] for b in range(i * tile // LANES, (i + 1) * tile // LANES)], axis=1
        )
        member = (iota((SLOTS, tile), 0).astype(F32) == slot).astype(F32).astype(BF)
        return dot(member, x_ref[here, own])

    tokens_sum = jnp.zeros((SLOTS, width), F32)
    normalise(0)
    for copy in w_copies[:3]:
        copy.wait()
    for i in range(1, tiles):
        normalise(i)
        tokens_sum += project(i - 1)
    tokens_sum += project(tiles - 1)
    part_ref[:SLOTS, own] = tokens_sum

    low_head = iota((QB, LANES), 1) < HEAD_DIM

    def two_heads(block, pair):
        both = q_ref[pl.ds(pl.multiple_of(block * QB, QB), QB), pair * LANES:(pair + 1) * LANES]
        zero = jnp.zeros_like(both)
        return jnp.concatenate(
            [jnp.where(low_head, both, zero), jnp.where(low_head, zero, both)], axis=0
        )

    def query_slots(block):
        return slot_rows_ref[pl.ds(block, 1), :]

    def masked_scores(block, pair, at, extent):
        keys = k_ref[pl.ds(at, extent), pair * LANES:(pair + 1) * LANES]
        scores = dot(keys, two_heads(block, pair), NT)
        same = slot_ref[pl.ds(at, extent), :] == query_slots(block)
        same = jnp.concatenate([same, same], axis=1)
        return jnp.where(same, scores, -1e30)

    def pooled_shares(block, raised, inverse):
        member = iota((SLOTS, QB), 0).astype(F32) == query_slots(block)
        zero = jnp.zeros((SLOTS, QB), F32)
        left = jnp.concatenate([jnp.where(member, inverse[:, :QB], 0.0), zero], axis=1)
        right = jnp.concatenate([zero, jnp.where(member, inverse[:, QB:], 0.0)], axis=1)
        shares = jnp.concatenate([left, right], axis=0).astype(BF)
        return dot(shares, raised.astype(BF), NT).astype(BF)

    def values_at(pair, at, extent):
        return v_ref[pl.ds(at, extent), pair * LANES:(pair + 1) * LANES]

    def straight(blocks, begins, extent):
        ats = [pl.multiple_of(jnp.minimum(begin, length - extent), 16) for begin in begins]
        for pair in range(pairs):
            chains = list(zip(blocks, ats))
            scores = [masked_scores(block, pair, at, extent) for block, at in chains]
            raised = [jnp.exp(s - jnp.max(s, axis=0, keepdims=True)) for s in scores]
            inverse = [1.0 / jnp.sum(r, axis=0, keepdims=True) for r in raised]
            shares = [pooled_shares(block, r, v) for block, r, v in zip(blocks, raised, inverse)]
            total = [dot(share, values_at(pair, at, extent)) for share, at in zip(shares, ats)]
            acc_ref[pair] += functools.reduce(jnp.add, total)

    def any_length(block):
        chunk = 256
        first_chunk = windows_sm[0, block] // chunk
        end_chunk = (windows_sm[1, block] + chunk - 1) // chunk
        for pair in range(pairs):

            def scores_at(index):
                at = pl.multiple_of(index * chunk, chunk)
                return at, masked_scores(block, pair, at, chunk)

            def forward(index, carry):
                top, total = carry
                _, scores = scores_at(index)
                higher = jnp.maximum(top, jnp.max(scores, axis=0, keepdims=True))
                raised = jnp.sum(jnp.exp(scores - higher), axis=0, keepdims=True)
                return higher, total * jnp.exp(top - higher) + raised

            top, total = lax.fori_loop(
                first_chunk, end_chunk, forward,
                (jnp.full((1, 2 * QB), -1e30, F32), jnp.zeros((1, 2 * QB), F32)),
            )
            inverse = 1.0 / total

            def again(index, nothing):
                at, scores = scores_at(index)
                raised = jnp.exp(scores - top)
                acc_ref[pair] += dot(pooled_shares(block, raised, inverse), values_at(pair, at, chunk))
                return nothing

            lax.fori_loop(first_chunk, end_chunk, again, 0)

    def group_step(group, nothing):
        blocks = [group * GROUP + i for i in range(GROUP)]
        begins = [windows_sm[0, block] for block in blocks]
        widest = functools.reduce(
            jnp.maximum, [windows_sm[1, block] - begin for block, begin in zip(blocks, begins)]
        )
        done = jnp.int32(0)
        for extent in (256, 384, 640):
            if extent > length:
                break

            @pl.when((widest > done) & (widest <= extent))
            def run(extent=extent):
                straight(blocks, begins, extent)

            done = jnp.int32(extent)

        @pl.when(widest > done)
        def slow():
            def one(index, nothing):
                any_length(group * GROUP + index)
                return nothing

            lax.fori_loop(0, GROUP, one, 0)

        return nothing

    lax.fori_loop(0, blocks_all // GROUP, group_step, 0)

    low = iota((SLOTS, LANES), 1) < HEAD_DIM
    context = jnp.concatenate(
        [jnp.where(low, acc_ref[pair, :SLOTS], acc_ref[pair, SLOTS:]) for pair in range(pairs)], axis=1
    )
    upper = context.astype(BF)
    lower = (context - upper.astype(F32)).astype(BF)
    w_copies[3].wait()
    part_ref[:SLOTS, :] += dot(upper, wo_ref[...]) + dot(lower, wo_ref[...])
    sent = pick_rows(place_ref[...], part_ref[...])
    row_wide = iota((rows, 2 * LANES), 0) % block_rows
    for target in range(mp):
        piece = sent[:, target * width:(target + 1) * width]
        piece = jnp.where(row_wide == capacity + 1, meta_ref[0:1, :], piece)
        out_ref[target] = jnp.where(row_wide == capacity + 2, meta_ref[1:2, :], piece)


def row_sums(doc_ids, assigned, tokens, ln_gain, w_query, w_key, w_value, w_out, sizes):
    length, tile, slots, capacity, block_rows, dp, mp, width, cents = sizes
    rows = dp * block_rows
    return pl.pallas_call(
        functools.partial(row_kernel, sizes),
        in_specs=[pl.BlockSpec(memory_space=pltpu.HBM)] * 8,
        out_shape=jax.ShapeDtypeStruct((mp, rows, width), F32),
        scratch_shapes=[
            pltpu.VMEM((length // LANES, LANES), jnp.int32),
            pltpu.SMEM((length // LANES, LANES), jnp.int32),
            pltpu.SMEM((1, slots), jnp.int32),
            pltpu.VMEM((1, D), F32),
            pltpu.VMEM((length, D), BF),
            pltpu.VMEM((D, 3 * width), BF),
            pltpu.VMEM((width, D), BF),
            pltpu.VMEM((2, tile, D), BF),
            pltpu.VMEM((length, width), BF),
            pltpu.VMEM((length, width), BF),
            pltpu.VMEM((length, width), BF),
            pltpu.VMEM((length, LANES), F32),
            pltpu.VMEM((length // LANES, LANES), F32),
            pltpu.SMEM((2, length // QB), jnp.int32),
            pltpu.VMEM((rows, LANES), BF),
            pltpu.VMEM((8, 2 * LANES), F32),
            pltpu.VMEM((width // LANES, 2 * SLOTS, LANES), F32),
            pltpu.VMEM((LANES, D), F32),
            pltpu.SemaphoreType.DMA((4,)),
            pltpu.SemaphoreType.DMA((length // tile,)),
            pltpu.SemaphoreType.DMA((4,)),
        ],
        compiler_params=pltpu.CompilerParams(vmem_limit_bytes=62 * 1024 * 1024),
        name="row_sums",
    )(
        doc_ids.reshape(length // LANES, LANES), assigned.reshape(1, slots), ln_gain.reshape(1, D),
        tokens, w_query, w_key, w_value, w_out,
    )


def products_kernel(
    sizes, here_ref, own_ref, cent_ref, mass_ref, pay_ref, docs_ref, near_ref, info_ref, own_out_ref
):
    length, tile, slots, capacity, block_rows, dp, mp, width, cents = sizes
    me = lax.axis_index("dp")
    rows = dp * block_rows
    lane = iota((1, LANES), 1)

    def rows_of(meta, first_row, count):
        goes_to, counts = meta[0:1, :LANES], meta[0:1, LANES:]
        named, is_last = meta[1:2, :LANES], meta[1:2, LANES:]
        held = (goes_to == (iota((count, LANES), 0) + first_row).astype(F32)).astype(F32)

        def column(values):
            return jnp.sum(held * values, axis=1, keepdims=True)

        return column(named), column(counts), column(is_last), column(jnp.ones((1, LANES), F32))

    def carry_of(source):
        block = here_ref[pl.ds(pl.multiple_of(source * block_rows, 8), block_rows), :]
        counts = block[capacity + 1:capacity + 2, LANES:]
        count = jnp.sum(jnp.where(lane == slots, counts, 0.0), axis=1, keepdims=True)
        return block[capacity:capacity + 1, :], count

    columns = []
    for source in range(dp):
        base = source * block_rows
        block = here_ref[base:base + block_rows, :]
        meta = block[capacity + 1:capacity + 3, :]
        named, counts, is_last, held = rows_of(meta, me * block_rows, block_rows)
        sums = jnp.where(held > 0, block, 0.0)
        if source < dp - 1:
            carry, carry_count = carry_of(source + 1)
            sums = sums + is_last * carry
            counts = counts + is_last * carry_count
        docs_ref[base:base + block_rows, :] = sums
        columns.append((named - (me * cents).astype(F32), counts, held))
    local = jnp.concatenate([c[0] for c in columns], axis=0)
    counts = jnp.concatenate([c[1] for c in columns], axis=0)
    held = jnp.concatenate([c[2] for c in columns], axis=0)
    valid = ((held > 0) & (counts > 0)).astype(F32)

    docs = docs_ref[...]
    names = (iota((rows, cents), 1).astype(F32) == local) & (valid > 0)
    names = names.astype(F32)
    mass = jnp.sum(names * mass_ref[...], axis=1, keepdims=True)
    near = pick_rows(names.astype(BF), cent_ref[...])
    near_ref[...] = near

    own = own_ref[...]
    _, own_counts, own_last, _ = rows_of(own_ref[capacity + 1:capacity + 3, :], 0, rows)
    following = jnp.minimum(me + 1, dp - 1)
    more = (me < dp - 1).astype(F32)
    carry, carry_count = carry_of(following)
    own = own + own_last * (carry * more)
    own_counts = own_counts + own_last * (carry_count * more)
    own_out_ref[...] = own

    gram = dot(docs, docs, NT, precision=lax.Precision.HIGHEST)
    spot = iota((rows, LANES), 1)
    cross = jnp.sum(near * docs, axis=1, keepdims=True)
    square = jnp.sum(near * near, axis=1, keepdims=True)
    own_square = jnp.sum(own * own, axis=1, keepdims=True)
    doc_square = jnp.sum(docs * docs, axis=1, keepdims=True)
    for target in range(mp):
        pay_ref[target] = jnp.zeros(pay_ref.shape[1:], F32)
        pay_ref[target, :, :rows] = gram
        for i, sums in enumerate((cross, square, own_square, doc_square)):
            pay_ref[target, :, rows + i:rows + i + 1] = sums
    info_ref[...] = jnp.where(
        spot == 0, local, jnp.where(spot == 1, counts, jnp.where(spot == 2, valid, jnp.where(spot == 3, mass, own_counts)))
    )


def update_kernel(
    sizes, pay_ref, docs_ref, near_ref, info_ref, own_ref, meta_ref, cent_ref, vec_ref, new_ref
):
    length, tile, slots, capacity, block_rows, dp, mp, width, cents = sizes
    rows = dp * block_rows
    info = info_ref[...]
    local, counts, valid, mass, own_counts = (info[:, i:i + 1] for i in range(5))
    pay = functools.reduce(jnp.add, [pay_ref[i] for i in range(mp)])
    cross, square, own_square, doc_square = (pay[:, rows + i:rows + i + 1] for i in range(4))

    def scale(sums, count):
        inverse = 1.0 / jnp.maximum(count, 1.0)
        return inverse * lax.rsqrt(sums * inverse * inverse * (1.0 / D) + 1e-06)

    vectors = own_ref[...] * scale(own_square, own_counts)
    goes_to = meta_ref[capacity + 1:capacity + 2, :LANES]
    place = ((iota((rows, LANES), 0).astype(F32) == goes_to).astype(F32)).T
    vec_ref[...] = pick_rows(place[:slots].astype(BF), vectors)

    share = scale(doc_square, counts) * valid
    across = jnp.where(valid > 0, local, -1.0)
    flat = jnp.broadcast_to(across, (rows, LANES)).T[:1]
    share_flat = jnp.broadcast_to(share, (rows, LANES)).T[:1]
    cross_flat = jnp.broadcast_to(cross, (rows, LANES)).T[:1]
    same = (across == flat) & (valid > 0)
    mixed = jnp.where(same, share_flat, 0.0)
    gained = dot(mixed, docs_ref[...], precision=lax.Precision.HIGHEST)
    twice = dot(mixed, pay[:, :rows], precision=lax.Precision.HIGHEST)
    norm = (
        mass * mass * square
        + 2.0 * mass * jnp.sum(mixed * cross_flat, axis=1, keepdims=True)
        + jnp.sum(twice * mixed, axis=1, keepdims=True)
    )
    blended = mass * near_ref[...] + gained
    scaled = blended * lax.rsqrt(norm * (1.0 / D) + 1e-06)
    before = same & (iota((rows, rows), 0) < iota((rows, rows), 1))
    repeated = jnp.sum(before.astype(F32), axis=0, keepdims=True)
    target = jnp.where((flat >= 0) & (repeated < 0.5), flat, -1.0)
    hits = (iota((cents, rows), 0).astype(F32) == target).astype(F32)
    updated = pick_rows(hits.astype(BF), scaled)
    hit = jnp.sum(hits, axis=1, keepdims=True)
    new_ref[...] = jnp.where(hit > 0, updated, cent_ref[...])


def shards(
    tokens, doc_ids, ln_gain, w_query, w_key, w_value, w_out, centroids, cluster_mass, assigned
):
    length = tokens.shape[0]
    slots = assigned.shape[0]
    width = w_out.shape[0]
    cents = centroids.shape[0]
    dp = lax.axis_size("dp")
    mp = lax.axis_size("mp")
    capacity = max(2, (slots + dp - 2) // (dp - 1))
    block_rows = round_up(capacity + 3, 8)
    rows = dp * block_rows
    sizes = (length, min(256, length), slots, capacity, block_rows, dp, mp, width, cents)
    limit = pltpu.CompilerParams(vmem_limit_bytes=48 * 1024 * 1024)

    partial = row_sums(doc_ids, assigned, tokens, ln_gain, w_query, w_key, w_value, w_out, sizes)
    shared = lax.all_to_all(partial, "mp", split_axis=0, concat_axis=0, tiled=True)
    own = jnp.sum(shared, axis=0)
    here = lax.all_to_all(own, "dp", split_axis=0, concat_axis=0, tiled=True)

    pay, docs, near, info, own_sums = pl.pallas_call(
        functools.partial(products_kernel, sizes),
        out_shape=(
            jax.ShapeDtypeStruct((mp, rows, round_up(rows + 4, LANES)), F32),
            jax.ShapeDtypeStruct((rows, width), F32),
            jax.ShapeDtypeStruct((rows, width), F32),
            jax.ShapeDtypeStruct((rows, LANES), F32),
            jax.ShapeDtypeStruct((rows, width), F32),
        ),
        compiler_params=limit,
        name="products",
    )(here, own, centroids, cluster_mass.reshape(1, cents))
    pay = lax.all_to_all(pay, "mp", split_axis=0, concat_axis=0, tiled=True)
    return pl.pallas_call(
        functools.partial(update_kernel, sizes),
        out_shape=(
            jax.ShapeDtypeStruct((slots, width), F32),
            jax.ShapeDtypeStruct((cents, width), F32),
        ),
        compiler_params=limit,
        name="update",
    )(pay, docs, near, info, own_sums, own, centroids)


def solution(mesh):
    placed = (
        P("dp", None),
        P("dp"),
        P(),
        P(None, "mp"),
        P(None, "mp"),
        P(None, "mp"),
        P("mp", None),
        P("dp", "mp"),
        P("dp"),
        P("dp"),
    )
    return jax.shard_map(
        shards,
        mesh=mesh,
        in_specs=placed,
        out_specs=(P("dp", "mp"), P("dp", "mp")),
        check_vma=False,
    )
```

```python
import functools
import math

import jax
import jax.numpy as jnp
from jax import lax
from jax.experimental import pallas as pl
from jax.experimental.pallas import tpu as pltpu
from jax.sharding import PartitionSpec as P

D = 1024
HEAD_DIM = 64
QB = 64
GROUP = 8
LANES = 128
BF = jnp.bfloat16
F32 = jnp.float32

NN = (((1,), (0,)), ((), ()))
NT = (((1,), (1,)), ((), ()))
TN = (((0,), (0,)), ((), ()))


def dot(a, b, dims=NN, precision=None):
    return lax.dot_general(a, b, dims, preferred_element_type=F32, precision=precision)


def iota(shape, dim):
    return lax.broadcasted_iota(jnp.int32, shape, dim)


def thirds(x):
    first = x.astype(BF)
    rest = x - first.astype(F32)
    second = rest.astype(BF)
    third = (rest - second.astype(F32)).astype(BF)
    return first, second, third


def pick_rows(one_hot, x, dims=NN):
    first, second, third = thirds(x)
    return dot(one_hot, first, dims) + (dot(one_hot, second, dims) + dot(one_hot, third, dims))


def round_up(n, by):
    return (n + by - 1) // by * by


def row_kernel(
    sizes, ids_hbm, assigned_hbm, gain_hbm, x_hbm, wq_hbm, wk_hbm, wv_hbm, wo_hbm, out_ref,
    ids_ref, ids_sm, assigned_sm, gain_ref, x_ref, w_ref, wo_ref, normed_ref, q_ref, k_ref, v_ref,
    slot_ref, query_slots_ref, windows_ref, windows_sm, pool_ref, meta_ref, share_ref, small_sems, x_sems, w_sems,
):
    length, tile, slots, capacity, block_rows, dp, mp, width, cents = sizes
    tiles = length // tile
    lane_blocks = length // LANES
    rows = dp * block_rows
    heads = width // HEAD_DIM
    halves = width // LANES
    row = lax.axis_index("dp")
    column = lax.axis_index("mp")

    small_copies = [
        pltpu.make_async_copy(ids_hbm, ids_ref, small_sems.at[0]),
        pltpu.make_async_copy(ids_hbm, ids_sm, small_sems.at[1]),
        pltpu.make_async_copy(assigned_hbm, assigned_sm, small_sems.at[2]),
        pltpu.make_async_copy(gain_hbm, gain_ref, small_sems.at[3]),
    ]
    x_copies = [
        pltpu.make_async_copy(x_hbm.at[pl.ds(i * tile, tile), :], x_ref.at[pl.ds(i * tile, tile), :], x_sems.at[i])
        for i in range(tiles)
    ]
    w_copies = [
        pltpu.make_async_copy(w_hbm, w_ref.at[i], w_sems.at[i])
        for i, w_hbm in enumerate((wq_hbm, wk_hbm, wv_hbm))
    ] + [pltpu.make_async_copy(wo_hbm, wo_ref, w_sems.at[3])]
    for copy in small_copies + x_copies[:1]:
        copy.start()
    for copy in w_copies[:3]:
        copy.start(priority=1)
    for copy in x_copies[1:]:
        copy.start()
    w_copies[3].start(priority=1)
    for copy in small_copies:
        copy.wait()

    ids = ids_ref[...]
    local = ids - row * slots
    slot_rows = jnp.where(local < 0, slots, local).astype(F32)
    turned = pltpu.roll(slot_rows, QB, 1)
    front = iota(slot_rows.shape, 1) < QB
    query_slots_ref[0] = jnp.where(front, slot_rows, turned)
    query_slots_ref[1] = jnp.where(front, turned, slot_rows)

    lane = iota((1, LANES), 1)
    named = jnp.full((1, LANES), -1, jnp.int32)
    for j in range(slots):
        named = jnp.where(lane == j, assigned_sm[0, j], named)
    owner = named // cents
    wide = jnp.broadcast_to(owner.astype(F32), (LANES, LANES))
    earlier = (wide.T == wide) & (iota((LANES, LANES), 0) < iota((LANES, LANES), 1))
    rank = jnp.sum(earlier.astype(F32), axis=0, keepdims=True)
    goes_to = jnp.where(lane < slots, owner.astype(F32) * block_rows + rank, -1.0)
    row_of = iota((rows, LANES), 0)
    place = (row_of.astype(F32) == goes_to) | (
        (row_of % block_rows == capacity) & (iota((rows, LANES), 1) == slots)
    )
    place = place.astype(F32).astype(BF)

    on_diagonal = iota((LANES, LANES), 0) == iota((LANES, LANES), 1)
    ones = jnp.ones((LANES, LANES), BF)
    counts = []
    for block in range(lane_blocks):
        here = slice(block * LANES, (block + 1) * LANES)
        slot = slot_rows[block:block + 1, :]
        diagonal = jnp.where(on_diagonal, slot, 0.0).astype(BF)
        slot_ref[here, :] = dot(diagonal, ones)
        member = (iota((LANES, LANES), 0).astype(F32) == slot).astype(F32).astype(BF)
        counts.append(dot(ones[:8], member, NT))
        pool_ref[:, here] = dot(place, member).astype(BF)
    counts = functools.reduce(jnp.add, counts)

    def order(shape, dim):
        slot = iota(shape, dim)
        return jnp.where(slot == slots, 0, slot + 1)

    before = (order((LANES, LANES), 0) < order((LANES, LANES), 1)) & (iota((LANES, LANES), 0) <= slots)
    before = before.astype(F32).astype(BF)
    upper = counts.astype(BF)
    starts = dot(upper, before) + dot((counts - upper.astype(F32)).astype(BF), before)

    def at_position(values, position):
        mine = iota(slot_rows.shape, 1).astype(F32) == slot_rows[:, position:position + 1]
        return jnp.sum(jnp.where(mine, values[:1], 0.0), axis=1, keepdims=True)

    spot = iota(slot_rows.shape, 1)
    table = jnp.zeros(slot_rows.shape, F32)
    for part in range(LANES // QB):
        table = jnp.where(spot == 2 * part, at_position(starts, part * QB), table)
        table = jnp.where(spot == 2 * part + 1, at_position(starts + counts, (part + 1) * QB - 1), table)
    windows_ref[...] = table.astype(jnp.int32)
    windows_copy = pltpu.make_async_copy(windows_ref, windows_sm, small_sems.at[4])
    windows_copy.start()

    last_slot = ids_sm[lane_blocks - 1, LANES - 1] - row * slots
    speaks = (column == 0).astype(F32)
    meta_ref[0:1, :LANES] = goes_to * speaks
    meta_ref[0:1, LANES:] = counts[:1] * speaks
    meta_ref[1:2, :LANES] = named.astype(F32) * speaks
    meta_ref[1:2, LANES:] = (lane == last_slot).astype(F32) * speaks
    share_ref[...] = jnp.zeros_like(share_ref)

    own = pl.ds(pl.multiple_of(column * width, width), width)
    gain = gain_ref[...]
    piece_rows = 32
    pieces = tile // piece_rows

    def piece_of(i, piece):
        at = i * tile + piece * piece_rows
        return x_ref[at:at + piece_rows, :].astype(F32)

    def averages(i):
        return [jnp.sum(piece_of(i, p), axis=1, keepdims=True) * (1.0 / D) for p in range(pieces)]

    def spreads(i, means):
        out = []
        for p in range(pieces):
            centered = piece_of(i, p) - means[p]
            variance = jnp.sum(centered * centered, axis=1, keepdims=True) * (1.0 / D)
            out.append(lax.rsqrt(variance + 1e-05))
        return out

    def scale(i, means, inverses):
        for p in range(pieces):
            scaled = (piece_of(i, p) - means[p]) * inverses[p] * gain
            normed_ref[i % 2, p * piece_rows:(p + 1) * piece_rows, :] = scaled.astype(BF)

    def project(i, which):
        here = slice(i * tile, (i + 1) * tile)
        result = dot(normed_ref[i % 2], w_ref[which])
        if which == 0:
            q_ref[here, :] = (result * (1.0 / math.sqrt(HEAD_DIM))).astype(BF)
        else:
            (k_ref if which == 1 else v_ref)[here, :] = result.astype(BF)

    tokens_sum = jnp.zeros((rows, width), F32)
    means, inverses = {}, {}
    for i in range(-2, tiles):
        ahead = i + 2
        if ahead < tiles:
            x_copies[ahead].wait()
            means[ahead] = averages(ahead)
        if i == 0:
            for copy in w_copies[:3]:
                copy.wait()
        if i >= 0:
            project(i, 0)
        if ahead < tiles:
            inverses[ahead] = spreads(ahead, means[ahead])
        if i >= 0:
            project(i, 1)
        if 0 <= i + 1 < tiles:
            scale(i + 1, means[i + 1], inverses[i + 1])
        if i >= 0:
            project(i, 2)
            here = slice(i * tile, (i + 1) * tile)
            tokens_sum += dot(pool_ref[:, here], x_ref[here, own])

    windows_copy.wait()

    def window(block_pair, part):
        return (windows_sm[block_pair, 2 * part] // 16) * 16, windows_sm[block_pair, 2 * part + 1]

    def all_heads(block):
        at = pl.multiple_of(block * QB, QB)
        zero = jnp.zeros((QB, LANES), BF)
        left = iota((QB, LANES), 1) < HEAD_DIM
        stacked = []
        for half in range(halves):
            piece = q_ref[pl.ds(at, QB), half * LANES:(half + 1) * LANES]
            for kept in (left, jnp.logical_not(left)):
                mine = jnp.where(kept, piece, zero)
                stacked.append(jnp.concatenate([mine if h == half else zero for h in range(halves)], axis=1))
        return jnp.concatenate(stacked, axis=0)

    def masked_scores(block, parity, at, extent):
        scores = dot(k_ref[pl.ds(at, extent), :], all_heads(block), NT)
        same = slot_ref[pl.ds(at, extent), :] == query_slots_ref[parity, pl.ds(block // 2, 1), :]
        return jnp.concatenate(
            [
                jnp.where(same, scores[:, half * LANES:(half + 1) * LANES], -1e30)
                for half in range(halves)
            ],
            axis=1,
        )

    head_of_lane = (iota((8, width), 1) // HEAD_DIM) == (iota((8, width), 0) % heads)
    upper_rows = iota((8, width), 0) < heads

    def key_shares(raised, inverse):
        upper = inverse.astype(BF).astype(F32)
        parts = jnp.where(upper_rows, upper, inverse - upper)
        return dot(jnp.where(head_of_lane, parts, 0.0).astype(BF), raised.astype(BF), NT)

    def straight(blocks, begins, extent):
        padded = round_up(extent, LANES)
        ats = [pl.multiple_of(jnp.minimum(begin, length - extent), 16) for begin in begins]
        scores = [masked_scores(block, i % 2, at, extent) for i, (block, at) in enumerate(zip(blocks, ats))]
        raised = [jnp.exp(s - jnp.max(s, axis=0, keepdims=True)) for s in scores]
        inverse = [1.0 / jnp.sum(r, axis=0, keepdims=True) for r in raised]
        for at, r, v in zip(ats, raised, inverse):
            if padded > extent:
                r = jnp.concatenate([r, jnp.zeros((padded - extent, width), F32)], axis=0)
            shares = jnp.concatenate([key_shares(r, v), jnp.zeros((8, LANES), F32)], axis=1)
            base = pl.multiple_of((at // LANES) * LANES, LANES)
            share_ref[:, pl.ds(base, padded + LANES)] += pltpu.roll(shares, at % LANES, 1)

    def any_length(block):
        chunk = 256
        begin, end = window(block // 2, block % 2)
        first_chunk = begin // chunk
        end_chunk = (end + chunk - 1) // chunk

        def scores_at(index):
            at = pl.multiple_of(index * chunk, chunk)
            scores = dot(k_ref[pl.ds(at, chunk), :], all_heads(block), NT)
            even = query_slots_ref[0, pl.ds(block // 2, 1), :]
            odd = query_slots_ref[1, pl.ds(block // 2, 1), :]
            query_slots = jnp.where(block % 2 == 0, even, odd)
            same = slot_ref[pl.ds(at, chunk), :] == query_slots
            masked = [
                jnp.where(same, scores[:, half * LANES:(half + 1) * LANES], -1e30) for half in range(halves)
            ]
            return at, jnp.concatenate(masked, axis=1)

        def forward(index, carry):
            top, total = carry
            _, scores = scores_at(index)
            higher = jnp.maximum(top, jnp.max(scores, axis=0, keepdims=True))
            raised = jnp.sum(jnp.exp(scores - higher), axis=0, keepdims=True)
            return higher, total * jnp.exp(top - higher) + raised

        top, total = lax.fori_loop(
            first_chunk, end_chunk, forward,
            (jnp.full((1, width), -1e30, F32), jnp.zeros((1, width), F32)),
        )
        inverse = 1.0 / total

        def again(index, nothing):
            at, scores = scores_at(index)
            share_ref[:, pl.ds(at, chunk)] += key_shares(jnp.exp(scores - top), inverse)
            return nothing

        lax.fori_loop(first_chunk, end_chunk, again, 0)

    def group_step(group, nothing):
        blocks = [group * GROUP + i for i in range(GROUP)]
        spans = [window(group * (GROUP // 2) + i // 2, i % 2) for i in range(GROUP)]
        begins = [begin for begin, _ in spans]
        widest = functools.reduce(jnp.maximum, [end - begin for begin, end in spans])
        done = jnp.int32(0)
        for extent in (192, 256, 384, 640):
            if extent > length:
                break

            @pl.when((widest > done) & (widest <= extent))
            def run(extent=extent):
                straight(blocks, begins, extent)

            done = jnp.int32(extent)

        @pl.when(widest > done)
        def slow():
            def one(index, nothing):
                any_length(group * GROUP + index)
                return nothing

            lax.fori_loop(0, GROUP, one, 0)

        return nothing

    lax.fori_loop(0, length // QB // GROUP, group_step, 0)

    shares = share_ref[:, :length]
    pool = pool_ref[...]
    weighted = jnp.concatenate(
        [pool * (shares[h:h + 1] + shares[heads + h:heads + h + 1]).astype(BF) for h in range(heads)], axis=0
    )
    every = dot(weighted, v_ref[...])
    lane_head = iota((rows, width), 1) // HEAD_DIM
    context = jnp.zeros((rows, width), F32)
    for h in range(heads):
        context = jnp.where(lane_head == h, every[h * rows:(h + 1) * rows], context)
    upper = context.astype(BF)
    lower = (context - upper.astype(F32)).astype(BF)
    w_copies[3].wait()
    sent = dot(upper, wo_ref[...]) + dot(lower, wo_ref[...])
    for target in range(mp):
        out_ref[target] = sent[:, target * width:(target + 1) * width]
    out_ref[column] += tokens_sum
    for target in range(mp):
        for block in range(dp):
            at = block * block_rows + capacity + 1
            out_ref[target, at:at + 2, :] = meta_ref[:2, :]


def row_sums(doc_ids, assigned, tokens, ln_gain, w_query, w_key, w_value, w_out, sizes):
    length, tile, slots, capacity, block_rows, dp, mp, width, cents = sizes
    rows = dp * block_rows
    return pl.pallas_call(
        functools.partial(row_kernel, sizes),
        in_specs=[pl.BlockSpec(memory_space=pltpu.HBM)] * 8,
        out_shape=jax.ShapeDtypeStruct((mp, rows, width), F32),
        scratch_shapes=[
            pltpu.VMEM((length // LANES, LANES), jnp.int32),
            pltpu.SMEM((length // LANES, LANES), jnp.int32),
            pltpu.SMEM((1, slots), jnp.int32),
            pltpu.VMEM((1, D), F32),
            pltpu.VMEM((length, D), BF),
            pltpu.VMEM((3, D, width), BF),
            pltpu.VMEM((width, D), BF),
            pltpu.VMEM((2, tile, D), BF),
            pltpu.VMEM((length, width), BF),
            pltpu.VMEM((length, width), BF),
            pltpu.VMEM((length, width), BF),
            pltpu.VMEM((length, LANES), F32),
            pltpu.VMEM((2, length // LANES, LANES), F32),
            pltpu.VMEM((length // LANES, LANES), jnp.int32),
            pltpu.SMEM((length // LANES, LANES), jnp.int32),
            pltpu.VMEM((rows, length), BF),
            pltpu.VMEM((8, 2 * LANES), F32),
            pltpu.VMEM((8, length + 2 * LANES), F32),
            pltpu.SemaphoreType.DMA((5,)),
            pltpu.SemaphoreType.DMA((length // tile,)),
            pltpu.SemaphoreType.DMA((4,)),
        ],
        compiler_params=pltpu.CompilerParams(vmem_limit_bytes=62 * 1024 * 1024),
        name="row_sums",
    )(
        doc_ids.reshape(length // LANES, LANES), assigned.reshape(1, slots), ln_gain.reshape(1, D),
        tokens, w_query, w_key, w_value, w_out,
    )


def products_kernel(
    sizes, here_ref, own_ref, cent_ref, mass_ref, pay_ref, docs_ref, near_ref, info_ref, own_out_ref
):
    length, tile, slots, capacity, block_rows, dp, mp, width, cents = sizes
    me = lax.axis_index("dp")
    rows = dp * block_rows
    lane = iota((1, LANES), 1)

    def rows_of(meta, first_row, count):
        goes_to, counts = meta[0:1, :LANES], meta[0:1, LANES:]
        named, is_last = meta[1:2, :LANES], meta[1:2, LANES:]
        held = (goes_to == (iota((count, LANES), 0) + first_row).astype(F32)).astype(F32)

        def column(values):
            return jnp.sum(held * values, axis=1, keepdims=True)

        return column(named), column(counts), column(is_last), column(jnp.ones((1, LANES), F32))

    def carry_of(source):
        block = here_ref[pl.ds(pl.multiple_of(source * block_rows, 8), block_rows), :]
        counts = block[capacity + 1:capacity + 2, LANES:]
        count = jnp.sum(jnp.where(lane == slots, counts, 0.0), axis=1, keepdims=True)
        return block[capacity:capacity + 1, :], count

    columns = []
    for source in range(dp):
        base = source * block_rows
        block = here_ref[base:base + block_rows, :]
        meta = block[capacity + 1:capacity + 3, :]
        named, counts, is_last, held = rows_of(meta, me * block_rows, block_rows)
        sums = jnp.where(held > 0, block, 0.0)
        if source < dp - 1:
            carry, carry_count = carry_of(source + 1)
            sums = sums + is_last * carry
            counts = counts + is_last * carry_count
        docs_ref[base:base + block_rows, :] = sums
        columns.append((named - (me * cents).astype(F32), counts, held))
    local = jnp.concatenate([c[0] for c in columns], axis=0)
    counts = jnp.concatenate([c[1] for c in columns], axis=0)
    held = jnp.concatenate([c[2] for c in columns], axis=0)
    valid = ((held > 0) & (counts > 0)).astype(F32)

    docs = docs_ref[...]
    names = (iota((rows, cents), 1).astype(F32) == local) & (valid > 0)
    names = names.astype(F32)
    mass = jnp.sum(names * mass_ref[...], axis=1, keepdims=True)
    near = pick_rows(names.astype(BF), cent_ref[...])
    near_ref[...] = near

    own = own_ref[...]
    _, own_counts, own_last, _ = rows_of(own_ref[capacity + 1:capacity + 3, :], 0, rows)
    following = jnp.minimum(me + 1, dp - 1)
    more = (me < dp - 1).astype(F32)
    carry, carry_count = carry_of(following)
    own = own + own_last * (carry * more)
    own_counts = own_counts + own_last * (carry_count * more)
    own_out_ref[...] = own

    gram = dot(docs, docs, NT, precision=lax.Precision.HIGHEST)
    spot = iota((rows, LANES), 1)
    cross = jnp.sum(near * docs, axis=1, keepdims=True)
    square = jnp.sum(near * near, axis=1, keepdims=True)
    own_square = jnp.sum(own * own, axis=1, keepdims=True)
    doc_square = jnp.sum(docs * docs, axis=1, keepdims=True)
    pay_ref[0] = jnp.zeros(pay_ref.shape[1:], F32)
    pay_ref[0, :, :rows] = gram
    for i, sums in enumerate((cross, square, own_square, doc_square)):
        pay_ref[0, :, rows + i:rows + i + 1] = sums
    for target in range(1, mp):
        pay_ref[target] = pay_ref[0]
    info_ref[...] = jnp.where(
        spot == 0, local, jnp.where(spot == 1, counts, jnp.where(spot == 2, valid, jnp.where(spot == 3, mass, own_counts)))
    )


def update_kernel(
    sizes, pay_ref, docs_ref, near_ref, info_ref, own_ref, meta_ref, cent_ref, vec_ref, new_ref
):
    length, tile, slots, capacity, block_rows, dp, mp, width, cents = sizes
    rows = dp * block_rows
    info = info_ref[...]
    local, counts, valid, mass, own_counts = (info[:, i:i + 1] for i in range(5))
    pay = functools.reduce(jnp.add, [pay_ref[i] for i in range(mp)])
    cross, square, own_square, doc_square = (pay[:, rows + i:rows + i + 1] for i in range(4))

    def scale(sums, count):
        inverse = 1.0 / jnp.maximum(count, 1.0)
        return inverse * lax.rsqrt(sums * inverse * inverse * (1.0 / D) + 1e-06)

    vectors = own_ref[...] * scale(own_square, own_counts)
    goes_to = meta_ref[capacity + 1:capacity + 2, :LANES]
    place = ((iota((rows, LANES), 0).astype(F32) == goes_to).astype(F32)).T
    vec_ref[...] = pick_rows(place[:slots].astype(BF), vectors)

    share = scale(doc_square, counts) * valid
    across = jnp.where(valid > 0, local, -1.0)
    flat = jnp.broadcast_to(across, (rows, LANES)).T[:1]
    share_flat = jnp.broadcast_to(share, (rows, LANES)).T[:1]
    cross_flat = jnp.broadcast_to(cross, (rows, LANES)).T[:1]
    same = (across == flat) & (valid > 0)
    mixed = jnp.where(same, share_flat, 0.0)
    gained = dot(mixed, docs_ref[...], precision=lax.Precision.HIGHEST)
    twice = dot(mixed, pay[:, :rows], precision=lax.Precision.HIGHEST)
    norm = (
        mass * mass * square
        + 2.0 * mass * jnp.sum(mixed * cross_flat, axis=1, keepdims=True)
        + jnp.sum(twice * mixed, axis=1, keepdims=True)
    )
    blended = mass * near_ref[...] + gained
    scaled = blended * lax.rsqrt(norm * (1.0 / D) + 1e-06)
    before = same & (iota((rows, rows), 0) < iota((rows, rows), 1))
    repeated = jnp.sum(before.astype(F32), axis=0, keepdims=True)
    target = jnp.where((flat >= 0) & (repeated < 0.5), flat, -1.0)
    hits = (iota((cents, rows), 0).astype(F32) == target).astype(F32)
    updated = pick_rows(hits.astype(BF), scaled)
    hit = jnp.sum(hits, axis=1, keepdims=True)
    new_ref[...] = jnp.where(hit > 0, updated, cent_ref[...])


def shards(
    tokens, doc_ids, ln_gain, w_query, w_key, w_value, w_out, centroids, cluster_mass, assigned
):
    length = tokens.shape[0]
    slots = assigned.shape[0]
    width = w_out.shape[0]
    cents = centroids.shape[0]
    dp = lax.axis_size("dp")
    mp = lax.axis_size("mp")
    capacity = max(2, (slots + dp - 2) // (dp - 1))
    block_rows = round_up(capacity + 3, 8)
    rows = dp * block_rows
    sizes = (length, min(256, length), slots, capacity, block_rows, dp, mp, width, cents)
    limit = pltpu.CompilerParams(vmem_limit_bytes=48 * 1024 * 1024)

    partial = row_sums(doc_ids, assigned, tokens, ln_gain, w_query, w_key, w_value, w_out, sizes)
    shared = lax.all_to_all(partial, "mp", split_axis=0, concat_axis=0, tiled=True)
    own = jnp.sum(shared, axis=0)
    here = lax.all_to_all(own, "dp", split_axis=0, concat_axis=0, tiled=True)

    pay, docs, near, info, own_sums = pl.pallas_call(
        functools.partial(products_kernel, sizes),
        out_shape=(
            jax.ShapeDtypeStruct((mp, rows, round_up(rows + 4, LANES)), F32),
            jax.ShapeDtypeStruct((rows, width), F32),
            jax.ShapeDtypeStruct((rows, width), F32),
            jax.ShapeDtypeStruct((rows, LANES), F32),
            jax.ShapeDtypeStruct((rows, width), F32),
        ),
        compiler_params=limit,
        name="products",
    )(here, own, centroids, cluster_mass.reshape(1, cents))
    pay = lax.all_to_all(pay, "mp", split_axis=0, concat_axis=0, tiled=True)
    return pl.pallas_call(
        functools.partial(update_kernel, sizes),
        out_shape=(
            jax.ShapeDtypeStruct((slots, width), F32),
            jax.ShapeDtypeStruct((cents, width), F32),
        ),
        compiler_params=limit,
        name="update",
    )(pay, docs, near, info, own_sums, own, centroids)


def solution(mesh):
    placed = (
        P("dp", None),
        P("dp"),
        P(),
        P(None, "mp"),
        P(None, "mp"),
        P(None, "mp"),
        P("mp", None),
        P("dp", "mp"),
        P("dp"),
        P("dp"),
    )
    return jax.shard_map(
        shards,
        mesh=mesh,
        in_specs=placed,
        out_specs=(P("dp", "mp"), P("dp", "mp")),
        check_vma=False,
    )
```

```python
import functools
import math

import jax
import jax.numpy as jnp
from jax import lax
from jax.experimental import pallas as pl
from jax.experimental.pallas import tpu as pltpu
from jax.sharding import PartitionSpec as P

D = 1024
HEAD_DIM = 64
QB = 64
GROUP = 8
EXTENTS = (192, 256, 384, 640)
LANES = 128
BF = jnp.bfloat16
F32 = jnp.float32

NN = (((1,), (0,)), ((), ()))
NT = (((1,), (1,)), ((), ()))
TN = (((0,), (0,)), ((), ()))


def dot(a, b, dims=NN, precision=None):
    return lax.dot_general(a, b, dims, preferred_element_type=F32, precision=precision)


def iota(shape, dim):
    return lax.broadcasted_iota(jnp.int32, shape, dim)


def thirds(x):
    first = x.astype(BF)
    rest = x - first.astype(F32)
    second = rest.astype(BF)
    third = (rest - second.astype(F32)).astype(BF)
    return first, second, third


def pick_rows(one_hot, x, dims=NN):
    first, second, third = thirds(x)
    return dot(one_hot, first, dims) + (dot(one_hot, second, dims) + dot(one_hot, third, dims))


def round_up(n, by):
    return (n + by - 1) // by * by


def row_kernel(
    sizes, ids_hbm, assigned_hbm, gain_hbm, x_hbm, wq_hbm, wk_hbm, wv_hbm, wo_hbm, out_ref,
    ids_ref, ids_sm, assigned_sm, gain_ref, x_ref, w_ref, wo_ref, normed_ref, q_ref, k_ref, v_ref,
    slot_ref, query_slots_ref, windows_ref, windows_sm, pool_ref, meta_ref, share_ref, scores_ref, raised_ref, small_sems, x_sems, w_sems,
):
    length, tile, slots, capacity, block_rows, dp, mp, width, cents = sizes
    tiles = length // tile
    lane_blocks = length // LANES
    rows = dp * block_rows
    heads = width // HEAD_DIM
    halves = width // LANES
    row = lax.axis_index("dp")
    column = lax.axis_index("mp")

    small_copies = [
        pltpu.make_async_copy(ids_hbm, ids_ref, small_sems.at[0]),
        pltpu.make_async_copy(ids_hbm, ids_sm, small_sems.at[1]),
        pltpu.make_async_copy(assigned_hbm, assigned_sm, small_sems.at[2]),
        pltpu.make_async_copy(gain_hbm, gain_ref, small_sems.at[3]),
    ]
    x_copies = [
        pltpu.make_async_copy(x_hbm.at[pl.ds(i * tile, tile), :], x_ref.at[pl.ds(i * tile, tile), :], x_sems.at[i])
        for i in range(tiles)
    ]
    w_copies = [
        pltpu.make_async_copy(w_hbm, w_ref.at[i], w_sems.at[i])
        for i, w_hbm in enumerate((wq_hbm, wk_hbm, wv_hbm))
    ] + [pltpu.make_async_copy(wo_hbm, wo_ref, w_sems.at[3])]
    for copy in small_copies + x_copies[:1]:
        copy.start()
    for copy in w_copies[:3]:
        copy.start(priority=1)
    for copy in x_copies[1:]:
        copy.start()
    w_copies[3].start(priority=1)
    for copy in small_copies:
        copy.wait()

    ids = ids_ref[...]
    local = ids - row * slots
    slot_rows = jnp.where(local < 0, slots, local).astype(F32)
    turned = pltpu.roll(slot_rows, QB, 1)
    front = iota(slot_rows.shape, 1) < QB
    query_slots_ref[0] = jnp.where(front, slot_rows, turned)
    query_slots_ref[1] = jnp.where(front, turned, slot_rows)

    lane = iota((1, LANES), 1)
    named = jnp.full((1, LANES), -1, jnp.int32)
    for j in range(slots):
        named = jnp.where(lane == j, assigned_sm[0, j], named)
    owner = named // cents
    wide = jnp.broadcast_to(owner.astype(F32), (LANES, LANES))
    earlier = (wide.T == wide) & (iota((LANES, LANES), 0) < iota((LANES, LANES), 1))
    rank = jnp.sum(earlier.astype(F32), axis=0, keepdims=True)
    goes_to = jnp.where(lane < slots, owner.astype(F32) * block_rows + rank, -1.0)
    row_of = iota((rows, LANES), 0)
    place = (row_of.astype(F32) == goes_to) | (
        (row_of % block_rows == capacity) & (iota((rows, LANES), 1) == slots)
    )
    place = place.astype(F32).astype(BF)

    on_diagonal = iota((LANES, LANES), 0) == iota((LANES, LANES), 1)
    ones = jnp.ones((LANES, LANES), BF)
    counts = []
    for block in range(lane_blocks):
        here = slice(block * LANES, (block + 1) * LANES)
        slot = slot_rows[block:block + 1, :]
        diagonal = jnp.where(on_diagonal, slot, 0.0).astype(BF)
        slot_ref[here, :] = dot(diagonal, ones)
        member = (iota((LANES, LANES), 0).astype(F32) == slot).astype(F32).astype(BF)
        counts.append(dot(ones[:8], member, NT))
        pool_ref[:, here] = dot(place, member).astype(BF)
    counts = functools.reduce(jnp.add, counts)

    def order(shape, dim):
        slot = iota(shape, dim)
        return jnp.where(slot == slots, 0, slot + 1)

    before = (order((LANES, LANES), 0) < order((LANES, LANES), 1)) & (iota((LANES, LANES), 0) <= slots)
    before = before.astype(F32).astype(BF)
    upper = counts.astype(BF)
    starts = dot(upper, before) + dot((counts - upper.astype(F32)).astype(BF), before)

    def at_position(values, position):
        mine = iota(slot_rows.shape, 1).astype(F32) == slot_rows[:, position:position + 1]
        return jnp.sum(jnp.where(mine, values[:1], 0.0), axis=1, keepdims=True)

    spot = iota(slot_rows.shape, 1)
    table = jnp.zeros(slot_rows.shape, F32)
    for part in range(LANES // QB):
        table = jnp.where(spot == 2 * part, at_position(starts, part * QB), table)
        table = jnp.where(spot == 2 * part + 1, at_position(starts + counts, (part + 1) * QB - 1), table)
    windows_ref[...] = table.astype(jnp.int32)
    windows_copy = pltpu.make_async_copy(windows_ref, windows_sm, small_sems.at[4])
    windows_copy.start()

    last_slot = ids_sm[lane_blocks - 1, LANES - 1] - row * slots
    speaks = (column == 0).astype(F32)
    meta_ref[0:1, :LANES] = goes_to * speaks
    meta_ref[0:1, LANES:] = counts[:1] * speaks
    meta_ref[1:2, :LANES] = named.astype(F32) * speaks
    meta_ref[1:2, LANES:] = (lane == last_slot).astype(F32) * speaks
    share_ref[...] = jnp.zeros_like(share_ref)

    own = pl.ds(pl.multiple_of(column * width, width), width)
    gain = gain_ref[...]
    piece_rows = 64
    pieces = tile // piece_rows
    lane_slices = [slice(j * LANES, (j + 1) * LANES) for j in range(D // LANES)]

    def piece_of(i, p, lanes):
        at = i * tile + p * piece_rows
        return x_ref[at:at + piece_rows, lanes].astype(F32)

    def averages(i):
        out = []
        for p in range(pieces):
            total = functools.reduce(jnp.add, [piece_of(i, p, lanes) for lanes in lane_slices])
            mean = jnp.sum(total, axis=1, keepdims=True) * (1.0 / D)
            out.append(jnp.broadcast_to(mean, (piece_rows, LANES)))
        return out

    def centre(i, means):
        out = []
        for p in range(pieces):
            here = slice(p * piece_rows, (p + 1) * piece_rows)
            squares = jnp.zeros((piece_rows, LANES), F32)
            for lanes in lane_slices:
                centered = piece_of(i, p, lanes) - means[p]
                squares += centered * centered
                normed_ref[i % 2, here, lanes] = (centered * gain[:, lanes]).astype(BF)
            variance = jnp.sum(squares, axis=1, keepdims=True) * (1.0 / D)
            out.append(lax.rsqrt(variance + 1e-05))
        return jnp.concatenate(out, axis=0)

    def project(i, which, inverse):
        here = slice(i * tile, (i + 1) * tile)
        if which == 0:
            inverse = inverse * (math.log2(math.e) / math.sqrt(HEAD_DIM))
        result = (dot(normed_ref[i % 2], w_ref[which]) * inverse).astype(BF)
        (q_ref, k_ref, v_ref)[which][here, :] = result

    tokens_sum = jnp.zeros((rows, width), F32)
    inverses = {}
    for i in range(-1, tiles):
        ahead = i + 1
        if ahead < tiles:
            x_copies[ahead].wait()
            means = averages(ahead)
        if i == 0:
            for copy in w_copies[:3]:
                copy.wait()
        if i >= 0:
            project(i, 0, inverses[i])
        if ahead < tiles:
            inverses[ahead] = centre(ahead, means)
        if i >= 0:
            project(i, 1, inverses[i])
            project(i, 2, inverses[i])
            here = slice(i * tile, (i + 1) * tile)
            tokens_sum += dot(pool_ref[:, here], x_ref[here, own])
    windows_copy.wait()

    def window(block_pair, part):
        return (windows_sm[block_pair, 2 * part] // 16) * 16, windows_sm[block_pair, 2 * part + 1]

    def all_heads(block):
        at = pl.multiple_of(block * QB, QB)
        zero = jnp.zeros((QB, LANES), BF)
        left = iota((QB, LANES), 1) < HEAD_DIM
        stacked = []
        for half in range(halves):
            piece = q_ref[pl.ds(at, QB), half * LANES:(half + 1) * LANES]
            for kept in (left, jnp.logical_not(left)):
                mine = jnp.where(kept, piece, zero)
                stacked.append(jnp.concatenate([mine if h == half else zero for h in range(halves)], axis=1))
        return jnp.concatenate(stacked, axis=0)

    head_of_lane = (iota((8, width), 1) // HEAD_DIM) == (iota((8, width), 0) % heads)
    upper_rows = iota((8, width), 0) < heads

    def key_shares(raised, inverse):
        upper = inverse.astype(BF).astype(F32)
        parts = jnp.where(upper_rows, upper, inverse - upper)
        return dot(jnp.where(head_of_lane, parts, 0.0).astype(BF), raised, NT)

    def straight(blocks, begins, extent):
        padded = round_up(extent, LANES)
        step = 64
        ats = [pl.multiple_of(jnp.minimum(begin, length - extent), 16) for begin in begins]
        halves_of = [slice(half * LANES, (half + 1) * LANES) for half in range(halves)]
        for i, (block, at) in enumerate(zip(blocks, ats)):
            scores_ref[i, :extent, :] = dot(k_ref[pl.ds(at, extent), :], all_heads(block), NT)
        tops = []
        for i, (block, at) in enumerate(zip(blocks, ats)):
            mine = query_slots_ref[i % 2, pl.ds(block // 2, 1), :]
            top = [jnp.full((8, LANES), -1e30, F32) for _ in range(halves)]
            for key in range(0, extent, step):
                same = slot_ref[pl.ds(at + key, step), :] == mine
                for half, lanes in enumerate(halves_of):
                    masked = jnp.where(same, scores_ref[i, key:key + step, lanes], -1e30)
                    scores_ref[i, key:key + step, lanes] = masked
                    highest = jnp.max(masked.reshape(step // 8, 8, LANES), axis=0)
                    top[half] = jnp.maximum(top[half], highest)
            tops.append([jnp.max(t, axis=0, keepdims=True) for t in top])
        inverses = []
        for i in range(len(blocks)):
            total = [jnp.zeros((8, LANES), F32) for _ in range(halves)]
            for key in range(0, extent, step):
                for half, lanes in enumerate(halves_of):
                    raised = jnp.exp2(scores_ref[i, key:key + step, lanes] - tops[i][half])
                    total[half] += jnp.sum(raised.reshape(step // 8, 8, LANES), axis=0)
                    raised_ref[i, key:key + step, lanes] = raised.astype(BF)
            if padded > extent:
                raised_ref[i, extent:padded, :] = jnp.zeros((padded - extent, width), BF)
            inverses.append(
                jnp.concatenate([1.0 / jnp.sum(t, axis=0, keepdims=True) for t in total], axis=1)
            )
        for i, at in enumerate(ats):
            shares = key_shares(raised_ref[i, :padded, :], inverses[i])
            shares = jnp.concatenate([shares, jnp.zeros((8, LANES), F32)], axis=1)
            base = pl.multiple_of((at // LANES) * LANES, LANES)
            share_ref[:, pl.ds(base, padded + LANES)] += pltpu.roll(shares, at % LANES, 1)

    def any_length(block):
        chunk = 256
        begin, end = window(block // 2, block % 2)
        first_chunk = begin // chunk
        end_chunk = (end + chunk - 1) // chunk

        def scores_at(index):
            at = pl.multiple_of(index * chunk, chunk)
            scores = dot(k_ref[pl.ds(at, chunk), :], all_heads(block), NT)
            even = query_slots_ref[0, pl.ds(block // 2, 1), :]
            odd = query_slots_ref[1, pl.ds(block // 2, 1), :]
            query_slots = jnp.where(block % 2 == 0, even, odd)
            same = slot_ref[pl.ds(at, chunk), :] == query_slots
            masked = [
                jnp.where(same, scores[:, half * LANES:(half + 1) * LANES], -1e30) for half in range(halves)
            ]
            return at, jnp.concatenate(masked, axis=1)

        def forward(index, carry):
            top, total = carry
            _, scores = scores_at(index)
            higher = jnp.maximum(top, jnp.max(scores, axis=0, keepdims=True))
            raised = jnp.sum(jnp.exp2(scores - higher), axis=0, keepdims=True)
            return higher, total * jnp.exp2(top - higher) + raised

        top, total = lax.fori_loop(
            first_chunk, end_chunk, forward,
            (jnp.full((1, width), -1e30, F32), jnp.zeros((1, width), F32)),
        )
        inverse = 1.0 / total

        def again(index, nothing):
            at, scores = scores_at(index)
            share_ref[:, pl.ds(at, chunk)] += key_shares(jnp.exp2(scores - top).astype(BF), inverse)
            return nothing

        lax.fori_loop(first_chunk, end_chunk, again, 0)

    def group_step(group, nothing):
        blocks = [group * GROUP + i for i in range(GROUP)]
        spans = [window(group * (GROUP // 2) + i // 2, i % 2) for i in range(GROUP)]
        begins = [begin for begin, _ in spans]
        widest = functools.reduce(jnp.maximum, [end - begin for begin, end in spans])
        done = jnp.int32(0)
        for extent in EXTENTS:
            if extent > length:
                break

            @pl.when((widest > done) & (widest <= extent))
            def run(extent=extent):
                straight(blocks, begins, extent)

            done = jnp.int32(extent)

        @pl.when(widest > done)
        def slow():
            def one(index, nothing):
                any_length(group * GROUP + index)
                return nothing

            lax.fori_loop(0, GROUP, one, 0)

        return nothing

    lax.fori_loop(0, length // QB // GROUP, group_step, 0)

    shares = share_ref[:, :length]
    pool = pool_ref[...]
    weighted = jnp.concatenate(
        [pool * (shares[h:h + 1] + shares[heads + h:heads + h + 1]).astype(BF) for h in range(heads)], axis=0
    )
    every = dot(weighted, v_ref[...])
    lane_head = iota((rows, width), 1) // HEAD_DIM
    context = jnp.zeros((rows, width), F32)
    for h in range(heads):
        context = jnp.where(lane_head == h, every[h * rows:(h + 1) * rows], context)
    upper = context.astype(BF)
    lower = (context - upper.astype(F32)).astype(BF)
    w_copies[3].wait()
    sent = dot(jnp.concatenate([upper, lower], axis=0), wo_ref[...])
    sent = sent[:rows] + sent[rows:]
    for target in range(mp):
        out_ref[target] = sent[:, target * width:(target + 1) * width]
    out_ref[column] += tokens_sum
    for target in range(mp):
        for block in range(dp):
            at = block * block_rows + capacity + 1
            out_ref[target, at:at + 2, :] = meta_ref[:2, :]


def row_sums(doc_ids, assigned, tokens, ln_gain, w_query, w_key, w_value, w_out, sizes):
    length, tile, slots, capacity, block_rows, dp, mp, width, cents = sizes
    rows = dp * block_rows
    return pl.pallas_call(
        functools.partial(row_kernel, sizes),
        in_specs=[pl.BlockSpec(memory_space=pltpu.HBM)] * 8,
        out_shape=jax.ShapeDtypeStruct((mp, rows, width), F32),
        scratch_shapes=[
            pltpu.VMEM((length // LANES, LANES), jnp.int32),
            pltpu.SMEM((length // LANES, LANES), jnp.int32),
            pltpu.SMEM((1, slots), jnp.int32),
            pltpu.VMEM((1, D), F32),
            pltpu.VMEM((length, D), BF),
            pltpu.VMEM((3, D, width), BF),
            pltpu.VMEM((width, D), BF),
            pltpu.VMEM((2, tile, D), BF),
            pltpu.VMEM((length, width), BF),
            pltpu.VMEM((length, width), BF),
            pltpu.VMEM((length, width), BF),
            pltpu.VMEM((length, LANES), F32),
            pltpu.VMEM((2, length // LANES, LANES), F32),
            pltpu.VMEM((length // LANES, LANES), jnp.int32),
            pltpu.SMEM((length // LANES, LANES), jnp.int32),
            pltpu.VMEM((rows, length), BF),
            pltpu.VMEM((8, 2 * LANES), F32),
            pltpu.VMEM((8, length + 2 * LANES), F32),
            pltpu.VMEM((GROUP, EXTENTS[-1], width), F32),
            pltpu.VMEM((GROUP, EXTENTS[-1], width), BF),
            pltpu.SemaphoreType.DMA((5,)),
            pltpu.SemaphoreType.DMA((length // tile,)),
            pltpu.SemaphoreType.DMA((4,)),
        ],
        compiler_params=pltpu.CompilerParams(vmem_limit_bytes=62 * 1024 * 1024),
        name="row_sums",
    )(
        doc_ids.reshape(length // LANES, LANES), assigned.reshape(1, slots), ln_gain.reshape(1, D),
        tokens, w_query, w_key, w_value, w_out,
    )


def products_kernel(
    sizes, here_ref, own_ref, cent_ref, mass_ref, pay_ref, docs_ref, near_ref, info_ref, own_out_ref
):
    length, tile, slots, capacity, block_rows, dp, mp, width, cents = sizes
    me = lax.axis_index("dp")
    rows = dp * block_rows
    lane = iota((1, LANES), 1)

    def rows_of(meta, first_row, count):
        goes_to, counts = meta[0:1, :LANES], meta[0:1, LANES:]
        named, is_last = meta[1:2, :LANES], meta[1:2, LANES:]
        held = (goes_to == (iota((count, LANES), 0) + first_row).astype(F32)).astype(F32)

        def column(values):
            return jnp.sum(held * values, axis=1, keepdims=True)

        return column(named), column(counts), column(is_last), column(jnp.ones((1, LANES), F32))

    def carry_of(source):
        block = here_ref[pl.ds(pl.multiple_of(source * block_rows, 8), block_rows), :]
        counts = block[capacity + 1:capacity + 2, LANES:]
        count = jnp.sum(jnp.where(lane == slots, counts, 0.0), axis=1, keepdims=True)
        return block[capacity:capacity + 1, :], count

    columns = []
    for source in range(dp):
        base = source * block_rows
        block = here_ref[base:base + block_rows, :]
        meta = block[capacity + 1:capacity + 3, :]
        named, counts, is_last, held = rows_of(meta, me * block_rows, block_rows)
        sums = jnp.where(held > 0, block, 0.0)
        if source < dp - 1:
            carry, carry_count = carry_of(source + 1)
            sums = sums + is_last * carry
            counts = counts + is_last * carry_count
        docs_ref[base:base + block_rows, :] = sums
        columns.append((named - (me * cents).astype(F32), counts, held))
    local = jnp.concatenate([c[0] for c in columns], axis=0)
    counts = jnp.concatenate([c[1] for c in columns], axis=0)
    held = jnp.concatenate([c[2] for c in columns], axis=0)
    valid = ((held > 0) & (counts > 0)).astype(F32)

    docs = docs_ref[...]
    names = (iota((rows, cents), 1).astype(F32) == local) & (valid > 0)
    names = names.astype(F32)
    mass = jnp.sum(names * mass_ref[...], axis=1, keepdims=True)
    near = pick_rows(names.astype(BF), cent_ref[...])
    near_ref[...] = near

    own = own_ref[...]
    _, own_counts, own_last, _ = rows_of(own_ref[capacity + 1:capacity + 3, :], 0, rows)
    following = jnp.minimum(me + 1, dp - 1)
    more = (me < dp - 1).astype(F32)
    carry, carry_count = carry_of(following)
    own = own + own_last * (carry * more)
    own_counts = own_counts + own_last * (carry_count * more)
    own_out_ref[...] = own

    gram = dot(docs, docs, NT, precision=lax.Precision.HIGHEST)
    spot = iota((rows, LANES), 1)
    cross = jnp.sum(near * docs, axis=1, keepdims=True)
    square = jnp.sum(near * near, axis=1, keepdims=True)
    own_square = jnp.sum(own * own, axis=1, keepdims=True)
    doc_square = jnp.sum(docs * docs, axis=1, keepdims=True)
    pay_ref[0] = jnp.zeros(pay_ref.shape[1:], F32)
    pay_ref[0, :, :rows] = gram
    for i, sums in enumerate((cross, square, own_square, doc_square)):
        pay_ref[0, :, rows + i:rows + i + 1] = sums
    for target in range(1, mp):
        pay_ref[target] = pay_ref[0]
    info_ref[...] = jnp.where(
        spot == 0, local, jnp.where(spot == 1, counts, jnp.where(spot == 2, valid, jnp.where(spot == 3, mass, own_counts)))
    )


def update_kernel(
    sizes, pay_ref, docs_ref, near_ref, info_ref, own_ref, meta_ref, cent_ref, vec_ref, new_ref
):
    length, tile, slots, capacity, block_rows, dp, mp, width, cents = sizes
    rows = dp * block_rows
    info = info_ref[...]
    local, counts, valid, mass, own_counts = (info[:, i:i + 1] for i in range(5))
    pay = functools.reduce(jnp.add, [pay_ref[i] for i in range(mp)])
    cross, square, own_square, doc_square = (pay[:, rows + i:rows + i + 1] for i in range(4))

    def scale(sums, count):
        inverse = 1.0 / jnp.maximum(count, 1.0)
        return inverse * lax.rsqrt(sums * inverse * inverse * (1.0 / D) + 1e-06)

    vectors = own_ref[...] * scale(own_square, own_counts)
    goes_to = meta_ref[capacity + 1:capacity + 2, :LANES]
    place = ((iota((rows, LANES), 0).astype(F32) == goes_to).astype(F32)).T
    vec_ref[...] = pick_rows(place[:slots].astype(BF), vectors)

    share = scale(doc_square, counts) * valid
    across = jnp.where(valid > 0, local, -1.0)
    flat = jnp.broadcast_to(across, (rows, LANES)).T[:1]
    share_flat = jnp.broadcast_to(share, (rows, LANES)).T[:1]
    cross_flat = jnp.broadcast_to(cross, (rows, LANES)).T[:1]
    same = (across == flat) & (valid > 0)
    mixed = jnp.where(same, share_flat, 0.0)
    gained = dot(mixed, docs_ref[...], precision=lax.Precision.HIGHEST)
    twice = dot(mixed, pay[:, :rows], precision=lax.Precision.HIGHEST)
    norm = (
        mass * mass * square
        + 2.0 * mass * jnp.sum(mixed * cross_flat, axis=1, keepdims=True)
        + jnp.sum(twice * mixed, axis=1, keepdims=True)
    )
    blended = mass * near_ref[...] + gained
    scaled = blended * lax.rsqrt(norm * (1.0 / D) + 1e-06)
    before = same & (iota((rows, rows), 0) < iota((rows, rows), 1))
    repeated = jnp.sum(before.astype(F32), axis=0, keepdims=True)
    target = jnp.where((flat >= 0) & (repeated < 0.5), flat, -1.0)
    hits = (iota((cents, rows), 0).astype(F32) == target).astype(F32)
    updated = pick_rows(hits.astype(BF), scaled)
    hit = jnp.sum(hits, axis=1, keepdims=True)
    new_ref[...] = jnp.where(hit > 0, updated, cent_ref[...])


def shards(
    tokens, doc_ids, ln_gain, w_query, w_key, w_value, w_out, centroids, cluster_mass, assigned
):
    length = tokens.shape[0]
    slots = assigned.shape[0]
    width = w_out.shape[0]
    cents = centroids.shape[0]
    dp = lax.axis_size("dp")
    mp = lax.axis_size("mp")
    capacity = max(2, (slots + dp - 2) // (dp - 1))
    block_rows = round_up(capacity + 3, 8)
    rows = dp * block_rows
    sizes = (length, min(256, length), slots, capacity, block_rows, dp, mp, width, cents)
    limit = pltpu.CompilerParams(vmem_limit_bytes=48 * 1024 * 1024)

    partial = row_sums(doc_ids, assigned, tokens, ln_gain, w_query, w_key, w_value, w_out, sizes)
    shared = lax.all_to_all(partial, "mp", split_axis=0, concat_axis=0, tiled=True)
    own = jnp.sum(shared, axis=0)
    here = lax.all_to_all(own, "dp", split_axis=0, concat_axis=0, tiled=True)

    pay, docs, near, info, own_sums = pl.pallas_call(
        functools.partial(products_kernel, sizes),
        out_shape=(
            jax.ShapeDtypeStruct((mp, rows, round_up(rows + 4, LANES)), F32),
            jax.ShapeDtypeStruct((rows, width), F32),
            jax.ShapeDtypeStruct((rows, width), F32),
            jax.ShapeDtypeStruct((rows, LANES), F32),
            jax.ShapeDtypeStruct((rows, width), F32),
        ),
        compiler_params=limit,
        name="products",
    )(here, own, centroids, cluster_mass.reshape(1, cents))
    pay = lax.all_to_all(pay, "mp", split_axis=0, concat_axis=0, tiled=True)
    return pl.pallas_call(
        functools.partial(update_kernel, sizes),
        out_shape=(
            jax.ShapeDtypeStruct((slots, width), F32),
            jax.ShapeDtypeStruct((cents, width), F32),
        ),
        compiler_params=limit,
        name="update",
    )(pay, docs, near, info, own_sums, own, centroids)


def solution(mesh):
    placed = (
        P("dp", None),
        P("dp"),
        P(),
        P(None, "mp"),
        P(None, "mp"),
        P(None, "mp"),
        P("mp", None),
        P("dp", "mp"),
        P("dp"),
        P("dp"),
    )
    return jax.shard_map(
        shards,
        mesh=mesh,
        in_specs=placed,
        out_specs=(P("dp", "mp"), P("dp", "mp")),
        check_vma=False,
    )
```

```python
import functools
import math

import jax
import jax.numpy as jnp
from jax import lax
from jax.experimental import pallas as pl
from jax.experimental.pallas import tpu as pltpu
from jax.sharding import PartitionSpec as P

D = 1024
HEAD_DIM = 64
QB = 128
GROUP = 4
EXTENTS = (256, 320, 384, 640)
LANES = 128
BF = jnp.bfloat16
F32 = jnp.float32

NN = (((1,), (0,)), ((), ()))
NT = (((1,), (1,)), ((), ()))
TN = (((0,), (0,)), ((), ()))


def dot(a, b, dims=NN, precision=None):
    return lax.dot_general(a, b, dims, preferred_element_type=F32, precision=precision)


def iota(shape, dim):
    return lax.broadcasted_iota(jnp.int32, shape, dim)


def thirds(x):
    first = x.astype(BF)
    rest = x - first.astype(F32)
    second = rest.astype(BF)
    third = (rest - second.astype(F32)).astype(BF)
    return first, second, third


def pick_rows(one_hot, x, dims=NN):
    first, second, third = thirds(x)
    return dot(one_hot, first, dims) + (dot(one_hot, second, dims) + dot(one_hot, third, dims))


def round_up(n, by):
    return (n + by - 1) // by * by


def row_kernel(
    sizes, ids_hbm, assigned_hbm, gain_hbm, x_hbm, wq_hbm, wk_hbm, wv_hbm, wo_hbm, out_ref,
    ids_ref, ids_sm, assigned_sm, gain_ref, x_ref, w_ref, wo_ref, normed_ref, q_ref, k_ref, v_ref,
    slot_ref, query_slots_ref, windows_ref, windows_sm, pool_ref, meta_ref, share_ref, scores_ref, small_sems, x_sems, w_sems,
):
    length, tile, slots, capacity, block_rows, dp, mp, width, cents = sizes
    tiles = length // tile
    lane_blocks = length // LANES
    rows = dp * block_rows
    pairs = width // LANES
    row = lax.axis_index("dp")
    column = lax.axis_index("mp")

    small_copies = [
        pltpu.make_async_copy(ids_hbm, ids_ref, small_sems.at[0]),
        pltpu.make_async_copy(ids_hbm, ids_sm, small_sems.at[1]),
        pltpu.make_async_copy(assigned_hbm, assigned_sm, small_sems.at[2]),
        pltpu.make_async_copy(gain_hbm, gain_ref, small_sems.at[3]),
    ]
    x_copies = [
        pltpu.make_async_copy(x_hbm.at[pl.ds(i * tile, tile), :], x_ref.at[pl.ds(i * tile, tile), :], x_sems.at[i])
        for i in range(tiles)
    ]
    w_copies = [
        pltpu.make_async_copy(w_hbm, w_ref.at[:, pl.ds(i * width, width)], w_sems.at[i])
        for i, w_hbm in enumerate((wq_hbm, wk_hbm, wv_hbm))
    ] + [pltpu.make_async_copy(wo_hbm, wo_ref, w_sems.at[3])]
    for copy in small_copies + x_copies[:1]:
        copy.start()
    for copy in w_copies[:3]:
        copy.start(priority=1)
    for copy in x_copies[1:]:
        copy.start()
    w_copies[3].start(priority=1)
    for copy in small_copies:
        copy.wait()

    ids = ids_ref[...]
    local = ids - row * slots
    slot_ids = jnp.where(local < 0, slots, local)
    slot_rows = slot_ids.astype(F32)
    query_slots_ref[...] = slot_rows

    lane = iota((1, LANES), 1)
    named = jnp.full((1, LANES), -1, jnp.int32)
    for j in range(slots):
        named = jnp.where(lane == j, assigned_sm[0, j], named)
    owner = named // cents
    wide = jnp.broadcast_to(owner.astype(F32), (LANES, LANES))
    earlier = (wide.T == wide) & (iota((LANES, LANES), 0) < iota((LANES, LANES), 1))
    rank = jnp.sum(earlier.astype(F32), axis=0, keepdims=True)
    goes_to = jnp.where(lane < slots, owner.astype(F32) * block_rows + rank, -1.0)
    goes = jnp.take_along_axis(jnp.broadcast_to(goes_to, slot_rows.shape), slot_ids, axis=1)
    row_of = iota((rows, LANES), 0)
    continued = (row_of % block_rows == capacity).astype(F32)
    row_of = row_of.astype(F32)
    lane_number = iota((8, LANES), 1).astype(F32)
    counts = jnp.zeros((8, LANES), F32)
    for block in range(lane_blocks):
        here = slice(block * LANES, (block + 1) * LANES)
        slot = slot_rows[block:block + 1, :]
        upright = jnp.broadcast_to(slot, (LANES, LANES)).T
        slot_ref[here, :] = upright
        for part in range(0, LANES, 8):
            counts += (upright[part:part + 8] == lane_number).astype(F32)
        mine = jnp.where(row_of == goes[block:block + 1, :], 1.0, 0.0)
        pool_ref[:, here] = jnp.where(slot == slots, continued, mine).astype(BF)
    counts = jnp.broadcast_to(jnp.sum(counts, axis=0, keepdims=True), (8, LANES))

    def order(shape, dim):
        slot = iota(shape, dim)
        return jnp.where(slot == slots, 0, slot + 1)

    before = (order((LANES, LANES), 0) < order((LANES, LANES), 1)) & (iota((LANES, LANES), 0) <= slots)
    before = before.astype(F32).astype(BF)
    upper = counts.astype(BF)
    starts = dot(upper, before) + dot((counts - upper.astype(F32)).astype(BF), before)

    def at_position(values, position):
        mine = iota(slot_rows.shape, 1).astype(F32) == slot_rows[:, position:position + 1]
        return jnp.sum(jnp.where(mine, values[:1], 0.0), axis=1, keepdims=True)

    spot = iota(slot_rows.shape, 1)
    table = jnp.where(spot == 0, at_position(starts, 0), at_position(starts + counts, QB - 1))
    windows_ref[...] = table.astype(jnp.int32)
    windows_copy = pltpu.make_async_copy(windows_ref, windows_sm, small_sems.at[4])
    windows_copy.start()

    last_slot = ids_sm[lane_blocks - 1, LANES - 1] - row * slots
    speaks = (column == 0).astype(F32)
    meta_ref[0:1, :LANES] = goes_to * speaks
    meta_ref[0:1, LANES:] = counts[:1] * speaks
    meta_ref[1:2, :LANES] = named.astype(F32) * speaks
    meta_ref[1:2, LANES:] = (lane == last_slot).astype(F32) * speaks
    share_ref[...] = jnp.zeros_like(share_ref)

    own = pl.ds(pl.multiple_of(column * width, width), width)
    gain = gain_ref[...]
    piece_rows = 64
    pieces = tile // piece_rows
    lane_slices = [slice(j * LANES, (j + 1) * LANES) for j in range(D // LANES)]

    def piece_of(i, p, lanes):
        at = i * tile + p * piece_rows
        return x_ref[at:at + piece_rows, lanes].astype(F32)

    def averages(i):
        out = []
        for p in range(pieces):
            total = functools.reduce(jnp.add, [piece_of(i, p, lanes) for lanes in lane_slices])
            mean = jnp.sum(total, axis=1, keepdims=True) * (1.0 / D)
            out.append(jnp.broadcast_to(mean, (piece_rows, LANES)))
        return out

    def spreads(i, means):
        out = []
        for p in range(pieces):
            squares = jnp.zeros((piece_rows, LANES), F32)
            for lanes in lane_slices:
                centered = piece_of(i, p, lanes) - means[p]
                squares += centered * centered
            variance = jnp.sum(squares, axis=1, keepdims=True) * (1.0 / D)
            out.append(jnp.broadcast_to(lax.rsqrt(variance + 1e-05), (piece_rows, LANES)))
        return out

    def scale(i, means, inverses):
        for p in range(pieces):
            here = slice(p * piece_rows, (p + 1) * piece_rows)
            for lanes in lane_slices:
                scaled = (piece_of(i, p, lanes) - means[p]) * inverses[p] * gain[:, lanes]
                normed_ref[i % 2, here, lanes] = scaled.astype(BF)

    def project(i):
        here = slice(i * tile, (i + 1) * tile)
        result = dot(normed_ref[i % 2], w_ref[...])
        q_ref[here, :] = (result[:, :width] * (1.0 / math.sqrt(HEAD_DIM))).astype(BF)
        k_ref[here, :] = result[:, width:2 * width].astype(BF)
        v_ref[here, :] = result[:, 2 * width:].astype(BF)

    tokens_sum = jnp.zeros((rows, width), F32)
    means, inverses = {}, {}
    for i in range(-2, tiles):
        ahead = i + 2
        if ahead < tiles:
            x_copies[ahead].wait()
            means[ahead] = averages(ahead)
        if i == 0:
            for copy in w_copies[:3]:
                copy.wait()
        if 0 <= i + 1 < tiles:
            scale(i + 1, means[i + 1], inverses[i + 1])
        if i >= 0:
            project(i)
            here = slice(i * tile, (i + 1) * tile)
            tokens_sum += dot(pool_ref[:, here], x_ref[here, own])
        if ahead < tiles:
            inverses[ahead] = spreads(ahead, means[ahead])
    windows_copy.wait()

    def window(block):
        return (windows_sm[block, 0] // 16) * 16, windows_sm[block, 1]

    low_head = iota((QB, LANES), 1) < HEAD_DIM
    low_lane = iota((8, LANES), 1) < HEAD_DIM

    def scores_of(block, pair, at, extent):
        lanes = slice(pair * LANES, (pair + 1) * LANES)
        both = q_ref[pl.ds(pl.multiple_of(block * QB, QB), QB), lanes]
        zero = jnp.zeros_like(both)
        queries = jnp.concatenate(
            [jnp.where(low_head, both, zero), jnp.where(low_head, zero, both)], axis=0
        )
        return dot(k_ref[pl.ds(at, extent), lanes], queries, NT)

    def masked(scores, at, extent, mine):
        return jnp.where(slot_ref[pl.ds(at, extent), :] == mine, scores, -1e30)

    def by_eights(x):
        return x.reshape(x.shape[0] // 8, 8, LANES)

    def add_shares(pair, at, extent, first, second):
        low = jnp.broadcast_to(low_lane[:1], (extent, LANES))
        sums = [jnp.sum(x, axis=1, keepdims=True) for x in (first, second)]
        share_ref[pair, pl.ds(at, extent), :] += jnp.where(low, sums[0], sums[1])

    def straight(blocks, begins, extent):
        step = 64
        ats = [pl.multiple_of(jnp.minimum(begin, length - extent), 16) for begin in begins]
        chains = [(block, at, pair) for pair in range(pairs) for block, at in zip(blocks, ats)]
        sides = (slice(0, LANES), slice(LANES, 2 * LANES))
        for i, (block, at, pair) in enumerate(chains):
            scores_ref[i, :extent, :] = scores_of(block, pair, at, extent)
        tops = []
        for i, (block, at, pair) in enumerate(chains):
            mine = query_slots_ref[pl.ds(block, 1), :]
            top = [jnp.full((8, LANES), -1e30, F32) for _ in sides]
            for key in range(0, extent, step):
                for side, lanes in enumerate(sides):
                    kept = masked(scores_ref[i, key:key + step, lanes], at + key, step, mine)
                    scores_ref[i, key:key + step, lanes] = kept
                    top[side] = jnp.maximum(top[side], jnp.max(by_eights(kept), axis=0))
            tops.append([jnp.max(t, axis=0, keepdims=True) for t in top])
        inverses = []
        for i in range(len(chains)):
            total = [jnp.zeros((8, LANES), F32) for _ in sides]
            for key in range(0, extent, step):
                for side, lanes in enumerate(sides):
                    raised = jnp.exp(scores_ref[i, key:key + step, lanes] - tops[i][side])
                    total[side] += jnp.sum(by_eights(raised), axis=0)
                    scores_ref[i, key:key + step, lanes] = raised
            inverses.append([1.0 / jnp.sum(t, axis=0, keepdims=True) for t in total])
        for i, (block, at, pair) in enumerate(chains):
            for key in range(0, extent, step):
                weights = [
                    scores_ref[i, key:key + step, lanes] * inverses[i][side]
                    for side, lanes in enumerate(sides)
                ]
                add_shares(pair, pl.multiple_of(at + key, 16), step, *weights)

    def any_length(block):
        chunk = 256
        begin, end = window(block)
        first_chunk = begin // chunk
        end_chunk = (end + chunk - 1) // chunk
        mine = query_slots_ref[pl.ds(block, 1), :]
        mine = jnp.concatenate([mine, mine], axis=1)
        for pair in range(pairs):

            def scores_at(index):
                at = pl.multiple_of(index * chunk, chunk)
                keys = slot_ref[pl.ds(at, chunk), :]
                same = jnp.concatenate([keys, keys], axis=1) == mine
                return at, jnp.where(same, scores_of(block, pair, at, chunk), -1e30)

            def forward(index, carry):
                top, total = carry
                _, scores = scores_at(index)
                higher = jnp.maximum(top, jnp.max(scores, axis=0, keepdims=True))
                raised = jnp.sum(jnp.exp(scores - higher), axis=0, keepdims=True)
                return higher, total * jnp.exp(top - higher) + raised

            top, total = lax.fori_loop(
                first_chunk, end_chunk, forward,
                (jnp.full((1, 2 * QB), -1e30, F32), jnp.zeros((1, 2 * QB), F32)),
            )
            inverse = 1.0 / total

            def again(index, nothing):
                at, scores = scores_at(index)
                weights = jnp.exp(scores - top) * inverse
                add_shares(pair, at, chunk, weights[:, :QB], weights[:, QB:])
                return nothing

            lax.fori_loop(first_chunk, end_chunk, again, 0)

    def group_step(group, nothing):
        blocks = [group * GROUP + i for i in range(GROUP)]
        spans = [window(block) for block in blocks]
        begins = [begin for begin, _ in spans]
        widest = functools.reduce(jnp.maximum, [end - begin for begin, end in spans])
        done = jnp.int32(0)
        for extent in EXTENTS:
            if extent > length:
                break

            @pl.when((widest > done) & (widest <= extent))
            def run(extent=extent):
                straight(blocks, begins, extent)

            done = jnp.int32(extent)

        @pl.when(widest > done)
        def slow():
            def one(index, nothing):
                any_length(group * GROUP + index)
                return nothing

            lax.fori_loop(0, GROUP, one, 0)

        return nothing

    lax.fori_loop(0, length // QB // GROUP, group_step, 0)

    context = jnp.zeros((rows, width), F32)
    for at in range(0, length, tile):
        here = slice(at, at + tile)
        weighted = [
            v_ref[here, pair * LANES:(pair + 1) * LANES].astype(F32) * share_ref[pair, here, :]
            for pair in range(pairs)
        ]
        context += dot(pool_ref[:, here], jnp.concatenate(weighted, axis=1).astype(BF))
    upper = context.astype(BF)
    lower = (context - upper.astype(F32)).astype(BF)
    w_copies[3].wait()
    sent = dot(jnp.concatenate([upper, lower], axis=0), wo_ref[...])
    sent = sent[:rows] + sent[rows:]
    for target in range(mp):
        out_ref[target] = sent[:, target * width:(target + 1) * width]
    out_ref[column] += tokens_sum
    for target in range(mp):
        for block in range(dp):
            at = block * block_rows + capacity + 1
            out_ref[target, at:at + 2, :] = meta_ref[:2, :]


def row_sums(doc_ids, assigned, tokens, ln_gain, w_query, w_key, w_value, w_out, sizes):
    length, tile, slots, capacity, block_rows, dp, mp, width, cents = sizes
    rows = dp * block_rows
    return pl.pallas_call(
        functools.partial(row_kernel, sizes),
        in_specs=[pl.BlockSpec(memory_space=pltpu.HBM)] * 8,
        out_shape=jax.ShapeDtypeStruct((mp, rows, width), F32),
        scratch_shapes=[
            pltpu.VMEM((length // LANES, LANES), jnp.int32),
            pltpu.SMEM((length // LANES, LANES), jnp.int32),
            pltpu.SMEM((1, slots), jnp.int32),
            pltpu.VMEM((1, D), F32),
            pltpu.VMEM((length, D), BF),
            pltpu.VMEM((D, 3 * width), BF),
            pltpu.VMEM((width, D), BF),
            pltpu.VMEM((2, tile, D), BF),
            pltpu.VMEM((length, width), BF),
            pltpu.VMEM((length, width), BF),
            pltpu.VMEM((length, width), BF),
            pltpu.VMEM((length, LANES), F32),
            pltpu.VMEM((length // LANES, LANES), F32),
            pltpu.VMEM((length // LANES, LANES), jnp.int32),
            pltpu.SMEM((length // LANES, LANES), jnp.int32),
            pltpu.VMEM((rows, length), BF),
            pltpu.VMEM((8, 2 * LANES), F32),
            pltpu.VMEM((width // LANES, length, LANES), F32),
            pltpu.VMEM((GROUP * width // LANES, EXTENTS[-1], 2 * QB), F32),
            pltpu.SemaphoreType.DMA((5,)),
            pltpu.SemaphoreType.DMA((length // tile,)),
            pltpu.SemaphoreType.DMA((4,)),
        ],
        compiler_params=pltpu.CompilerParams(vmem_limit_bytes=62 * 1024 * 1024),
        name="row_sums",
    )(
        doc_ids.reshape(length // LANES, LANES), assigned.reshape(1, slots), ln_gain.reshape(1, D),
        tokens, w_query, w_key, w_value, w_out,
    )


def products_kernel(
    sizes, here_ref, own_ref, cent_ref, mass_ref, pay_ref, docs_ref, near_ref, info_ref, own_out_ref
):
    length, tile, slots, capacity, block_rows, dp, mp, width, cents = sizes
    me = lax.axis_index("dp")
    rows = dp * block_rows
    lane = iota((1, LANES), 1)

    def rows_of(meta, first_row, count):
        goes_to, counts = meta[0:1, :LANES], meta[0:1, LANES:]
        named, is_last = meta[1:2, :LANES], meta[1:2, LANES:]
        held = (goes_to == (iota((count, LANES), 0) + first_row).astype(F32)).astype(F32)

        def column(values):
            return jnp.sum(held * values, axis=1, keepdims=True)

        return column(named), column(counts), column(is_last), column(jnp.ones((1, LANES), F32))

    def carry_of(source):
        block = here_ref[pl.ds(pl.multiple_of(source * block_rows, 8), block_rows), :]
        counts = block[capacity + 1:capacity + 2, LANES:]
        count = jnp.sum(jnp.where(lane == slots, counts, 0.0), axis=1, keepdims=True)
        return block[capacity:capacity + 1, :], count

    columns = []
    for source in range(dp):
        base = source * block_rows
        block = here_ref[base:base + block_rows, :]
        meta = block[capacity + 1:capacity + 3, :]
        named, counts, is_last, held = rows_of(meta, me * block_rows, block_rows)
        sums = jnp.where(held > 0, block, 0.0)
        if source < dp - 1:
            carry, carry_count = carry_of(source + 1)
            sums = sums + is_last * carry
            counts = counts + is_last * carry_count
        docs_ref[base:base + block_rows, :] = sums
        columns.append((named - (me * cents).astype(F32), counts, held))
    local = jnp.concatenate([c[0] for c in columns], axis=0)
    counts = jnp.concatenate([c[1] for c in columns], axis=0)
    held = jnp.concatenate([c[2] for c in columns], axis=0)
    valid = ((held > 0) & (counts > 0)).astype(F32)

    docs = docs_ref[...]
    names = (iota((rows, cents), 1).astype(F32) == local) & (valid > 0)
    names = names.astype(F32)
    mass = jnp.sum(names * mass_ref[...], axis=1, keepdims=True)
    near = pick_rows(names.astype(BF), cent_ref[...])
    near_ref[...] = near

    own = own_ref[...]
    _, own_counts, own_last, _ = rows_of(own_ref[capacity + 1:capacity + 3, :], 0, rows)
    following = jnp.minimum(me + 1, dp - 1)
    more = (me < dp - 1).astype(F32)
    carry, carry_count = carry_of(following)
    own = own + own_last * (carry * more)
    own_counts = own_counts + own_last * (carry_count * more)
    own_out_ref[...] = own

    gram = dot(docs, docs, NT, precision=lax.Precision.HIGHEST)
    spot = iota((rows, LANES), 1)
    cross = jnp.sum(near * docs, axis=1, keepdims=True)
    square = jnp.sum(near * near, axis=1, keepdims=True)
    own_square = jnp.sum(own * own, axis=1, keepdims=True)
    doc_square = jnp.sum(docs * docs, axis=1, keepdims=True)
    pay_ref[0] = jnp.zeros(pay_ref.shape[1:], F32)
    pay_ref[0, :, :rows] = gram
    for i, sums in enumerate((cross, square, own_square, doc_square)):
        pay_ref[0, :, rows + i:rows + i + 1] = sums
    for target in range(1, mp):
        pay_ref[target] = pay_ref[0]
    info_ref[...] = jnp.where(
        spot == 0, local, jnp.where(spot == 1, counts, jnp.where(spot == 2, valid, jnp.where(spot == 3, mass, own_counts)))
    )


def update_kernel(
    sizes, pay_ref, docs_ref, near_ref, info_ref, own_ref, meta_ref, cent_ref, vec_ref, new_ref
):
    length, tile, slots, capacity, block_rows, dp, mp, width, cents = sizes
    rows = dp * block_rows
    info = info_ref[...]
    local, counts, valid, mass, own_counts = (info[:, i:i + 1] for i in range(5))
    pay = functools.reduce(jnp.add, [pay_ref[i] for i in range(mp)])
    cross, square, own_square, doc_square = (pay[:, rows + i:rows + i + 1] for i in range(4))

    def scale(sums, count):
        inverse = 1.0 / jnp.maximum(count, 1.0)
        return inverse * lax.rsqrt(sums * inverse * inverse * (1.0 / D) + 1e-06)

    vectors = own_ref[...] * scale(own_square, own_counts)
    goes_to = meta_ref[capacity + 1:capacity + 2, :LANES]
    place = ((iota((rows, LANES), 0).astype(F32) == goes_to).astype(F32)).T
    vec_ref[...] = pick_rows(place[:slots].astype(BF), vectors)

    share = scale(doc_square, counts) * valid
    across = jnp.where(valid > 0, local, -1.0)
    flat = jnp.broadcast_to(across, (rows, LANES)).T[:1]
    share_flat = jnp.broadcast_to(share, (rows, LANES)).T[:1]
    cross_flat = jnp.broadcast_to(cross, (rows, LANES)).T[:1]
    same = (across == flat) & (valid > 0)
    mixed = jnp.where(same, share_flat, 0.0)
    gained = dot(mixed, docs_ref[...], precision=lax.Precision.HIGHEST)
    twice = dot(mixed, pay[:, :rows], precision=lax.Precision.HIGHEST)
    norm = (
        mass * mass * square
        + 2.0 * mass * jnp.sum(mixed * cross_flat, axis=1, keepdims=True)
        + jnp.sum(twice * mixed, axis=1, keepdims=True)
    )
    blended = mass * near_ref[...] + gained
    scaled = blended * lax.rsqrt(norm * (1.0 / D) + 1e-06)
    before = same & (iota((rows, rows), 0) < iota((rows, rows), 1))
    repeated = jnp.sum(before.astype(F32), axis=0, keepdims=True)
    target = jnp.where((flat >= 0) & (repeated < 0.5), flat, -1.0)
    hits = (iota((cents, rows), 0).astype(F32) == target).astype(F32)
    updated = pick_rows(hits.astype(BF), scaled)
    hit = jnp.sum(hits, axis=1, keepdims=True)
    new_ref[...] = jnp.where(hit > 0, updated, cent_ref[...])


def shards(
    tokens, doc_ids, ln_gain, w_query, w_key, w_value, w_out, centroids, cluster_mass, assigned
):
    length = tokens.shape[0]
    slots = assigned.shape[0]
    width = w_out.shape[0]
    cents = centroids.shape[0]
    dp = lax.axis_size("dp")
    mp = lax.axis_size("mp")
    capacity = max(2, (slots + dp - 2) // (dp - 1))
    block_rows = round_up(capacity + 3, 8)
    rows = dp * block_rows
    sizes = (length, min(256, length), slots, capacity, block_rows, dp, mp, width, cents)
    limit = pltpu.CompilerParams(vmem_limit_bytes=48 * 1024 * 1024)

    partial = row_sums(doc_ids, assigned, tokens, ln_gain, w_query, w_key, w_value, w_out, sizes)
    shared = lax.all_to_all(partial, "mp", split_axis=0, concat_axis=0, tiled=True)
    own = jnp.sum(shared, axis=0)
    here = lax.all_to_all(own, "dp", split_axis=0, concat_axis=0, tiled=True)

    pay, docs, near, info, own_sums = pl.pallas_call(
        functools.partial(products_kernel, sizes),
        out_shape=(
            jax.ShapeDtypeStruct((mp, rows, round_up(rows + 4, LANES)), F32),
            jax.ShapeDtypeStruct((rows, width), F32),
            jax.ShapeDtypeStruct((rows, width), F32),
            jax.ShapeDtypeStruct((rows, LANES), F32),
            jax.ShapeDtypeStruct((rows, width), F32),
        ),
        compiler_params=limit,
        name="products",
    )(here, own, centroids, cluster_mass.reshape(1, cents))
    pay = lax.all_to_all(pay, "mp", split_axis=0, concat_axis=0, tiled=True)
    return pl.pallas_call(
        functools.partial(update_kernel, sizes),
        out_shape=(
            jax.ShapeDtypeStruct((slots, width), F32),
            jax.ShapeDtypeStruct((cents, width), F32),
        ),
        compiler_params=limit,
        name="update",
    )(pay, docs, near, info, own_sums, own, centroids)


def solution(mesh):
    placed = (
        P("dp", None),
        P("dp"),
        P(),
        P(None, "mp"),
        P(None, "mp"),
        P(None, "mp"),
        P("mp", None),
        P("dp", "mp"),
        P("dp"),
        P("dp"),
    )
    return jax.shard_map(
        shards,
        mesh=mesh,
        in_specs=placed,
        out_specs=(P("dp", "mp"), P("dp", "mp")),
        check_vma=False,
    )
```

```python
import functools
import math

import jax
import jax.numpy as jnp
from jax import lax
from jax.experimental import pallas as pl
from jax.experimental.pallas import tpu as pltpu
from jax.sharding import PartitionSpec as P

D = 1024
HEAD_DIM = 64
QB = 64
GROUP = 8
EXTENTS = (192, 256, 384, 640)
LANES = 128
BF = jnp.bfloat16
F32 = jnp.float32

NN = (((1,), (0,)), ((), ()))
NT = (((1,), (1,)), ((), ()))
TN = (((0,), (0,)), ((), ()))


def dot(a, b, dims=NN, precision=None):
    return lax.dot_general(a, b, dims, preferred_element_type=F32, precision=precision)


def iota(shape, dim):
    return lax.broadcasted_iota(jnp.int32, shape, dim)


def thirds(x):
    first = x.astype(BF)
    rest = x - first.astype(F32)
    second = rest.astype(BF)
    third = (rest - second.astype(F32)).astype(BF)
    return first, second, third


def pick_rows(one_hot, x, dims=NN):
    first, second, third = thirds(x)
    return dot(one_hot, first, dims) + (dot(one_hot, second, dims) + dot(one_hot, third, dims))


def round_up(n, by):
    return (n + by - 1) // by * by


def row_kernel(
    sizes, ids_hbm, assigned_hbm, gain_hbm, x_hbm, wq_hbm, wk_hbm, wv_hbm, wo_hbm, out_ref,
    ids_ref, ids_sm, assigned_sm, gain_ref, x_ref, w_ref, wo_ref, normed_ref, q_ref, k_ref, v_ref,
    slot_ref, query_slots_ref, windows_ref, windows_sm, pool_ref, meta_ref, share_ref, scores_ref, raised_ref, small_sems, x_sems, w_sems,
):
    length, tile, slots, capacity, block_rows, dp, mp, width, cents = sizes
    tiles = length // tile
    lane_blocks = length // LANES
    rows = dp * block_rows
    heads = width // HEAD_DIM
    halves = width // LANES
    row = lax.axis_index("dp")
    column = lax.axis_index("mp")

    small_copies = [
        pltpu.make_async_copy(ids_hbm, ids_ref, small_sems.at[0]),
        pltpu.make_async_copy(ids_hbm, ids_sm, small_sems.at[1]),
        pltpu.make_async_copy(assigned_hbm, assigned_sm, small_sems.at[2]),
        pltpu.make_async_copy(gain_hbm, gain_ref, small_sems.at[3]),
    ]
    x_copies = [
        pltpu.make_async_copy(x_hbm.at[pl.ds(i * tile, tile), :], x_ref.at[pl.ds(i * tile, tile), :], x_sems.at[i])
        for i in range(tiles)
    ]
    w_copies = [
        pltpu.make_async_copy(w_hbm, w_ref.at[i], w_sems.at[i])
        for i, w_hbm in enumerate((wq_hbm, wk_hbm, wv_hbm))
    ] + [pltpu.make_async_copy(wo_hbm, wo_ref, w_sems.at[3])]
    for copy in small_copies + x_copies[:1]:
        copy.start()
    for copy in w_copies[:3]:
        copy.start(priority=1)
    for copy in x_copies[1:]:
        copy.start()
    w_copies[3].start(priority=1)
    for copy in small_copies:
        copy.wait()

    ids = ids_ref[...]
    local = ids - row * slots
    slot_ids = jnp.where(local < 0, slots, local)
    slot_rows = slot_ids.astype(F32)
    turned = pltpu.roll(slot_rows, QB, 1)
    front = iota(slot_rows.shape, 1) < QB
    query_slots_ref[0] = jnp.where(front, slot_rows, turned)
    query_slots_ref[1] = jnp.where(front, turned, slot_rows)

    lane = iota((1, LANES), 1)
    named = jnp.full((1, LANES), -1, jnp.int32)
    for j in range(slots):
        named = jnp.where(lane == j, assigned_sm[0, j], named)
    owner = named // cents
    wide = jnp.broadcast_to(owner.astype(F32), (LANES, LANES))
    earlier = (wide.T == wide) & (iota((LANES, LANES), 0) < iota((LANES, LANES), 1))
    rank = jnp.sum(earlier.astype(F32), axis=0, keepdims=True)
    goes_to = jnp.where(lane < slots, owner.astype(F32) * block_rows + rank, -1.0)
    goes = jnp.take_along_axis(jnp.broadcast_to(goes_to, slot_rows.shape), slot_ids, axis=1)
    row_of = iota((rows, LANES), 0)
    continued = (row_of % block_rows == capacity).astype(F32)
    row_of = row_of.astype(F32)
    lane_number = iota((8, LANES), 1).astype(F32)
    counts = jnp.zeros((8, LANES), F32)
    for block in range(lane_blocks):
        here = slice(block * LANES, (block + 1) * LANES)
        slot = slot_rows[block:block + 1, :]
        upright = jnp.broadcast_to(slot, (LANES, LANES)).T
        slot_ref[here, :] = upright
        for part in range(0, LANES, 8):
            counts += (upright[part:part + 8] == lane_number).astype(F32)
        mine = jnp.where(row_of == goes[block:block + 1, :], 1.0, 0.0)
        pool_ref[:, here] = jnp.where(slot == slots, continued, mine).astype(BF)
    counts = jnp.broadcast_to(jnp.sum(counts, axis=0, keepdims=True), (8, LANES))

    def order(shape, dim):
        slot = iota(shape, dim)
        return jnp.where(slot == slots, 0, slot + 1)

    before = (order((LANES, LANES), 0) < order((LANES, LANES), 1)) & (iota((LANES, LANES), 0) <= slots)
    before = before.astype(F32).astype(BF)
    upper = counts.astype(BF)
    starts = dot(upper, before) + dot((counts - upper.astype(F32)).astype(BF), before)

    def at_position(values, position):
        mine = iota(slot_rows.shape, 1).astype(F32) == slot_rows[:, position:position + 1]
        return jnp.sum(jnp.where(mine, values[:1], 0.0), axis=1, keepdims=True)

    spot = iota(slot_rows.shape, 1)
    table = jnp.zeros(slot_rows.shape, F32)
    for part in range(LANES // QB):
        table = jnp.where(spot == 2 * part, at_position(starts, part * QB), table)
        table = jnp.where(spot == 2 * part + 1, at_position(starts + counts, (part + 1) * QB - 1), table)
    windows_ref[...] = table.astype(jnp.int32)
    windows_copy = pltpu.make_async_copy(windows_ref, windows_sm, small_sems.at[4])
    windows_copy.start()

    last_slot = ids_sm[lane_blocks - 1, LANES - 1] - row * slots
    speaks = (column == 0).astype(F32)
    meta_ref[0:1, :LANES] = goes_to * speaks
    meta_ref[0:1, LANES:] = counts[:1] * speaks
    meta_ref[1:2, :LANES] = named.astype(F32) * speaks
    meta_ref[1:2, LANES:] = (lane == last_slot).astype(F32) * speaks
    share_ref[...] = jnp.zeros_like(share_ref)

    own = pl.ds(pl.multiple_of(column * width, width), width)
    gain = gain_ref[...]
    piece_rows = 64
    pieces = tile // piece_rows
    lane_slices = [slice(j * LANES, (j + 1) * LANES) for j in range(D // LANES)]

    def piece_of(i, p, lanes):
        at = i * tile + p * piece_rows
        return x_ref[at:at + piece_rows, lanes].astype(F32)

    def normalise(i, group):
        means, inverses = [], []
        for p in group:
            total = functools.reduce(jnp.add, [piece_of(i, p, lanes) for lanes in lane_slices])
            mean = jnp.sum(total, axis=1, keepdims=True) * (1.0 / D)
            means.append(jnp.broadcast_to(mean, (piece_rows, LANES)))
        for p, mean in zip(group, means):
            squares = jnp.zeros((piece_rows, LANES), F32)
            for lanes in lane_slices:
                centered = piece_of(i, p, lanes) - mean
                squares += centered * centered
            variance = jnp.sum(squares, axis=1, keepdims=True) * (1.0 / D)
            inverses.append(jnp.broadcast_to(lax.rsqrt(variance + 1e-05), (piece_rows, LANES)))
        for p, mean, inverse in zip(group, means, inverses):
            here = slice(p * piece_rows, (p + 1) * piece_rows)
            for lanes in lane_slices:
                scaled = (piece_of(i, p, lanes) - mean) * inverse * gain[:, lanes]
                normed_ref[i % 2, here, lanes] = scaled.astype(BF)

    def project(i, which):
        here = slice(i * tile, (i + 1) * tile)
        result = dot(normed_ref[i % 2], w_ref[which])
        if which == 0:
            result = result * (1.0 / math.sqrt(HEAD_DIM))
        (q_ref, k_ref, v_ref)[which][here, :] = result.astype(BF)

    groups = [range(pieces * g // 3, pieces * (g + 1) // 3) for g in range(3)]
    tokens_sum = jnp.zeros((rows, width), F32)
    x_copies[0].wait()
    for group in groups:
        normalise(0, group)
    for copy in w_copies[:3]:
        copy.wait()
    for i in range(tiles):
        if i + 1 < tiles:
            x_copies[i + 1].wait()
        for which, group in enumerate(groups):
            if i + 1 < tiles:
                normalise(i + 1, group)
            project(i, which)
        here = slice(i * tile, (i + 1) * tile)
        tokens_sum += dot(pool_ref[:, here], x_ref[here, own])
    windows_copy.wait()

    def window(block_pair, part):
        return (windows_sm[block_pair, 2 * part] // 16) * 16, windows_sm[block_pair, 2 * part + 1]

    def all_heads(block):
        at = pl.multiple_of(block * QB, QB)
        zero = jnp.zeros((QB, LANES), BF)
        left = iota((QB, LANES), 1) < HEAD_DIM
        stacked = []
        for half in range(halves):
            piece = q_ref[pl.ds(at, QB), half * LANES:(half + 1) * LANES]
            for kept in (left, jnp.logical_not(left)):
                mine = jnp.where(kept, piece, zero)
                stacked.append(jnp.concatenate([mine if h == half else zero for h in range(halves)], axis=1))
        return jnp.concatenate(stacked, axis=0)

    head_of_lane = (iota((8, width), 1) // HEAD_DIM) == (iota((8, width), 0) % heads)
    upper_rows = iota((8, width), 0) < heads

    def key_shares(raised, inverse):
        upper = inverse.astype(BF).astype(F32)
        parts = jnp.where(upper_rows, upper, inverse - upper)
        return dot(jnp.where(head_of_lane, parts, 0.0).astype(BF), raised, NT)

    def straight(blocks, begins, extent):
        padded = round_up(extent, LANES)
        step = 64
        ats = [pl.multiple_of(jnp.minimum(begin, length - extent), 16) for begin in begins]
        halves_of = [slice(half * LANES, (half + 1) * LANES) for half in range(halves)]
        for i, (block, at) in enumerate(zip(blocks, ats)):
            scores_ref[i, :extent, :] = dot(k_ref[pl.ds(at, extent), :], all_heads(block), NT)
        tops = []
        for i, (block, at) in enumerate(zip(blocks, ats)):
            mine = query_slots_ref[i % 2, pl.ds(block // 2, 1), :]
            top = [jnp.full((8, LANES), -1e30, F32) for _ in range(halves)]
            for key in range(0, extent, step):
                same = slot_ref[pl.ds(at + key, step), :] == mine
                for half, lanes in enumerate(halves_of):
                    masked = jnp.where(same, scores_ref[i, key:key + step, lanes], -1e30)
                    scores_ref[i, key:key + step, lanes] = masked
                    highest = jnp.max(masked.reshape(step // 8, 8, LANES), axis=0)
                    top[half] = jnp.maximum(top[half], highest)
            tops.append([jnp.max(t, axis=0, keepdims=True) for t in top])
        inverses = []
        for i in range(len(blocks)):
            total = [jnp.zeros((8, LANES), F32) for _ in range(halves)]
            for key in range(0, extent, step):
                for half, lanes in enumerate(halves_of):
                    raised = jnp.exp(scores_ref[i, key:key + step, lanes] - tops[i][half])
                    total[half] += jnp.sum(raised.reshape(step // 8, 8, LANES), axis=0)
                    raised_ref[i, key:key + step, lanes] = raised.astype(BF)
            if padded > extent:
                raised_ref[i, extent:padded, :] = jnp.zeros((padded - extent, width), BF)
            inverses.append(
                jnp.concatenate([1.0 / jnp.sum(t, axis=0, keepdims=True) for t in total], axis=1)
            )
        for i, at in enumerate(ats):
            shares = key_shares(raised_ref[i, :padded, :], inverses[i])
            shares = jnp.concatenate([shares, jnp.zeros((8, LANES), F32)], axis=1)
            base = pl.multiple_of((at // LANES) * LANES, LANES)
            share_ref[:, pl.ds(base, padded + LANES)] += pltpu.roll(shares, at % LANES, 1)

    def any_length(block):
        chunk = 256
        begin, end = window(block // 2, block % 2)
        first_chunk = begin // chunk
        end_chunk = (end + chunk - 1) // chunk

        def scores_at(index):
            at = pl.multiple_of(index * chunk, chunk)
            scores = dot(k_ref[pl.ds(at, chunk), :], all_heads(block), NT)
            even = query_slots_ref[0, pl.ds(block // 2, 1), :]
            odd = query_slots_ref[1, pl.ds(block // 2, 1), :]
            query_slots = jnp.where(block % 2 == 0, even, odd)
            same = slot_ref[pl.ds(at, chunk), :] == query_slots
            masked = [
                jnp.where(same, scores[:, half * LANES:(half + 1) * LANES], -1e30) for half in range(halves)
            ]
            return at, jnp.concatenate(masked, axis=1)

        def forward(index, carry):
            top, total = carry
            _, scores = scores_at(index)
            higher = jnp.maximum(top, jnp.max(scores, axis=0, keepdims=True))
            raised = jnp.sum(jnp.exp(scores - higher), axis=0, keepdims=True)
            return higher, total * jnp.exp(top - higher) + raised

        top, total = lax.fori_loop(
            first_chunk, end_chunk, forward,
            (jnp.full((1, width), -1e30, F32), jnp.zeros((1, width), F32)),
        )
        inverse = 1.0 / total

        def again(index, nothing):
            at, scores = scores_at(index)
            share_ref[:, pl.ds(at, chunk)] += key_shares(jnp.exp(scores - top).astype(BF), inverse)
            return nothing

        lax.fori_loop(first_chunk, end_chunk, again, 0)

    def group_step(group, nothing):
        blocks = [group * GROUP + i for i in range(GROUP)]
        spans = [window(group * (GROUP // 2) + i // 2, i % 2) for i in range(GROUP)]
        begins = [begin for begin, _ in spans]
        widest = functools.reduce(jnp.maximum, [end - begin for begin, end in spans])
        done = jnp.int32(0)
        for extent in EXTENTS:
            if extent > length:
                break

            @pl.when((widest > done) & (widest <= extent))
            def run(extent=extent):
                straight(blocks, begins, extent)

            done = jnp.int32(extent)

        @pl.when(widest > done)
        def slow():
            def one(index, nothing):
                any_length(group * GROUP + index)
                return nothing

            lax.fori_loop(0, GROUP, one, 0)

        return nothing

    lax.fori_loop(0, length // QB // GROUP, group_step, 0)

    shares = share_ref[:, :length]
    pool = pool_ref[...]
    weighted = jnp.concatenate(
        [pool * (shares[h:h + 1] + shares[heads + h:heads + h + 1]).astype(BF) for h in range(heads)], axis=0
    )
    every = dot(weighted, v_ref[...])
    lane_head = iota((rows, width), 1) // HEAD_DIM
    context = jnp.zeros((rows, width), F32)
    for h in range(heads):
        context = jnp.where(lane_head == h, every[h * rows:(h + 1) * rows], context)
    upper = context.astype(BF)
    lower = (context - upper.astype(F32)).astype(BF)
    w_copies[3].wait()
    sent = dot(jnp.concatenate([upper, lower], axis=0), wo_ref[...])
    sent = sent[:rows] + sent[rows:]
    for target in range(mp):
        out_ref[target] = sent[:, target * width:(target + 1) * width]
    out_ref[column] += tokens_sum
    for target in range(mp):
        for block in range(dp):
            at = block * block_rows + capacity + 1
            out_ref[target, at:at + 2, :] = meta_ref[:2, :]


def row_sums(doc_ids, assigned, tokens, ln_gain, w_query, w_key, w_value, w_out, sizes):
    length, tile, slots, capacity, block_rows, dp, mp, width, cents = sizes
    rows = dp * block_rows
    return pl.pallas_call(
        functools.partial(row_kernel, sizes),
        in_specs=[pl.BlockSpec(memory_space=pltpu.HBM)] * 8,
        out_shape=jax.ShapeDtypeStruct((mp, rows, width), F32),
        scratch_shapes=[
            pltpu.VMEM((length // LANES, LANES), jnp.int32),
            pltpu.SMEM((length // LANES, LANES), jnp.int32),
            pltpu.SMEM((1, slots), jnp.int32),
            pltpu.VMEM((1, D), F32),
            pltpu.VMEM((length, D), BF),
            pltpu.VMEM((3, D, width), BF),
            pltpu.VMEM((width, D), BF),
            pltpu.VMEM((2, tile, D), BF),
            pltpu.VMEM((length, width), BF),
            pltpu.VMEM((length, width), BF),
            pltpu.VMEM((length, width), BF),
            pltpu.VMEM((length, LANES), F32),
            pltpu.VMEM((2, length // LANES, LANES), F32),
            pltpu.VMEM((length // LANES, LANES), jnp.int32),
            pltpu.SMEM((length // LANES, LANES), jnp.int32),
            pltpu.VMEM((rows, length), BF),
            pltpu.VMEM((8, 2 * LANES), F32),
            pltpu.VMEM((8, length + 2 * LANES), F32),
            pltpu.VMEM((GROUP, EXTENTS[-1], width), F32),
            pltpu.VMEM((GROUP, EXTENTS[-1], width), BF),
            pltpu.SemaphoreType.DMA((5,)),
            pltpu.SemaphoreType.DMA((length // tile,)),
            pltpu.SemaphoreType.DMA((4,)),
        ],
        compiler_params=pltpu.CompilerParams(vmem_limit_bytes=62 * 1024 * 1024),
        name="row_sums",
    )(
        doc_ids.reshape(length // LANES, LANES), assigned.reshape(1, slots), ln_gain.reshape(1, D),
        tokens, w_query, w_key, w_value, w_out,
    )


def products_kernel(
    sizes, here_ref, own_ref, cent_ref, mass_ref, pay_ref, docs_ref, near_ref, info_ref, own_out_ref
):
    length, tile, slots, capacity, block_rows, dp, mp, width, cents = sizes
    me = lax.axis_index("dp")
    rows = dp * block_rows
    lane = iota((1, LANES), 1)

    def rows_of(meta, first_row, count):
        goes_to, counts = meta[0:1, :LANES], meta[0:1, LANES:]
        named, is_last = meta[1:2, :LANES], meta[1:2, LANES:]
        held = (goes_to == (iota((count, LANES), 0) + first_row).astype(F32)).astype(F32)

        def column(values):
            return jnp.sum(held * values, axis=1, keepdims=True)

        return column(named), column(counts), column(is_last), column(jnp.ones((1, LANES), F32))

    def carry_of(source):
        block = here_ref[pl.ds(pl.multiple_of(source * block_rows, 8), block_rows), :]
        counts = block[capacity + 1:capacity + 2, LANES:]
        count = jnp.sum(jnp.where(lane == slots, counts, 0.0), axis=1, keepdims=True)
        return block[capacity:capacity + 1, :], count

    columns = []
    for source in range(dp):
        base = source * block_rows
        block = here_ref[base:base + block_rows, :]
        meta = block[capacity + 1:capacity + 3, :]
        named, counts, is_last, held = rows_of(meta, me * block_rows, block_rows)
        sums = jnp.where(held > 0, block, 0.0)
        if source < dp - 1:
            carry, carry_count = carry_of(source + 1)
            sums = sums + is_last * carry
            counts = counts + is_last * carry_count
        docs_ref[base:base + block_rows, :] = sums
        columns.append((named - (me * cents).astype(F32), counts, held))
    local = jnp.concatenate([c[0] for c in columns], axis=0)
    counts = jnp.concatenate([c[1] for c in columns], axis=0)
    held = jnp.concatenate([c[2] for c in columns], axis=0)
    valid = ((held > 0) & (counts > 0)).astype(F32)

    docs = docs_ref[...]
    names = (iota((rows, cents), 1).astype(F32) == local) & (valid > 0)
    names = names.astype(F32)
    mass = jnp.sum(names * mass_ref[...], axis=1, keepdims=True)
    near = pick_rows(names.astype(BF), cent_ref[...])
    near_ref[...] = near

    own = own_ref[...]
    _, own_counts, own_last, _ = rows_of(own_ref[capacity + 1:capacity + 3, :], 0, rows)
    following = jnp.minimum(me + 1, dp - 1)
    more = (me < dp - 1).astype(F32)
    carry, carry_count = carry_of(following)
    own = own + own_last * (carry * more)
    own_counts = own_counts + own_last * (carry_count * more)
    own_out_ref[...] = own

    gram = dot(docs, docs, NT, precision=lax.Precision.HIGHEST)
    spot = iota((rows, LANES), 1)
    cross = jnp.sum(near * docs, axis=1, keepdims=True)
    square = jnp.sum(near * near, axis=1, keepdims=True)
    own_square = jnp.sum(own * own, axis=1, keepdims=True)
    doc_square = jnp.sum(docs * docs, axis=1, keepdims=True)
    pay_ref[0] = jnp.zeros(pay_ref.shape[1:], F32)
    pay_ref[0, :, :rows] = gram
    for i, sums in enumerate((cross, square, own_square, doc_square)):
        pay_ref[0, :, rows + i:rows + i + 1] = sums
    for target in range(1, mp):
        pay_ref[target] = pay_ref[0]
    info_ref[...] = jnp.where(
        spot == 0, local, jnp.where(spot == 1, counts, jnp.where(spot == 2, valid, jnp.where(spot == 3, mass, own_counts)))
    )


def update_kernel(
    sizes, pay_ref, docs_ref, near_ref, info_ref, own_ref, meta_ref, cent_ref, vec_ref, new_ref
):
    length, tile, slots, capacity, block_rows, dp, mp, width, cents = sizes
    rows = dp * block_rows
    info = info_ref[...]
    local, counts, valid, mass, own_counts = (info[:, i:i + 1] for i in range(5))
    pay = functools.reduce(jnp.add, [pay_ref[i] for i in range(mp)])
    cross, square, own_square, doc_square = (pay[:, rows + i:rows + i + 1] for i in range(4))

    def scale(sums, count):
        inverse = 1.0 / jnp.maximum(count, 1.0)
        return inverse * lax.rsqrt(sums * inverse * inverse * (1.0 / D) + 1e-06)

    vectors = own_ref[...] * scale(own_square, own_counts)
    goes_to = meta_ref[capacity + 1:capacity + 2, :LANES]
    place = ((iota((rows, LANES), 0).astype(F32) == goes_to).astype(F32)).T
    vec_ref[...] = pick_rows(place[:slots].astype(BF), vectors)

    share = scale(doc_square, counts) * valid
    across = jnp.where(valid > 0, local, -1.0)
    flat = jnp.broadcast_to(across, (rows, LANES)).T[:1]
    share_flat = jnp.broadcast_to(share, (rows, LANES)).T[:1]
    cross_flat = jnp.broadcast_to(cross, (rows, LANES)).T[:1]
    same = (across == flat) & (valid > 0)
    mixed = jnp.where(same, share_flat, 0.0)
    gained = dot(mixed, docs_ref[...], precision=lax.Precision.HIGHEST)
    twice = dot(mixed, pay[:, :rows], precision=lax.Precision.HIGHEST)
    norm = (
        mass * mass * square
        + 2.0 * mass * jnp.sum(mixed * cross_flat, axis=1, keepdims=True)
        + jnp.sum(twice * mixed, axis=1, keepdims=True)
    )
    blended = mass * near_ref[...] + gained
    scaled = blended * lax.rsqrt(norm * (1.0 / D) + 1e-06)
    before = same & (iota((rows, rows), 0) < iota((rows, rows), 1))
    repeated = jnp.sum(before.astype(F32), axis=0, keepdims=True)
    target = jnp.where((flat >= 0) & (repeated < 0.5), flat, -1.0)
    hits = (iota((cents, rows), 0).astype(F32) == target).astype(F32)
    updated = pick_rows(hits.astype(BF), scaled)
    hit = jnp.sum(hits, axis=1, keepdims=True)
    new_ref[...] = jnp.where(hit > 0, updated, cent_ref[...])


def shards(
    tokens, doc_ids, ln_gain, w_query, w_key, w_value, w_out, centroids, cluster_mass, assigned
):
    length = tokens.shape[0]
    slots = assigned.shape[0]
    width = w_out.shape[0]
    cents = centroids.shape[0]
    dp = lax.axis_size("dp")
    mp = lax.axis_size("mp")
    capacity = max(2, (slots + dp - 2) // (dp - 1))
    block_rows = round_up(capacity + 3, 8)
    rows = dp * block_rows
    sizes = (length, min(512, length), slots, capacity, block_rows, dp, mp, width, cents)
    limit = pltpu.CompilerParams(vmem_limit_bytes=48 * 1024 * 1024)

    partial = row_sums(doc_ids, assigned, tokens, ln_gain, w_query, w_key, w_value, w_out, sizes)
    shared = lax.all_to_all(partial, "mp", split_axis=0, concat_axis=0, tiled=True)
    own = jnp.sum(shared, axis=0)
    here = lax.all_to_all(own, "dp", split_axis=0, concat_axis=0, tiled=True)

    pay, docs, near, info, own_sums = pl.pallas_call(
        functools.partial(products_kernel, sizes),
        out_shape=(
            jax.ShapeDtypeStruct((mp, rows, round_up(rows + 4, LANES)), F32),
            jax.ShapeDtypeStruct((rows, width), F32),
            jax.ShapeDtypeStruct((rows, width), F32),
            jax.ShapeDtypeStruct((rows, LANES), F32),
            jax.ShapeDtypeStruct((rows, width), F32),
        ),
        compiler_params=limit,
        name="products",
    )(here, own, centroids, cluster_mass.reshape(1, cents))
    pay = lax.all_to_all(pay, "mp", split_axis=0, concat_axis=0, tiled=True)
    return pl.pallas_call(
        functools.partial(update_kernel, sizes),
        out_shape=(
            jax.ShapeDtypeStruct((slots, width), F32),
            jax.ShapeDtypeStruct((cents, width), F32),
        ),
        compiler_params=limit,
        name="update",
    )(pay, docs, near, info, own_sums, own, centroids)


def solution(mesh):
    placed = (
        P("dp", None),
        P("dp"),
        P(),
        P(None, "mp"),
        P(None, "mp"),
        P(None, "mp"),
        P("mp", None),
        P("dp", "mp"),
        P("dp"),
        P("dp"),
    )
    return jax.shard_map(
        shards,
        mesh=mesh,
        in_specs=placed,
        out_specs=(P("dp", "mp"), P("dp", "mp")),
        check_vma=False,
    )
```

```python
import functools
import math

import jax
import jax.numpy as jnp
from jax import lax
from jax.experimental import pallas as pl
from jax.experimental.pallas import tpu as pltpu
from jax.sharding import PartitionSpec as P

D = 1024
HEAD_DIM = 64
QB = 64
GROUP = 8
EXTENTS = (192, 256, 320, 384, 512, 640)
LANES = 128
BF = jnp.bfloat16
F32 = jnp.float32

NN = (((1,), (0,)), ((), ()))
NT = (((1,), (1,)), ((), ()))
TN = (((0,), (0,)), ((), ()))


def dot(a, b, dims=NN, precision=None):
    return lax.dot_general(a, b, dims, preferred_element_type=F32, precision=precision)


def iota(shape, dim):
    return lax.broadcasted_iota(jnp.int32, shape, dim)


def thirds(x):
    first = x.astype(BF)
    rest = x - first.astype(F32)
    second = rest.astype(BF)
    third = (rest - second.astype(F32)).astype(BF)
    return first, second, third


def pick_rows(one_hot, x, dims=NN):
    first, second, third = thirds(x)
    return dot(one_hot, first, dims) + (dot(one_hot, second, dims) + dot(one_hot, third, dims))


def round_up(n, by):
    return (n + by - 1) // by * by


def row_kernel(
    sizes, ids_hbm, assigned_hbm, gain_hbm, x_hbm, wq_hbm, wk_hbm, wv_hbm, wo_hbm, out_ref,
    ids_ref, ids_sm, assigned_sm, gain_ref, x_ref, w_ref, wo_ref, normed_ref, q_ref, k_ref, v_ref,
    slot_ref, query_slots_ref, windows_ref, windows_sm, pool_ref, meta_ref, share_ref, scores_ref, raised_ref, small_sems, x_sems, w_sems,
):
    length, tile, slots, capacity, block_rows, dp, mp, width, cents = sizes
    small = tile // 2
    sizes_of = [small] + [tile] * (length // tile - 1) + [small]
    begins_of = [sum(sizes_of[:i]) for i in range(len(sizes_of))]
    tiles = len(sizes_of)
    lane_blocks = length // LANES
    rows = dp * block_rows
    heads = width // HEAD_DIM
    halves = width // LANES
    row = lax.axis_index("dp")
    column = lax.axis_index("mp")

    small_copies = [
        pltpu.make_async_copy(ids_hbm, ids_ref, small_sems.at[0]),
        pltpu.make_async_copy(ids_hbm, ids_sm, small_sems.at[1]),
        pltpu.make_async_copy(assigned_hbm, assigned_sm, small_sems.at[2]),
        pltpu.make_async_copy(gain_hbm, gain_ref, small_sems.at[3]),
    ]
    x_copies = [
        pltpu.make_async_copy(x_hbm.at[pl.ds(at, size), :], x_ref.at[pl.ds(at, size), :], x_sems.at[i])
        for i, (at, size) in enumerate(zip(begins_of, sizes_of))
    ]
    w_copies = [
        pltpu.make_async_copy(w_hbm, w_ref.at[i], w_sems.at[i])
        for i, w_hbm in enumerate((wq_hbm, wk_hbm, wv_hbm))
    ] + [pltpu.make_async_copy(wo_hbm, wo_ref, w_sems.at[3])]
    for copy in small_copies + x_copies[:1]:
        copy.start()
    for copy in w_copies[:3]:
        copy.start(priority=1)
    for copy in x_copies[1:]:
        copy.start()
    w_copies[3].start(priority=1)
    for copy in small_copies:
        copy.wait()

    ids = ids_ref[...]
    local = ids - row * slots
    slot_ids = jnp.where(local < 0, slots, local)
    slot_rows = slot_ids.astype(F32)
    turned = pltpu.roll(slot_rows, QB, 1)
    front = iota(slot_rows.shape, 1) < QB
    query_slots_ref[0] = jnp.where(front, slot_rows, turned)
    query_slots_ref[1] = jnp.where(front, turned, slot_rows)

    lane = iota((1, LANES), 1)
    named = jnp.full((1, LANES), -1, jnp.int32)
    for j in range(slots):
        named = jnp.where(lane == j, assigned_sm[0, j], named)
    owner = named // cents
    wide = jnp.broadcast_to(owner.astype(F32), (LANES, LANES))
    earlier = (wide.T == wide) & (iota((LANES, LANES), 0) < iota((LANES, LANES), 1))
    rank = jnp.sum(earlier.astype(F32), axis=0, keepdims=True)
    goes_to = jnp.where(lane < slots, owner.astype(F32) * block_rows + rank, -1.0)
    goes = jnp.take_along_axis(jnp.broadcast_to(goes_to, slot_rows.shape), slot_ids, axis=1)
    row_of = iota((rows, LANES), 0)
    continued = (row_of % block_rows == capacity).astype(F32)
    row_of = row_of.astype(F32)
    lane_number = iota((8, LANES), 1).astype(F32)
    counts = jnp.zeros((8, LANES), F32)
    for block in range(lane_blocks):
        here = slice(block * LANES, (block + 1) * LANES)
        slot = slot_rows[block:block + 1, :]
        upright = jnp.broadcast_to(slot, (LANES, LANES)).T
        slot_ref[here, :] = upright
        for part in range(0, LANES, 8):
            counts += (upright[part:part + 8] == lane_number).astype(F32)
        mine = jnp.where(row_of == goes[block:block + 1, :], 1.0, 0.0)
        pool_ref[:, here] = jnp.where(slot == slots, continued, mine).astype(BF)
    counts = jnp.broadcast_to(jnp.sum(counts, axis=0, keepdims=True), (8, LANES))

    def order(shape, dim):
        slot = iota(shape, dim)
        return jnp.where(slot == slots, 0, slot + 1)

    before = (order((LANES, LANES), 0) < order((LANES, LANES), 1)) & (iota((LANES, LANES), 0) <= slots)
    before = before.astype(F32).astype(BF)
    upper = counts.astype(BF)
    starts = dot(upper, before) + dot((counts - upper.astype(F32)).astype(BF), before)

    def at_position(values, position):
        mine = iota(slot_rows.shape, 1).astype(F32) == slot_rows[:, position:position + 1]
        return jnp.sum(jnp.where(mine, values[:1], 0.0), axis=1, keepdims=True)

    spot = iota(slot_rows.shape, 1)
    table = jnp.zeros(slot_rows.shape, F32)
    for part in range(LANES // QB):
        table = jnp.where(spot == 2 * part, at_position(starts, part * QB), table)
        table = jnp.where(spot == 2 * part + 1, at_position(starts + counts, (part + 1) * QB - 1), table)
    windows_ref[...] = table.astype(jnp.int32)
    windows_copy = pltpu.make_async_copy(windows_ref, windows_sm, small_sems.at[4])
    windows_copy.start()

    last_slot = ids_sm[lane_blocks - 1, LANES - 1] - row * slots
    speaks = (column == 0).astype(F32)
    meta_ref[0:1, :LANES] = goes_to * speaks
    meta_ref[0:1, LANES:] = counts[:1] * speaks
    meta_ref[1:2, :LANES] = named.astype(F32) * speaks
    meta_ref[1:2, LANES:] = (lane == last_slot).astype(F32) * speaks
    share_ref[...] = jnp.zeros_like(share_ref)

    own = pl.ds(pl.multiple_of(column * width, width), width)
    gain = gain_ref[...]
    piece_rows = 64
    lane_slices = [slice(j * LANES, (j + 1) * LANES) for j in range(D // LANES)]

    def piece_of(i, p, lanes):
        at = begins_of[i] + p * piece_rows
        return x_ref[at:at + piece_rows, lanes].astype(F32)

    def normalise(i, group):
        means, inverses = [], []
        for p in group:
            total = functools.reduce(jnp.add, [piece_of(i, p, lanes) for lanes in lane_slices])
            mean = jnp.sum(total, axis=1, keepdims=True) * (1.0 / D)
            means.append(jnp.broadcast_to(mean, (piece_rows, LANES)))
        for p, mean in zip(group, means):
            squares = jnp.zeros((piece_rows, LANES), F32)
            for lanes in lane_slices:
                centered = piece_of(i, p, lanes) - mean
                squares += centered * centered
            variance = jnp.sum(squares, axis=1, keepdims=True) * (1.0 / D)
            inverses.append(jnp.broadcast_to(lax.rsqrt(variance + 1e-05), (piece_rows, LANES)))
        for p, mean, inverse in zip(group, means, inverses):
            here = slice(p * piece_rows, (p + 1) * piece_rows)
            for lanes in lane_slices:
                scaled = (piece_of(i, p, lanes) - mean) * inverse * gain[:, lanes]
                normed_ref[i % 2, here, lanes] = scaled.astype(BF)

    def project(i, which):
        here = slice(begins_of[i], begins_of[i] + sizes_of[i])
        result = dot(normed_ref[i % 2, :sizes_of[i], :], w_ref[which])
        if which == 0:
            result = result * (1.0 / math.sqrt(HEAD_DIM))
        (q_ref, k_ref, v_ref)[which][here, :] = result.astype(BF)

    def groups(i):
        pieces = sizes_of[i] // piece_rows
        return [range(pieces * g // 3, pieces * (g + 1) // 3) for g in range(3)]

    tokens_sum = jnp.zeros((rows, width), F32)
    x_copies[0].wait()
    normalise(0, range(sizes_of[0] // piece_rows))
    for copy in w_copies[:3]:
        copy.wait()
    for i in range(tiles):
        if i + 1 < tiles:
            x_copies[i + 1].wait()
        for which in range(3):
            if i + 1 < tiles:
                normalise(i + 1, groups(i + 1)[which])
            project(i, which)
        here = slice(begins_of[i], begins_of[i] + sizes_of[i])
        tokens_sum += dot(pool_ref[:, here], x_ref[here, own])
    windows_copy.wait()

    def window(block_pair, part):
        return (windows_sm[block_pair, 2 * part] // 16) * 16, windows_sm[block_pair, 2 * part + 1]

    def all_heads(block):
        at = pl.multiple_of(block * QB, QB)
        zero = jnp.zeros((QB, LANES), BF)
        left = iota((QB, LANES), 1) < HEAD_DIM
        stacked = []
        for half in range(halves):
            piece = q_ref[pl.ds(at, QB), half * LANES:(half + 1) * LANES]
            for kept in (left, jnp.logical_not(left)):
                mine = jnp.where(kept, piece, zero)
                stacked.append(jnp.concatenate([mine if h == half else zero for h in range(halves)], axis=1))
        return jnp.concatenate(stacked, axis=0)

    head_of_lane = (iota((8, width), 1) // HEAD_DIM) == (iota((8, width), 0) % heads)
    upper_rows = iota((8, width), 0) < heads

    def key_shares(raised, inverse):
        upper = inverse.astype(BF).astype(F32)
        parts = jnp.where(upper_rows, upper, inverse - upper)
        return dot(jnp.where(head_of_lane, parts, 0.0).astype(BF), raised, NT)

    def straight(blocks, begins, extent):
        padded = round_up(extent, LANES)
        step = 64
        ats = [pl.multiple_of(jnp.minimum(begin, length - extent), 16) for begin in begins]
        halves_of = [slice(half * LANES, (half + 1) * LANES) for half in range(halves)]
        tops, inverses = {}, {}

        def score(i):
            scores_ref[i, :extent, :] = dot(k_ref[pl.ds(ats[i], extent), :], all_heads(blocks[i]), NT)

        def mask(i):
            mine = query_slots_ref[i % 2, pl.ds(blocks[i] // 2, 1), :]
            top = [jnp.full((8, LANES), -1e30, F32) for _ in range(halves)]
            for key in range(0, extent, step):
                same = slot_ref[pl.ds(ats[i] + key, step), :] == mine
                for half, lanes in enumerate(halves_of):
                    masked = jnp.where(same, scores_ref[i, key:key + step, lanes], -1e30)
                    scores_ref[i, key:key + step, lanes] = masked
                    highest = jnp.max(masked.reshape(step // 8, 8, LANES), axis=0)
                    top[half] = jnp.maximum(top[half], highest)
            tops[i] = [jnp.max(t, axis=0, keepdims=True) for t in top]

        def raise_all(i):
            total = [jnp.zeros((8, LANES), F32) for _ in range(halves)]
            for key in range(0, extent, step):
                for half, lanes in enumerate(halves_of):
                    raised = jnp.exp(scores_ref[i, key:key + step, lanes] - tops[i][half])
                    total[half] += jnp.sum(raised.reshape(step // 8, 8, LANES), axis=0)
                    raised_ref[i, key:key + step, lanes] = raised.astype(BF)
            if padded > extent:
                raised_ref[i, extent:padded, :] = jnp.zeros((padded - extent, width), BF)
            inverses[i] = jnp.concatenate(
                [1.0 / jnp.sum(t, axis=0, keepdims=True) for t in total], axis=1
            )

        def share(i):
            shares = key_shares(raised_ref[i, :padded, :], inverses[i])
            shares = jnp.concatenate([shares, jnp.zeros((8, LANES), F32)], axis=1)
            base = pl.multiple_of((ats[i] // LANES) * LANES, LANES)
            share_ref[:, pl.ds(base, padded + LANES)] += pltpu.roll(shares, ats[i] % LANES, 1)

        stages = (score, mask, raise_all, share)
        behind = (0, 2, 3, 5)
        for turn in range(len(blocks) + behind[-1]):
            for stage, late in zip(stages, behind):
                if 0 <= turn - late < len(blocks):
                    stage(turn - late)

    def any_length(block):
        chunk = 256
        begin, end = window(block // 2, block % 2)
        first_chunk = begin // chunk
        end_chunk = (end + chunk - 1) // chunk

        def scores_at(index):
            at = pl.multiple_of(index * chunk, chunk)
            scores = dot(k_ref[pl.ds(at, chunk), :], all_heads(block), NT)
            even = query_slots_ref[0, pl.ds(block // 2, 1), :]
            odd = query_slots_ref[1, pl.ds(block // 2, 1), :]
            query_slots = jnp.where(block % 2 == 0, even, odd)
            same = slot_ref[pl.ds(at, chunk), :] == query_slots
            masked = [
                jnp.where(same, scores[:, half * LANES:(half + 1) * LANES], -1e30) for half in range(halves)
            ]
            return at, jnp.concatenate(masked, axis=1)

        def forward(index, carry):
            top, total = carry
            _, scores = scores_at(index)
            higher = jnp.maximum(top, jnp.max(scores, axis=0, keepdims=True))
            raised = jnp.sum(jnp.exp(scores - higher), axis=0, keepdims=True)
            return higher, total * jnp.exp(top - higher) + raised

        top, total = lax.fori_loop(
            first_chunk, end_chunk, forward,
            (jnp.full((1, width), -1e30, F32), jnp.zeros((1, width), F32)),
        )
        inverse = 1.0 / total

        def again(index, nothing):
            at, scores = scores_at(index)
            share_ref[:, pl.ds(at, chunk)] += key_shares(jnp.exp(scores - top).astype(BF), inverse)
            return nothing

        lax.fori_loop(first_chunk, end_chunk, again, 0)

    def group_step(group, nothing):
        blocks = [group * GROUP + i for i in range(GROUP)]
        spans = [window(group * (GROUP // 2) + i // 2, i % 2) for i in range(GROUP)]
        begins = [begin for begin, _ in spans]
        widest = functools.reduce(jnp.maximum, [end - begin for begin, end in spans])
        done = jnp.int32(0)
        for extent in EXTENTS:
            if extent > length:
                break

            @pl.when((widest > done) & (widest <= extent))
            def run(extent=extent):
                straight(blocks, begins, extent)

            done = jnp.int32(extent)

        @pl.when(widest > done)
        def slow():
            def one(index, nothing):
                any_length(group * GROUP + index)
                return nothing

            lax.fori_loop(0, GROUP, one, 0)

        return nothing

    lax.fori_loop(0, length // QB // GROUP, group_step, 0)

    shares = share_ref[:, :length]
    pool = pool_ref[...]
    weighted = jnp.concatenate(
        [pool * (shares[h:h + 1] + shares[heads + h:heads + h + 1]).astype(BF) for h in range(heads)], axis=0
    )
    every = dot(weighted, v_ref[...])
    lane_head = iota((rows, width), 1) // HEAD_DIM
    context = jnp.zeros((rows, width), F32)
    for h in range(heads):
        context = jnp.where(lane_head == h, every[h * rows:(h + 1) * rows], context)
    upper = context.astype(BF)
    lower = (context - upper.astype(F32)).astype(BF)
    w_copies[3].wait()
    sent = dot(jnp.concatenate([upper, lower], axis=0), wo_ref[...])
    sent = sent[:rows] + sent[rows:]
    for target in range(mp):
        out_ref[target] = sent[:, target * width:(target + 1) * width]
    out_ref[column] += tokens_sum
    for target in range(mp):
        for block in range(dp):
            at = block * block_rows + capacity + 1
            out_ref[target, at:at + 2, :] = meta_ref[:2, :]


def row_sums(doc_ids, assigned, tokens, ln_gain, w_query, w_key, w_value, w_out, sizes):
    length, tile, slots, capacity, block_rows, dp, mp, width, cents = sizes
    rows = dp * block_rows
    return pl.pallas_call(
        functools.partial(row_kernel, sizes),
        in_specs=[pl.BlockSpec(memory_space=pltpu.HBM)] * 8,
        out_shape=jax.ShapeDtypeStruct((mp, rows, width), F32),
        scratch_shapes=[
            pltpu.VMEM((length // LANES, LANES), jnp.int32),
            pltpu.SMEM((length // LANES, LANES), jnp.int32),
            pltpu.SMEM((1, slots), jnp.int32),
            pltpu.VMEM((1, D), F32),
            pltpu.VMEM((length, D), BF),
            pltpu.VMEM((3, D, width), BF),
            pltpu.VMEM((width, D), BF),
            pltpu.VMEM((2, tile, D), BF),
            pltpu.VMEM((length, width), BF),
            pltpu.VMEM((length, width), BF),
            pltpu.VMEM((length, width), BF),
            pltpu.VMEM((length, LANES), F32),
            pltpu.VMEM((2, length // LANES, LANES), F32),
            pltpu.VMEM((length // LANES, LANES), jnp.int32),
            pltpu.SMEM((length // LANES, LANES), jnp.int32),
            pltpu.VMEM((rows, length), BF),
            pltpu.VMEM((8, 2 * LANES), F32),
            pltpu.VMEM((8, length + 2 * LANES), F32),
            pltpu.VMEM((GROUP, EXTENTS[-1], width), F32),
            pltpu.VMEM((GROUP, EXTENTS[-1], width), BF),
            pltpu.SemaphoreType.DMA((5,)),
            pltpu.SemaphoreType.DMA((length // tile + 1,)),
            pltpu.SemaphoreType.DMA((4,)),
        ],
        compiler_params=pltpu.CompilerParams(vmem_limit_bytes=62 * 1024 * 1024),
        name="row_sums",
    )(
        doc_ids.reshape(length // LANES, LANES), assigned.reshape(1, slots), ln_gain.reshape(1, D),
        tokens, w_query, w_key, w_value, w_out,
    )


def products_kernel(
    sizes, here_ref, own_ref, cent_ref, mass_ref, pay_ref, docs_ref, near_ref, info_ref, own_out_ref
):
    length, tile, slots, capacity, block_rows, dp, mp, width, cents = sizes
    me = lax.axis_index("dp")
    rows = dp * block_rows
    lane = iota((1, LANES), 1)

    def rows_of(meta, first_row, count):
        goes_to, counts = meta[0:1, :LANES], meta[0:1, LANES:]
        named, is_last = meta[1:2, :LANES], meta[1:2, LANES:]
        held = (goes_to == (iota((count, LANES), 0) + first_row).astype(F32)).astype(F32)

        def column(values):
            return jnp.sum(held * values, axis=1, keepdims=True)

        return column(named), column(counts), column(is_last), column(jnp.ones((1, LANES), F32))

    def carry_of(source):
        block = here_ref[pl.ds(pl.multiple_of(source * block_rows, 8), block_rows), :]
        counts = block[capacity + 1:capacity + 2, LANES:]
        count = jnp.sum(jnp.where(lane == slots, counts, 0.0), axis=1, keepdims=True)
        return block[capacity:capacity + 1, :], count

    columns = []
    for source in range(dp):
        base = source * block_rows
        block = here_ref[base:base + block_rows, :]
        meta = block[capacity + 1:capacity + 3, :]
        named, counts, is_last, held = rows_of(meta, me * block_rows, block_rows)
        sums = jnp.where(held > 0, block, 0.0)
        if source < dp - 1:
            carry, carry_count = carry_of(source + 1)
            sums = sums + is_last * carry
            counts = counts + is_last * carry_count
        docs_ref[base:base + block_rows, :] = sums
        columns.append((named - (me * cents).astype(F32), counts, held))
    local = jnp.concatenate([c[0] for c in columns], axis=0)
    counts = jnp.concatenate([c[1] for c in columns], axis=0)
    held = jnp.concatenate([c[2] for c in columns], axis=0)
    valid = ((held > 0) & (counts > 0)).astype(F32)

    docs = docs_ref[...]
    names = (iota((rows, cents), 1).astype(F32) == local) & (valid > 0)
    names = names.astype(F32)
    mass = jnp.sum(names * mass_ref[...], axis=1, keepdims=True)
    near = pick_rows(names.astype(BF), cent_ref[...])
    near_ref[...] = near

    own = own_ref[...]
    _, own_counts, own_last, _ = rows_of(own_ref[capacity + 1:capacity + 3, :], 0, rows)
    following = jnp.minimum(me + 1, dp - 1)
    more = (me < dp - 1).astype(F32)
    carry, carry_count = carry_of(following)
    own = own + own_last * (carry * more)
    own_counts = own_counts + own_last * (carry_count * more)
    own_out_ref[...] = own

    gram = dot(docs, docs, NT, precision=lax.Precision.HIGHEST)
    spot = iota((rows, LANES), 1)
    cross = jnp.sum(near * docs, axis=1, keepdims=True)
    square = jnp.sum(near * near, axis=1, keepdims=True)
    own_square = jnp.sum(own * own, axis=1, keepdims=True)
    doc_square = jnp.sum(docs * docs, axis=1, keepdims=True)
    pay_ref[0] = jnp.zeros(pay_ref.shape[1:], F32)
    pay_ref[0, :, :rows] = gram
    for i, sums in enumerate((cross, square, own_square, doc_square)):
        pay_ref[0, :, rows + i:rows + i + 1] = sums
    for target in range(1, mp):
        pay_ref[target] = pay_ref[0]
    info_ref[...] = jnp.where(
        spot == 0, local, jnp.where(spot == 1, counts, jnp.where(spot == 2, valid, jnp.where(spot == 3, mass, own_counts)))
    )


def update_kernel(
    sizes, pay_ref, docs_ref, near_ref, info_ref, own_ref, meta_ref, cent_ref, vec_ref, new_ref
):
    length, tile, slots, capacity, block_rows, dp, mp, width, cents = sizes
    rows = dp * block_rows
    info = info_ref[...]
    local, counts, valid, mass, own_counts = (info[:, i:i + 1] for i in range(5))
    pay = functools.reduce(jnp.add, [pay_ref[i] for i in range(mp)])
    cross, square, own_square, doc_square = (pay[:, rows + i:rows + i + 1] for i in range(4))

    def scale(sums, count):
        inverse = 1.0 / jnp.maximum(count, 1.0)
        return inverse * lax.rsqrt(sums * inverse * inverse * (1.0 / D) + 1e-06)

    vectors = own_ref[...] * scale(own_square, own_counts)
    goes_to = meta_ref[capacity + 1:capacity + 2, :LANES]
    place = ((iota((rows, LANES), 0).astype(F32) == goes_to).astype(F32)).T
    vec_ref[...] = pick_rows(place[:slots].astype(BF), vectors)

    share = scale(doc_square, counts) * valid
    across = jnp.where(valid > 0, local, -1.0)
    flat = jnp.broadcast_to(across, (rows, LANES)).T[:1]
    share_flat = jnp.broadcast_to(share, (rows, LANES)).T[:1]
    cross_flat = jnp.broadcast_to(cross, (rows, LANES)).T[:1]
    same = (across == flat) & (valid > 0)
    mixed = jnp.where(same, share_flat, 0.0)
    gained = dot(mixed, docs_ref[...], precision=lax.Precision.HIGHEST)
    twice = dot(mixed, pay[:, :rows], precision=lax.Precision.HIGHEST)
    norm = (
        mass * mass * square
        + 2.0 * mass * jnp.sum(mixed * cross_flat, axis=1, keepdims=True)
        + jnp.sum(twice * mixed, axis=1, keepdims=True)
    )
    blended = mass * near_ref[...] + gained
    scaled = blended * lax.rsqrt(norm * (1.0 / D) + 1e-06)
    before = same & (iota((rows, rows), 0) < iota((rows, rows), 1))
    repeated = jnp.sum(before.astype(F32), axis=0, keepdims=True)
    target = jnp.where((flat >= 0) & (repeated < 0.5), flat, -1.0)
    hits = (iota((cents, rows), 0).astype(F32) == target).astype(F32)
    updated = pick_rows(hits.astype(BF), scaled)
    hit = jnp.sum(hits, axis=1, keepdims=True)
    new_ref[...] = jnp.where(hit > 0, updated, cent_ref[...])


def shards(
    tokens, doc_ids, ln_gain, w_query, w_key, w_value, w_out, centroids, cluster_mass, assigned
):
    length = tokens.shape[0]
    slots = assigned.shape[0]
    width = w_out.shape[0]
    cents = centroids.shape[0]
    dp = lax.axis_size("dp")
    mp = lax.axis_size("mp")
    capacity = max(2, (slots + dp - 2) // (dp - 1))
    block_rows = round_up(capacity + 3, 8)
    rows = dp * block_rows
    sizes = (length, min(512, length), slots, capacity, block_rows, dp, mp, width, cents)
    limit = pltpu.CompilerParams(vmem_limit_bytes=48 * 1024 * 1024)

    partial = row_sums(doc_ids, assigned, tokens, ln_gain, w_query, w_key, w_value, w_out, sizes)
    shared = lax.all_to_all(partial, "mp", split_axis=0, concat_axis=0, tiled=True)
    own = jnp.sum(shared, axis=0)
    here = lax.all_to_all(own, "dp", split_axis=0, concat_axis=0, tiled=True)

    pay, docs, near, info, own_sums = pl.pallas_call(
        functools.partial(products_kernel, sizes),
        out_shape=(
            jax.ShapeDtypeStruct((mp, rows, round_up(rows + 4, LANES)), F32),
            jax.ShapeDtypeStruct((rows, width), F32),
            jax.ShapeDtypeStruct((rows, width), F32),
            jax.ShapeDtypeStruct((rows, LANES), F32),
            jax.ShapeDtypeStruct((rows, width), F32),
        ),
        compiler_params=limit,
        name="products",
    )(here, own, centroids, cluster_mass.reshape(1, cents))
    pay = lax.all_to_all(pay, "mp", split_axis=0, concat_axis=0, tiled=True)
    return pl.pallas_call(
        functools.partial(update_kernel, sizes),
        out_shape=(
            jax.ShapeDtypeStruct((slots, width), F32),
            jax.ShapeDtypeStruct((cents, width), F32),
        ),
        compiler_params=limit,
        name="update",
    )(pay, docs, near, info, own_sums, own, centroids)


def solution(mesh):
    placed = (
        P("dp", None),
        P("dp"),
        P(),
        P(None, "mp"),
        P(None, "mp"),
        P(None, "mp"),
        P("mp", None),
        P("dp", "mp"),
        P("dp"),
        P("dp"),
    )
    return jax.shard_map(
        shards,
        mesh=mesh,
        in_specs=placed,
        out_specs=(P("dp", "mp"), P("dp", "mp")),
        check_vma=False,
    )
```

```python
import functools
import math

import jax
import jax.numpy as jnp
from jax import lax
from jax.experimental import pallas as pl
from jax.experimental.pallas import tpu as pltpu
from jax.sharding import PartitionSpec as P

D = 1024
HEAD_DIM = 64
QB = 64
GROUP = 8
EXTENTS = (192, 256, 320, 384, 512, 640)
LANES = 128
BF = jnp.bfloat16
F32 = jnp.float32

NN = (((1,), (0,)), ((), ()))
NT = (((1,), (1,)), ((), ()))
TN = (((0,), (0,)), ((), ()))


def dot(a, b, dims=NN, precision=None):
    return lax.dot_general(a, b, dims, preferred_element_type=F32, precision=precision)


def iota(shape, dim):
    return lax.broadcasted_iota(jnp.int32, shape, dim)


def thirds(x):
    first = x.astype(BF)
    rest = x - first.astype(F32)
    second = rest.astype(BF)
    third = (rest - second.astype(F32)).astype(BF)
    return first, second, third


def pick_rows(one_hot, x, dims=NN):
    first, second, third = thirds(x)
    return dot(one_hot, first, dims) + (dot(one_hot, second, dims) + dot(one_hot, third, dims))


def round_up(n, by):
    return (n + by - 1) // by * by


def row_kernel(
    sizes, ids_hbm, assigned_hbm, gain_hbm, x_hbm, wq_hbm, wk_hbm, wv_hbm, wo_hbm, out_ref,
    ids_ref, ids_sm, assigned_sm, gain_ref, x_ref, w_ref, wo_ref, normed_ref, q_ref, k_ref, v_ref,
    slot_ref, query_slots_ref, windows_ref, windows_sm, pool_ref, meta_ref, share_ref, scores_ref, raised_ref, small_sems, x_sems, w_sems,
):
    length, tile, slots, capacity, block_rows, dp, mp, width, cents = sizes
    tiles = length // tile
    lane_blocks = length // LANES
    rows = dp * block_rows
    heads = width // HEAD_DIM
    halves = width // LANES
    row = lax.axis_index("dp")
    column = lax.axis_index("mp")

    small_copies = [
        pltpu.make_async_copy(ids_hbm, ids_ref, small_sems.at[0]),
        pltpu.make_async_copy(ids_hbm, ids_sm, small_sems.at[1]),
        pltpu.make_async_copy(assigned_hbm, assigned_sm, small_sems.at[2]),
        pltpu.make_async_copy(gain_hbm, gain_ref, small_sems.at[3]),
    ]
    part_rows = tile // 4
    x_copies = [
        pltpu.make_async_copy(x_hbm.at[pl.ds(at, part_rows), :], x_ref.at[pl.ds(at, part_rows), :], x_sems.at[i])
        for i, at in enumerate(range(0, length, part_rows))
    ]
    w_copies = [
        pltpu.make_async_copy(w_hbm, w_ref.at[i], w_sems.at[i])
        for i, w_hbm in enumerate((wq_hbm, wk_hbm, wv_hbm))
    ] + [pltpu.make_async_copy(wo_hbm, wo_ref, w_sems.at[3])]
    for copy in small_copies + x_copies[:4]:
        copy.start()
    for copy in w_copies[:3]:
        copy.start(priority=1)
    for copy in x_copies[4:]:
        copy.start()
    w_copies[3].start(priority=1)
    for copy in small_copies:
        copy.wait()

    ids = ids_ref[...]
    local = ids - row * slots
    slot_ids = jnp.where(local < 0, slots, local)
    slot_rows = slot_ids.astype(F32)
    turned = pltpu.roll(slot_rows, QB, 1)
    front = iota(slot_rows.shape, 1) < QB
    query_slots_ref[0] = jnp.where(front, slot_rows, turned)
    query_slots_ref[1] = jnp.where(front, turned, slot_rows)

    lane = iota((1, LANES), 1)
    named = jnp.full((1, LANES), -1, jnp.int32)
    for j in range(slots):
        named = jnp.where(lane == j, assigned_sm[0, j], named)
    owner = named // cents
    wide = jnp.broadcast_to(owner.astype(F32), (LANES, LANES))
    earlier = (wide.T == wide) & (iota((LANES, LANES), 0) < iota((LANES, LANES), 1))
    rank = jnp.sum(earlier.astype(F32), axis=0, keepdims=True)
    goes_to = jnp.where(lane < slots, owner.astype(F32) * block_rows + rank, -1.0)
    goes = jnp.take_along_axis(jnp.broadcast_to(goes_to, slot_rows.shape), slot_ids, axis=1)
    row_of = iota((rows, LANES), 0)
    continued = (row_of % block_rows == capacity).astype(F32)
    row_of = row_of.astype(F32)
    lane_number = iota((8, LANES), 1).astype(F32)
    counts = jnp.zeros((8, LANES), F32)
    for block in range(lane_blocks):
        here = slice(block * LANES, (block + 1) * LANES)
        slot = slot_rows[block:block + 1, :]
        upright = jnp.broadcast_to(slot, (LANES, LANES)).T
        slot_ref[here, :] = upright
        for part in range(0, LANES, 8):
            counts += (upright[part:part + 8] == lane_number).astype(F32)
        mine = jnp.where(row_of == goes[block:block + 1, :], 1.0, 0.0)
        pool_ref[:, here] = jnp.where(slot == slots, continued, mine).astype(BF)
    counts = jnp.broadcast_to(jnp.sum(counts, axis=0, keepdims=True), (8, LANES))

    def order(shape, dim):
        slot = iota(shape, dim)
        return jnp.where(slot == slots, 0, slot + 1)

    before = (order((LANES, LANES), 0) < order((LANES, LANES), 1)) & (iota((LANES, LANES), 0) <= slots)
    before = before.astype(F32).astype(BF)
    upper = counts.astype(BF)
    starts = dot(upper, before) + dot((counts - upper.astype(F32)).astype(BF), before)

    def at_position(values, position):
        mine = iota(slot_rows.shape, 1).astype(F32) == slot_rows[:, position:position + 1]
        return jnp.sum(jnp.where(mine, values[:1], 0.0), axis=1, keepdims=True)

    spot = iota(slot_rows.shape, 1)
    table = jnp.zeros(slot_rows.shape, F32)
    for part in range(LANES // QB):
        table = jnp.where(spot == 2 * part, at_position(starts, part * QB), table)
        table = jnp.where(spot == 2 * part + 1, at_position(starts + counts, (part + 1) * QB - 1), table)
    windows_ref[...] = table.astype(jnp.int32)
    windows_copy = pltpu.make_async_copy(windows_ref, windows_sm, small_sems.at[4])
    windows_copy.start()

    last_slot = ids_sm[lane_blocks - 1, LANES - 1] - row * slots
    speaks = (column == 0).astype(F32)
    meta_ref[0:1, :LANES] = goes_to * speaks
    meta_ref[0:1, LANES:] = counts[:1] * speaks
    meta_ref[1:2, :LANES] = named.astype(F32) * speaks
    meta_ref[1:2, LANES:] = (lane == last_slot).astype(F32) * speaks
    share_ref[...] = jnp.zeros_like(share_ref)

    own = pl.ds(pl.multiple_of(column * width, width), width)
    gain = gain_ref[...]
    piece_rows = 64
    pieces = tile // piece_rows
    lane_slices = [slice(j * LANES, (j + 1) * LANES) for j in range(D // LANES)]

    def piece_of(i, p, lanes):
        at = i * tile + p * piece_rows
        return x_ref[at:at + piece_rows, lanes].astype(F32)

    def normalise(i, group):
        means, inverses = [], []
        for p in group:
            total = functools.reduce(jnp.add, [piece_of(i, p, lanes) for lanes in lane_slices])
            mean = jnp.sum(total, axis=1, keepdims=True) * (1.0 / D)
            means.append(jnp.broadcast_to(mean, (piece_rows, LANES)))
        for p, mean in zip(group, means):
            squares = jnp.zeros((piece_rows, LANES), F32)
            for lanes in lane_slices:
                centered = piece_of(i, p, lanes) - mean
                squares += centered * centered
            variance = jnp.sum(squares, axis=1, keepdims=True) * (1.0 / D)
            inverses.append(jnp.broadcast_to(lax.rsqrt(variance + 1e-05), (piece_rows, LANES)))
        for p, mean, inverse in zip(group, means, inverses):
            here = slice(p * piece_rows, (p + 1) * piece_rows)
            for lanes in lane_slices:
                scaled = (piece_of(i, p, lanes) - mean) * inverse * gain[:, lanes]
                normed_ref[i % 2, here, lanes] = scaled.astype(BF)

    def project(i, which):
        here = slice(i * tile, (i + 1) * tile)
        result = dot(normed_ref[i % 2], w_ref[which])
        if which == 0:
            result = result * (1.0 / math.sqrt(HEAD_DIM))
        (q_ref, k_ref, v_ref)[which][here, :] = result.astype(BF)

    groups = [range(pieces * g // 3, pieces * (g + 1) // 3) for g in range(3)]
    tokens_sum = jnp.zeros((rows, width), F32)
    for quarter in range(4):
        x_copies[quarter].wait()
        normalise(0, range(pieces * quarter // 4, pieces * (quarter + 1) // 4))
    for copy in w_copies[:3]:
        copy.wait()
    for i in range(tiles):
        if i + 1 < tiles:
            for quarter in range(4):
                x_copies[4 * (i + 1) + quarter].wait()
        for which, group in enumerate(groups):
            if i + 1 < tiles:
                normalise(i + 1, group)
            project(i, which)
        here = slice(i * tile, (i + 1) * tile)
        tokens_sum += dot(pool_ref[:, here], x_ref[here, own])
    windows_copy.wait()

    def window(block_pair, part):
        return (windows_sm[block_pair, 2 * part] // 16) * 16, windows_sm[block_pair, 2 * part + 1]

    def all_heads(block):
        at = pl.multiple_of(block * QB, QB)
        zero = jnp.zeros((QB, LANES), BF)
        left = iota((QB, LANES), 1) < HEAD_DIM
        stacked = []
        for half in range(halves):
            piece = q_ref[pl.ds(at, QB), half * LANES:(half + 1) * LANES]
            for kept in (left, jnp.logical_not(left)):
                mine = jnp.where(kept, piece, zero)
                stacked.append(jnp.concatenate([mine if h == half else zero for h in range(halves)], axis=1))
        return jnp.concatenate(stacked, axis=0)

    head_of_lane = (iota((8, width), 1) // HEAD_DIM) == (iota((8, width), 0) % heads)
    upper_rows = iota((8, width), 0) < heads

    def key_shares(raised, inverse):
        upper = inverse.astype(BF).astype(F32)
        parts = jnp.where(upper_rows, upper, inverse - upper)
        return dot(jnp.where(head_of_lane, parts, 0.0).astype(BF), raised, NT)

    def straight(blocks, begins, extent):
        padded = round_up(extent, LANES)
        step = 64
        ats = [pl.multiple_of(jnp.minimum(begin, length - extent), 16) for begin in begins]
        halves_of = [slice(half * LANES, (half + 1) * LANES) for half in range(halves)]
        for i, (block, at) in enumerate(zip(blocks, ats)):
            scores_ref[i, :extent, :] = dot(k_ref[pl.ds(at, extent), :], all_heads(block), NT)
        tops = []
        for i, (block, at) in enumerate(zip(blocks, ats)):
            mine = query_slots_ref[i % 2, pl.ds(block // 2, 1), :]
            top = [jnp.full((8, LANES), -1e30, F32) for _ in range(halves)]
            for key in range(0, extent, step):
                same = slot_ref[pl.ds(at + key, step), :] == mine
                for half, lanes in enumerate(halves_of):
                    masked = jnp.where(same, scores_ref[i, key:key + step, lanes], -1e30)
                    scores_ref[i, key:key + step, lanes] = masked
                    highest = jnp.max(masked.reshape(step // 8, 8, LANES), axis=0)
                    top[half] = jnp.maximum(top[half], highest)
            tops.append([jnp.max(t, axis=0, keepdims=True) for t in top])
        inverses = []
        for i in range(len(blocks)):
            total = [jnp.zeros((8, LANES), F32) for _ in range(halves)]
            for key in range(0, extent, step):
                for half, lanes in enumerate(halves_of):
                    raised = jnp.exp(scores_ref[i, key:key + step, lanes] - tops[i][half])
                    total[half] += jnp.sum(raised.reshape(step // 8, 8, LANES), axis=0)
                    raised_ref[i, key:key + step, lanes] = raised.astype(BF)
            if padded > extent:
                raised_ref[i, extent:padded, :] = jnp.zeros((padded - extent, width), BF)
            inverses.append(
                jnp.concatenate([1.0 / jnp.sum(t, axis=0, keepdims=True) for t in total], axis=1)
            )
        for i, at in enumerate(ats):
            shares = key_shares(raised_ref[i, :padded, :], inverses[i])
            shares = jnp.concatenate([shares, jnp.zeros((8, LANES), F32)], axis=1)
            base = pl.multiple_of((at // LANES) * LANES, LANES)
            share_ref[:, pl.ds(base, padded + LANES)] += pltpu.roll(shares, at % LANES, 1)

    def any_length(block):
        chunk = 256
        begin, end = window(block // 2, block % 2)
        first_chunk = begin // chunk
        end_chunk = (end + chunk - 1) // chunk

        def scores_at(index):
            at = pl.multiple_of(index * chunk, chunk)
            scores = dot(k_ref[pl.ds(at, chunk), :], all_heads(block), NT)
            even = query_slots_ref[0, pl.ds(block // 2, 1), :]
            odd = query_slots_ref[1, pl.ds(block // 2, 1), :]
            query_slots = jnp.where(block % 2 == 0, even, odd)
            same = slot_ref[pl.ds(at, chunk), :] == query_slots
            masked = [
                jnp.where(same, scores[:, half * LANES:(half + 1) * LANES], -1e30) for half in range(halves)
            ]
            return at, jnp.concatenate(masked, axis=1)

        def forward(index, carry):
            top, total = carry
            _, scores = scores_at(index)
            higher = jnp.maximum(top, jnp.max(scores, axis=0, keepdims=True))
            raised = jnp.sum(jnp.exp(scores - higher), axis=0, keepdims=True)
            return higher, total * jnp.exp(top - higher) + raised

        top, total = lax.fori_loop(
            first_chunk, end_chunk, forward,
            (jnp.full((1, width), -1e30, F32), jnp.zeros((1, width), F32)),
        )
        inverse = 1.0 / total

        def again(index, nothing):
            at, scores = scores_at(index)
            share_ref[:, pl.ds(at, chunk)] += key_shares(jnp.exp(scores - top).astype(BF), inverse)
            return nothing

        lax.fori_loop(first_chunk, end_chunk, again, 0)

    def group_step(group, nothing):
        blocks = [group * GROUP + i for i in range(GROUP)]
        spans = [window(group * (GROUP // 2) + i // 2, i % 2) for i in range(GROUP)]
        begins = [begin for begin, _ in spans]
        widest = functools.reduce(jnp.maximum, [end - begin for begin, end in spans])
        done = jnp.int32(0)
        for extent in EXTENTS:
            if extent > length:
                break

            @pl.when((widest > done) & (widest <= extent))
            def run(extent=extent):
                straight(blocks, begins, extent)

            done = jnp.int32(extent)

        @pl.when(widest > done)
        def slow():
            def one(index, nothing):
                any_length(group * GROUP + index)
                return nothing

            lax.fori_loop(0, GROUP, one, 0)

        return nothing

    lax.fori_loop(0, length // QB // GROUP, group_step, 0)

    shares = share_ref[:, :length]
    pool = pool_ref[...]
    weighted = jnp.concatenate(
        [pool * (shares[h:h + 1] + shares[heads + h:heads + h + 1]).astype(BF) for h in range(heads)], axis=0
    )
    every = dot(weighted, v_ref[...])
    lane_head = iota((rows, width), 1) // HEAD_DIM
    context = jnp.zeros((rows, width), F32)
    for h in range(heads):
        context = jnp.where(lane_head == h, every[h * rows:(h + 1) * rows], context)
    upper = context.astype(BF)
    lower = (context - upper.astype(F32)).astype(BF)
    w_copies[3].wait()
    sent = dot(jnp.concatenate([upper, lower], axis=0), wo_ref[...])
    sent = sent[:rows] + sent[rows:]
    for target in range(mp):
        out_ref[target] = sent[:, target * width:(target + 1) * width]
    out_ref[column] += tokens_sum
    for target in range(mp):
        for block in range(dp):
            at = block * block_rows + capacity + 1
            out_ref[target, at:at + 2, :] = meta_ref[:2, :]


def row_sums(doc_ids, assigned, tokens, ln_gain, w_query, w_key, w_value, w_out, sizes):
    length, tile, slots, capacity, block_rows, dp, mp, width, cents = sizes
    rows = dp * block_rows
    return pl.pallas_call(
        functools.partial(row_kernel, sizes),
        in_specs=[pl.BlockSpec(memory_space=pltpu.HBM)] * 8,
        out_shape=jax.ShapeDtypeStruct((mp, rows, width), F32),
        scratch_shapes=[
            pltpu.VMEM((length // LANES, LANES), jnp.int32),
            pltpu.SMEM((length // LANES, LANES), jnp.int32),
            pltpu.SMEM((1, slots), jnp.int32),
            pltpu.VMEM((1, D), F32),
            pltpu.VMEM((length, D), BF),
            pltpu.VMEM((3, D, width), BF),
            pltpu.VMEM((width, D), BF),
            pltpu.VMEM((2, tile, D), BF),
            pltpu.VMEM((length, width), BF),
            pltpu.VMEM((length, width), BF),
            pltpu.VMEM((length, width), BF),
            pltpu.VMEM((length, LANES), F32),
            pltpu.VMEM((2, length // LANES, LANES), F32),
            pltpu.VMEM((length // LANES, LANES), jnp.int32),
            pltpu.SMEM((length // LANES, LANES), jnp.int32),
            pltpu.VMEM((rows, length), BF),
            pltpu.VMEM((8, 2 * LANES), F32),
            pltpu.VMEM((8, length + 2 * LANES), F32),
            pltpu.VMEM((GROUP, EXTENTS[-1], width), F32),
            pltpu.VMEM((GROUP, EXTENTS[-1], width), BF),
            pltpu.SemaphoreType.DMA((5,)),
            pltpu.SemaphoreType.DMA((4 * length // tile,)),
            pltpu.SemaphoreType.DMA((4,)),
        ],
        compiler_params=pltpu.CompilerParams(vmem_limit_bytes=62 * 1024 * 1024),
        name="row_sums",
    )(
        doc_ids.reshape(length // LANES, LANES), assigned.reshape(1, slots), ln_gain.reshape(1, D),
        tokens, w_query, w_key, w_value, w_out,
    )


def products_kernel(
    sizes, here_ref, own_ref, cent_ref, mass_ref, pay_ref, docs_ref, near_ref, info_ref, own_out_ref
):
    length, tile, slots, capacity, block_rows, dp, mp, width, cents = sizes
    me = lax.axis_index("dp")
    rows = dp * block_rows
    lane = iota((1, LANES), 1)

    def rows_of(meta, first_row, count):
        goes_to, counts = meta[0:1, :LANES], meta[0:1, LANES:]
        named, is_last = meta[1:2, :LANES], meta[1:2, LANES:]
        held = (goes_to == (iota((count, LANES), 0) + first_row).astype(F32)).astype(F32)

        def column(values):
            return jnp.sum(held * values, axis=1, keepdims=True)

        return column(named), column(counts), column(is_last), column(jnp.ones((1, LANES), F32))

    def carry_of(source):
        block = here_ref[pl.ds(pl.multiple_of(source * block_rows, 8), block_rows), :]
        counts = block[capacity + 1:capacity + 2, LANES:]
        count = jnp.sum(jnp.where(lane == slots, counts, 0.0), axis=1, keepdims=True)
        return block[capacity:capacity + 1, :], count

    columns = []
    for source in range(dp):
        base = source * block_rows
        block = here_ref[base:base + block_rows, :]
        meta = block[capacity + 1:capacity + 3, :]
        named, counts, is_last, held = rows_of(meta, me * block_rows, block_rows)
        sums = jnp.where(held > 0, block, 0.0)
        if source < dp - 1:
            carry, carry_count = carry_of(source + 1)
            sums = sums + is_last * carry
            counts = counts + is_last * carry_count
        docs_ref[base:base + block_rows, :] = sums
        columns.append((named - (me * cents).astype(F32), counts, held))
    local = jnp.concatenate([c[0] for c in columns], axis=0)
    counts = jnp.concatenate([c[1] for c in columns], axis=0)
    held = jnp.concatenate([c[2] for c in columns], axis=0)
    valid = ((held > 0) & (counts > 0)).astype(F32)

    docs = docs_ref[...]
    names = (iota((rows, cents), 1).astype(F32) == local) & (valid > 0)
    names = names.astype(F32)
    mass = jnp.sum(names * mass_ref[...], axis=1, keepdims=True)
    near = pick_rows(names.astype(BF), cent_ref[...])
    near_ref[...] = near

    own = own_ref[...]
    _, own_counts, own_last, _ = rows_of(own_ref[capacity + 1:capacity + 3, :], 0, rows)
    following = jnp.minimum(me + 1, dp - 1)
    more = (me < dp - 1).astype(F32)
    carry, carry_count = carry_of(following)
    own = own + own_last * (carry * more)
    own_counts = own_counts + own_last * (carry_count * more)
    own_out_ref[...] = own

    gram = dot(docs, docs, NT, precision=lax.Precision.HIGHEST)
    spot = iota((rows, LANES), 1)
    cross = jnp.sum(near * docs, axis=1, keepdims=True)
    square = jnp.sum(near * near, axis=1, keepdims=True)
    own_square = jnp.sum(own * own, axis=1, keepdims=True)
    doc_square = jnp.sum(docs * docs, axis=1, keepdims=True)
    pay_ref[0] = jnp.zeros(pay_ref.shape[1:], F32)
    pay_ref[0, :, :rows] = gram
    for i, sums in enumerate((cross, square, own_square, doc_square)):
        pay_ref[0, :, rows + i:rows + i + 1] = sums
    for target in range(1, mp):
        pay_ref[target] = pay_ref[0]
    info_ref[...] = jnp.where(
        spot == 0, local, jnp.where(spot == 1, counts, jnp.where(spot == 2, valid, jnp.where(spot == 3, mass, own_counts)))
    )


def update_kernel(
    sizes, pay_ref, docs_ref, near_ref, info_ref, own_ref, meta_ref, cent_ref, vec_ref, new_ref
):
    length, tile, slots, capacity, block_rows, dp, mp, width, cents = sizes
    rows = dp * block_rows
    info = info_ref[...]
    local, counts, valid, mass, own_counts = (info[:, i:i + 1] for i in range(5))
    pay = functools.reduce(jnp.add, [pay_ref[i] for i in range(mp)])
    cross, square, own_square, doc_square = (pay[:, rows + i:rows + i + 1] for i in range(4))

    def scale(sums, count):
        inverse = 1.0 / jnp.maximum(count, 1.0)
        return inverse * lax.rsqrt(sums * inverse * inverse * (1.0 / D) + 1e-06)

    vectors = own_ref[...] * scale(own_square, own_counts)
    goes_to = meta_ref[capacity + 1:capacity + 2, :LANES]
    place = ((iota((rows, LANES), 0).astype(F32) == goes_to).astype(F32)).T
    vec_ref[...] = pick_rows(place[:slots].astype(BF), vectors)

    share = scale(doc_square, counts) * valid
    across = jnp.where(valid > 0, local, -1.0)
    flat = jnp.broadcast_to(across, (rows, LANES)).T[:1]
    share_flat = jnp.broadcast_to(share, (rows, LANES)).T[:1]
    cross_flat = jnp.broadcast_to(cross, (rows, LANES)).T[:1]
    same = (across == flat) & (valid > 0)
    mixed = jnp.where(same, share_flat, 0.0)
    gained = dot(mixed, docs_ref[...], precision=lax.Precision.HIGHEST)
    twice = dot(mixed, pay[:, :rows], precision=lax.Precision.HIGHEST)
    norm = (
        mass * mass * square
        + 2.0 * mass * jnp.sum(mixed * cross_flat, axis=1, keepdims=True)
        + jnp.sum(twice * mixed, axis=1, keepdims=True)
    )
    blended = mass * near_ref[...] + gained
    scaled = blended * lax.rsqrt(norm * (1.0 / D) + 1e-06)
    before = same & (iota((rows, rows), 0) < iota((rows, rows), 1))
    repeated = jnp.sum(before.astype(F32), axis=0, keepdims=True)
    target = jnp.where((flat >= 0) & (repeated < 0.5), flat, -1.0)
    hits = (iota((cents, rows), 0).astype(F32) == target).astype(F32)
    updated = pick_rows(hits.astype(BF), scaled)
    hit = jnp.sum(hits, axis=1, keepdims=True)
    new_ref[...] = jnp.where(hit > 0, updated, cent_ref[...])


def shards(
    tokens, doc_ids, ln_gain, w_query, w_key, w_value, w_out, centroids, cluster_mass, assigned
):
    length = tokens.shape[0]
    slots = assigned.shape[0]
    width = w_out.shape[0]
    cents = centroids.shape[0]
    dp = lax.axis_size("dp")
    mp = lax.axis_size("mp")
    capacity = max(2, (slots + dp - 2) // (dp - 1))
    block_rows = round_up(capacity + 3, 8)
    rows = dp * block_rows
    sizes = (length, min(1024, length), slots, capacity, block_rows, dp, mp, width, cents)
    limit = pltpu.CompilerParams(vmem_limit_bytes=48 * 1024 * 1024)

    partial = row_sums(doc_ids, assigned, tokens, ln_gain, w_query, w_key, w_value, w_out, sizes)
    shared = lax.all_to_all(partial, "mp", split_axis=0, concat_axis=0, tiled=True)
    own = jnp.sum(shared, axis=0)
    here = lax.all_to_all(own, "dp", split_axis=0, concat_axis=0, tiled=True)

    pay, docs, near, info, own_sums = pl.pallas_call(
        functools.partial(products_kernel, sizes),
        out_shape=(
            jax.ShapeDtypeStruct((mp, rows, round_up(rows + 4, LANES)), F32),
            jax.ShapeDtypeStruct((rows, width), F32),
            jax.ShapeDtypeStruct((rows, width), F32),
            jax.ShapeDtypeStruct((rows, LANES), F32),
            jax.ShapeDtypeStruct((rows, width), F32),
        ),
        compiler_params=limit,
        name="products",
    )(here, own, centroids, cluster_mass.reshape(1, cents))
    pay = lax.all_to_all(pay, "mp", split_axis=0, concat_axis=0, tiled=True)
    return pl.pallas_call(
        functools.partial(update_kernel, sizes),
        out_shape=(
            jax.ShapeDtypeStruct((slots, width), F32),
            jax.ShapeDtypeStruct((cents, width), F32),
        ),
        compiler_params=limit,
        name="update",
    )(pay, docs, near, info, own_sums, own, centroids)


def solution(mesh):
    placed = (
        P("dp", None),
        P("dp"),
        P(),
        P(None, "mp"),
        P(None, "mp"),
        P(None, "mp"),
        P("mp", None),
        P("dp", "mp"),
        P("dp"),
        P("dp"),
    )
    return jax.shard_map(
        shards,
        mesh=mesh,
        in_specs=placed,
        out_specs=(P("dp", "mp"), P("dp", "mp")),
        check_vma=False,
    )
```

```python
import functools
import math

import jax
import jax.numpy as jnp
from jax import lax
from jax.experimental import pallas as pl
from jax.experimental.pallas import tpu as pltpu
from jax.sharding import PartitionSpec as P

D = 1024
HEAD_DIM = 64
QB = 64
GROUP = 8
EXTENTS = (192, 256, 320, 384, 512, 640)
LANES = 128
BF = jnp.bfloat16
F32 = jnp.float32

NN = (((1,), (0,)), ((), ()))
NT = (((1,), (1,)), ((), ()))
TN = (((0,), (0,)), ((), ()))


def dot(a, b, dims=NN, precision=None):
    return lax.dot_general(a, b, dims, preferred_element_type=F32, precision=precision)


def iota(shape, dim):
    return lax.broadcasted_iota(jnp.int32, shape, dim)


def thirds(x):
    first = x.astype(BF)
    rest = x - first.astype(F32)
    second = rest.astype(BF)
    third = (rest - second.astype(F32)).astype(BF)
    return first, second, third


def pick_rows(one_hot, x, dims=NN):
    first, second, third = thirds(x)
    return dot(one_hot, first, dims) + (dot(one_hot, second, dims) + dot(one_hot, third, dims))


def round_up(n, by):
    return (n + by - 1) // by * by


def row_kernel(
    sizes, ids_hbm, assigned_hbm, gain_hbm, x_hbm, wq_hbm, wk_hbm, wv_hbm, wo_hbm, out_ref,
    ids_ref, ids_sm, assigned_sm, gain_ref, x_ref, w_ref, wo_ref, normed_ref, q_ref, k_ref, v_ref,
    slot_ref, query_slots_ref, windows_ref, windows_sm, pool_ref, meta_ref, share_ref, scores_ref, raised_ref, small_sems, x_sems, w_sems,
):
    length, tile, slots, capacity, block_rows, dp, mp, width, cents = sizes
    tiles = length // tile
    lane_blocks = length // LANES
    rows = dp * block_rows
    heads = width // HEAD_DIM
    halves = width // LANES
    row = lax.axis_index("dp")
    column = lax.axis_index("mp")

    small_copies = [
        pltpu.make_async_copy(ids_hbm, ids_ref, small_sems.at[0]),
        pltpu.make_async_copy(ids_hbm, ids_sm, small_sems.at[1]),
        pltpu.make_async_copy(assigned_hbm, assigned_sm, small_sems.at[2]),
        pltpu.make_async_copy(gain_hbm, gain_ref, small_sems.at[3]),
    ]
    part_rows = tile // 4
    x_copies = [
        pltpu.make_async_copy(x_hbm.at[pl.ds(at, part_rows), :], x_ref.at[pl.ds(at, part_rows), :], x_sems.at[i])
        for i, at in enumerate(range(0, length, part_rows))
    ]
    w_copies = [
        pltpu.make_async_copy(w_hbm, w_ref.at[i], w_sems.at[i])
        for i, w_hbm in enumerate((wq_hbm, wk_hbm, wv_hbm))
    ] + [pltpu.make_async_copy(wo_hbm, wo_ref, w_sems.at[3])]
    for copy in small_copies + x_copies[:4]:
        copy.start()
    for copy in w_copies[:3]:
        copy.start(priority=1)
    for copy in x_copies[4:]:
        copy.start()
    w_copies[3].start(priority=1)
    for copy in small_copies:
        copy.wait()

    ids = ids_ref[...]
    local = ids - row * slots
    slot_ids = jnp.where(local < 0, slots, local)
    slot_rows = slot_ids.astype(F32)
    turned = pltpu.roll(slot_rows, QB, 1)
    front = iota(slot_rows.shape, 1) < QB
    query_slots_ref[0] = jnp.where(front, slot_rows, turned)
    query_slots_ref[1] = jnp.where(front, turned, slot_rows)

    lane = iota((1, LANES), 1)
    named = jnp.full((1, LANES), -1, jnp.int32)
    for j in range(slots):
        named = jnp.where(lane == j, assigned_sm[0, j], named)
    owner = named // cents
    wide = jnp.broadcast_to(owner.astype(F32), (LANES, LANES))
    earlier = (wide.T == wide) & (iota((LANES, LANES), 0) < iota((LANES, LANES), 1))
    rank = jnp.sum(earlier.astype(F32), axis=0, keepdims=True)
    goes_to = jnp.where(lane < slots, owner.astype(F32) * block_rows + rank, -1.0)
    goes = jnp.take_along_axis(jnp.broadcast_to(goes_to, slot_rows.shape), slot_ids, axis=1)
    row_of = iota((rows, LANES), 0)
    continued = (row_of % block_rows == capacity).astype(F32)
    row_of = row_of.astype(F32)
    lane_number = iota((8, LANES), 1).astype(F32)
    counts = jnp.zeros((8, LANES), F32)
    for block in range(lane_blocks):
        here = slice(block * LANES, (block + 1) * LANES)
        slot = slot_rows[block:block + 1, :]
        upright = jnp.broadcast_to(slot, (LANES, LANES)).T
        slot_ref[here, :] = upright
        for part in range(0, LANES, 8):
            counts += (upright[part:part + 8] == lane_number).astype(F32)
        mine = jnp.where(row_of == goes[block:block + 1, :], 1.0, 0.0)
        pool_ref[:, here] = jnp.where(slot == slots, continued, mine).astype(BF)
    counts = jnp.broadcast_to(jnp.sum(counts, axis=0, keepdims=True), (8, LANES))

    def order(shape, dim):
        slot = iota(shape, dim)
        return jnp.where(slot == slots, 0, slot + 1)

    before = (order((LANES, LANES), 0) < order((LANES, LANES), 1)) & (iota((LANES, LANES), 0) <= slots)
    before = before.astype(F32).astype(BF)
    upper = counts.astype(BF)
    starts = dot(upper, before) + dot((counts - upper.astype(F32)).astype(BF), before)

    def at_position(values, position):
        mine = iota(slot_rows.shape, 1).astype(F32) == slot_rows[:, position:position + 1]
        return jnp.sum(jnp.where(mine, values[:1], 0.0), axis=1, keepdims=True)

    spot = iota(slot_rows.shape, 1)
    table = jnp.zeros(slot_rows.shape, F32)
    for part in range(LANES // QB):
        table = jnp.where(spot == 2 * part, at_position(starts, part * QB), table)
        table = jnp.where(spot == 2 * part + 1, at_position(starts + counts, (part + 1) * QB - 1), table)
    windows_ref[...] = table.astype(jnp.int32)
    windows_copy = pltpu.make_async_copy(windows_ref, windows_sm, small_sems.at[4])
    windows_copy.start()

    last_slot = ids_sm[lane_blocks - 1, LANES - 1] - row * slots
    speaks = (column == 0).astype(F32)
    meta_ref[0:1, :LANES] = goes_to * speaks
    meta_ref[0:1, LANES:] = counts[:1] * speaks
    meta_ref[1:2, :LANES] = named.astype(F32) * speaks
    meta_ref[1:2, LANES:] = (lane == last_slot).astype(F32) * speaks
    share_ref[...] = jnp.zeros_like(share_ref)

    own = pl.ds(pl.multiple_of(column * width, width), width)
    gain = gain_ref[...]
    piece_rows = 64
    pieces = tile // piece_rows
    lane_slices = [slice(j * LANES, (j + 1) * LANES) for j in range(D // LANES)]

    def piece_of(i, p, lanes):
        at = i * tile + p * piece_rows
        return x_ref[at:at + piece_rows, lanes].astype(F32)

    def normalise(i, group):
        means, inverses = [], []
        for p in group:
            total = functools.reduce(jnp.add, [piece_of(i, p, lanes) for lanes in lane_slices])
            mean = jnp.sum(total, axis=1, keepdims=True) * (1.0 / D)
            means.append(jnp.broadcast_to(mean, (piece_rows, LANES)))
        for p, mean in zip(group, means):
            squares = jnp.zeros((piece_rows, LANES), F32)
            for lanes in lane_slices:
                centered = piece_of(i, p, lanes) - mean
                squares += centered * centered
            variance = jnp.sum(squares, axis=1, keepdims=True) * (1.0 / D)
            inverses.append(jnp.broadcast_to(lax.rsqrt(variance + 1e-05), (piece_rows, LANES)))
        for p, mean, inverse in zip(group, means, inverses):
            here = slice(p * piece_rows, (p + 1) * piece_rows)
            for lanes in lane_slices:
                scaled = (piece_of(i, p, lanes) - mean) * inverse * gain[:, lanes]
                normed_ref[i % 2, here, lanes] = scaled.astype(BF)

    def project(i, which):
        here = slice(i * tile, (i + 1) * tile)
        result = dot(normed_ref[i % 2], w_ref[which])
        if which == 0:
            result = result * (1.0 / math.sqrt(HEAD_DIM))
        (q_ref, k_ref, v_ref)[which][here, :] = result.astype(BF)

    groups = [range(pieces * g // 3, pieces * (g + 1) // 3) for g in range(3)]
    tokens_sum = jnp.zeros((rows, width), F32)
    for quarter in range(4):
        x_copies[quarter].wait()
        normalise(0, range(pieces * quarter // 4, pieces * (quarter + 1) // 4))
    for copy in w_copies[:3]:
        copy.wait()
    for i in range(tiles):
        if i + 1 < tiles:
            for quarter in range(4):
                x_copies[4 * (i + 1) + quarter].wait()
        for which, group in enumerate(groups):
            if i + 1 < tiles:
                normalise(i + 1, group)
            project(i, which)
        here = slice(i * tile, (i + 1) * tile)
        tokens_sum += dot(pool_ref[:, here], x_ref[here, own])
    windows_copy.wait()

    def window(block_pair, part):
        return (windows_sm[block_pair, 2 * part] // 16) * 16, windows_sm[block_pair, 2 * part + 1]

    def all_heads(block):
        at = pl.multiple_of(block * QB, QB)
        zero = jnp.zeros((QB, LANES), BF)
        left = iota((QB, LANES), 1) < HEAD_DIM
        stacked = []
        for half in range(halves):
            piece = q_ref[pl.ds(at, QB), half * LANES:(half + 1) * LANES]
            for kept in (left, jnp.logical_not(left)):
                mine = jnp.where(kept, piece, zero)
                stacked.append(jnp.concatenate([mine if h == half else zero for h in range(halves)], axis=1))
        return jnp.concatenate(stacked, axis=0)

    head_of_lane = (iota((8, width), 1) // HEAD_DIM) == (iota((8, width), 0) % heads)
    upper_rows = iota((8, width), 0) < heads

    def key_shares(raised, inverse):
        upper = inverse.astype(BF).astype(F32)
        parts = jnp.where(upper_rows, upper, inverse - upper)
        return dot(jnp.where(head_of_lane, parts, 0.0).astype(BF), raised, NT)

    def straight(blocks, begins, extent):
        padded = round_up(extent, LANES)
        step = 64
        ats = [pl.multiple_of(jnp.minimum(begin, length - extent), 16) for begin in begins]
        halves_of = [slice(half * LANES, (half + 1) * LANES) for half in range(halves)]
        for i, (block, at) in enumerate(zip(blocks, ats)):
            scores_ref[i, :extent, :] = dot(k_ref[pl.ds(at, extent), :], all_heads(block), NT)
        tops = []
        for i, (block, at) in enumerate(zip(blocks, ats)):
            mine = query_slots_ref[i % 2, pl.ds(block // 2, 1), :]
            top = [jnp.full((8, LANES), -1e30, F32) for _ in range(halves)]
            for key in range(0, extent, step):
                same = slot_ref[pl.ds(at + key, step), :] == mine
                for half, lanes in enumerate(halves_of):
                    masked = jnp.where(same, scores_ref[i, key:key + step, lanes], -1e30)
                    scores_ref[i, key:key + step, lanes] = masked
                    highest = jnp.max(masked.reshape(step // 8, 8, LANES), axis=0)
                    top[half] = jnp.maximum(top[half], highest)
            tops.append([jnp.max(t, axis=0, keepdims=True) for t in top])
        inverses = []
        for i in range(len(blocks)):
            total = [jnp.zeros((8, LANES), F32) for _ in range(halves)]
            for key in range(0, extent, step):
                for half, lanes in enumerate(halves_of):
                    raised = jnp.exp(scores_ref[i, key:key + step, lanes] - tops[i][half])
                    total[half] += jnp.sum(raised.reshape(step // 8, 8, LANES), axis=0)
                    raised_ref[i, key:key + step, lanes] = raised.astype(BF)
            if padded > extent:
                raised_ref[i, extent:padded, :] = jnp.zeros((padded - extent, width), BF)
            inverses.append(
                jnp.concatenate([1.0 / jnp.sum(t, axis=0, keepdims=True) for t in total], axis=1)
            )
        for i, at in enumerate(ats):
            shares = key_shares(raised_ref[i, :padded, :], inverses[i])
            shares = jnp.concatenate([shares, jnp.zeros((8, LANES), F32)], axis=1)
            base = pl.multiple_of((at // LANES) * LANES, LANES)
            share_ref[:, pl.ds(base, padded + LANES)] += pltpu.roll(shares, at % LANES, 1)

    def any_length(block):
        chunk = 256
        begin, end = window(block // 2, block % 2)
        first_chunk = begin // chunk
        end_chunk = (end + chunk - 1) // chunk

        def scores_at(index):
            at = pl.multiple_of(index * chunk, chunk)
            scores = dot(k_ref[pl.ds(at, chunk), :], all_heads(block), NT)
            even = query_slots_ref[0, pl.ds(block // 2, 1), :]
            odd = query_slots_ref[1, pl.ds(block // 2, 1), :]
            query_slots = jnp.where(block % 2 == 0, even, odd)
            same = slot_ref[pl.ds(at, chunk), :] == query_slots
            masked = [
                jnp.where(same, scores[:, half * LANES:(half + 1) * LANES], -1e30) for half in range(halves)
            ]
            return at, jnp.concatenate(masked, axis=1)

        def forward(index, carry):
            top, total = carry
            _, scores = scores_at(index)
            higher = jnp.maximum(top, jnp.max(scores, axis=0, keepdims=True))
            raised = jnp.sum(jnp.exp(scores - higher), axis=0, keepdims=True)
            return higher, total * jnp.exp(top - higher) + raised

        top, total = lax.fori_loop(
            first_chunk, end_chunk, forward,
            (jnp.full((1, width), -1e30, F32), jnp.zeros((1, width), F32)),
        )
        inverse = 1.0 / total

        def again(index, nothing):
            at, scores = scores_at(index)
            share_ref[:, pl.ds(at, chunk)] += key_shares(jnp.exp(scores - top).astype(BF), inverse)
            return nothing

        lax.fori_loop(first_chunk, end_chunk, again, 0)

    def group_step(group, nothing):
        blocks = [group * GROUP + i for i in range(GROUP)]
        spans = [window(group * (GROUP // 2) + i // 2, i % 2) for i in range(GROUP)]
        begins = [begin for begin, _ in spans]
        widest = functools.reduce(jnp.maximum, [end - begin for begin, end in spans])
        done = jnp.int32(0)
        for extent in EXTENTS:
            if extent > length:
                break

            @pl.when((widest > done) & (widest <= extent))
            def run(extent=extent):
                straight(blocks, begins, extent)

            done = jnp.int32(extent)

        @pl.when(widest > done)
        def slow():
            def one(index, nothing):
                any_length(group * GROUP + index)
                return nothing

            lax.fori_loop(0, GROUP, one, 0)

        return nothing

    lax.fori_loop(0, length // QB // GROUP, group_step, 0)

    shares = share_ref[:, :length]
    pool = pool_ref[...]
    weighted = jnp.concatenate(
        [pool * (shares[h:h + 1] + shares[heads + h:heads + h + 1]).astype(BF) for h in range(heads)], axis=0
    )
    every = dot(weighted, v_ref[...])
    lane_head = iota((rows, width), 1) // HEAD_DIM
    context = jnp.zeros((rows, width), F32)
    for h in range(heads):
        context = jnp.where(lane_head == h, every[h * rows:(h + 1) * rows], context)
    upper = context.astype(BF)
    lower = (context - upper.astype(F32)).astype(BF)
    w_copies[3].wait()
    sent = dot(jnp.concatenate([upper, lower], axis=0), wo_ref[...])
    sent = sent[:rows] + sent[rows:]
    for target in range(mp):
        out_ref[target] = sent[:, target * width:(target + 1) * width]
    out_ref[column] += tokens_sum
    for target in range(mp):
        for block in range(dp):
            at = block * block_rows + capacity + 1
            out_ref[target, at:at + 2, :] = meta_ref[:2, :]


def row_sums(doc_ids, assigned, tokens, ln_gain, w_query, w_key, w_value, w_out, sizes):
    length, tile, slots, capacity, block_rows, dp, mp, width, cents = sizes
    rows = dp * block_rows
    return pl.pallas_call(
        functools.partial(row_kernel, sizes),
        in_specs=[pl.BlockSpec(memory_space=pltpu.HBM)] * 8,
        out_shape=jax.ShapeDtypeStruct((mp, rows, width), F32),
        scratch_shapes=[
            pltpu.VMEM((length // LANES, LANES), jnp.int32),
            pltpu.SMEM((length // LANES, LANES), jnp.int32),
            pltpu.SMEM((1, slots), jnp.int32),
            pltpu.VMEM((1, D), F32),
            pltpu.VMEM((length, D), BF),
            pltpu.VMEM((3, D, width), BF),
            pltpu.VMEM((width, D), BF),
            pltpu.VMEM((2, tile, D), BF),
            pltpu.VMEM((length, width), BF),
            pltpu.VMEM((length, width), BF),
            pltpu.VMEM((length, width), BF),
            pltpu.VMEM((length, LANES), F32),
            pltpu.VMEM((2, length // LANES, LANES), F32),
            pltpu.VMEM((length // LANES, LANES), jnp.int32),
            pltpu.SMEM((length // LANES, LANES), jnp.int32),
            pltpu.VMEM((rows, length), BF),
            pltpu.VMEM((8, 2 * LANES), F32),
            pltpu.VMEM((8, length + 2 * LANES), F32),
            pltpu.VMEM((GROUP, EXTENTS[-1], width), F32),
            pltpu.VMEM((GROUP, EXTENTS[-1], width), BF),
            pltpu.SemaphoreType.DMA((5,)),
            pltpu.SemaphoreType.DMA((4 * length // tile,)),
            pltpu.SemaphoreType.DMA((4,)),
        ],
        compiler_params=pltpu.CompilerParams(vmem_limit_bytes=62 * 1024 * 1024),
        name="row_sums",
    )(
        doc_ids.reshape(length // LANES, LANES), assigned.reshape(1, slots), ln_gain.reshape(1, D),
        tokens, w_query, w_key, w_value, w_out,
    )


def products_kernel(
    sizes, here_ref, own_ref, cent_ref, mass_ref, pay_ref, docs_ref, near_ref, info_ref, own_out_ref
):
    length, tile, slots, capacity, block_rows, dp, mp, width, cents = sizes
    me = lax.axis_index("dp")
    rows = dp * block_rows
    lane = iota((1, LANES), 1)

    def rows_of(meta, first_row, count):
        goes_to, counts = meta[0:1, :LANES], meta[0:1, LANES:]
        named, is_last = meta[1:2, :LANES], meta[1:2, LANES:]
        held = (goes_to == (iota((count, LANES), 0) + first_row).astype(F32)).astype(F32)

        def column(values):
            return jnp.sum(held * values, axis=1, keepdims=True)

        return column(named), column(counts), column(is_last), column(jnp.ones((1, LANES), F32))

    def carry_of(source):
        block = here_ref[pl.ds(pl.multiple_of(source * block_rows, 8), block_rows), :]
        counts = block[capacity + 1:capacity + 2, LANES:]
        count = jnp.sum(jnp.where(lane == slots, counts, 0.0), axis=1, keepdims=True)
        return block[capacity:capacity + 1, :], count

    columns = []
    for source in range(dp):
        base = source * block_rows
        block = here_ref[base:base + block_rows, :]
        meta = block[capacity + 1:capacity + 3, :]
        named, counts, is_last, held = rows_of(meta, me * block_rows, block_rows)
        sums = jnp.where(held > 0, block, 0.0)
        if source < dp - 1:
            carry, carry_count = carry_of(source + 1)
            sums = sums + is_last * carry
            counts = counts + is_last * carry_count
        docs_ref[base:base + block_rows, :] = sums
        columns.append((named - (me * cents).astype(F32), counts, held))
    local = jnp.concatenate([c[0] for c in columns], axis=0)
    counts = jnp.concatenate([c[1] for c in columns], axis=0)
    held = jnp.concatenate([c[2] for c in columns], axis=0)
    valid = ((held > 0) & (counts > 0)).astype(F32)

    docs = docs_ref[...]
    names = (iota((rows, cents), 1).astype(F32) == local) & (valid > 0)
    names = names.astype(F32)
    mass = jnp.sum(names * mass_ref[...], axis=1, keepdims=True)
    near = pick_rows(names.astype(BF), cent_ref[...])
    near_ref[...] = near

    own = own_ref[...]
    _, own_counts, own_last, _ = rows_of(own_ref[capacity + 1:capacity + 3, :], 0, rows)
    following = jnp.minimum(me + 1, dp - 1)
    more = (me < dp - 1).astype(F32)
    carry, carry_count = carry_of(following)
    own = own + own_last * (carry * more)
    own_counts = own_counts + own_last * (carry_count * more)
    own_out_ref[...] = own

    gram = dot(docs, docs, NT, precision=lax.Precision.HIGHEST)
    spot = iota((rows, LANES), 1)
    cross = jnp.sum(near * docs, axis=1, keepdims=True)
    square = jnp.sum(near * near, axis=1, keepdims=True)
    own_square = jnp.sum(own * own, axis=1, keepdims=True)
    doc_square = jnp.sum(docs * docs, axis=1, keepdims=True)
    pay_ref[...] = jnp.zeros_like(pay_ref)
    pay_ref[:, :rows] = gram
    for i, sums in enumerate((cross, square, own_square, doc_square)):
        pay_ref[:, rows + i:rows + i + 1] = sums
    info_ref[...] = jnp.where(
        spot == 0, local, jnp.where(spot == 1, counts, jnp.where(spot == 2, valid, jnp.where(spot == 3, mass, own_counts)))
    )


def update_kernel(sizes, *refs):
    *pay_refs, docs_ref, near_ref, info_ref, own_ref, meta_ref, cent_ref, vec_ref, new_ref = refs
    length, tile, slots, capacity, block_rows, dp, mp, width, cents = sizes
    rows = dp * block_rows
    info = info_ref[...]
    local, counts, valid, mass, own_counts = (info[:, i:i + 1] for i in range(5))
    pay = functools.reduce(jnp.add, [pay_ref[...] for pay_ref in pay_refs])
    cross, square, own_square, doc_square = (pay[:, rows + i:rows + i + 1] for i in range(4))

    def scale(sums, count):
        inverse = 1.0 / jnp.maximum(count, 1.0)
        return inverse * lax.rsqrt(sums * inverse * inverse * (1.0 / D) + 1e-06)

    vectors = own_ref[...] * scale(own_square, own_counts)
    goes_to = meta_ref[capacity + 1:capacity + 2, :LANES]
    place = ((iota((rows, LANES), 0).astype(F32) == goes_to).astype(F32)).T
    vec_ref[...] = pick_rows(place[:slots].astype(BF), vectors)

    share = scale(doc_square, counts) * valid
    across = jnp.where(valid > 0, local, -1.0)
    flat = jnp.broadcast_to(across, (rows, LANES)).T[:1]
    share_flat = jnp.broadcast_to(share, (rows, LANES)).T[:1]
    cross_flat = jnp.broadcast_to(cross, (rows, LANES)).T[:1]
    same = (across == flat) & (valid > 0)
    mixed = jnp.where(same, share_flat, 0.0)
    gained = dot(mixed, docs_ref[...], precision=lax.Precision.HIGHEST)
    twice = dot(mixed, pay[:, :rows], precision=lax.Precision.HIGHEST)
    norm = (
        mass * mass * square
        + 2.0 * mass * jnp.sum(mixed * cross_flat, axis=1, keepdims=True)
        + jnp.sum(twice * mixed, axis=1, keepdims=True)
    )
    blended = mass * near_ref[...] + gained
    scaled = blended * lax.rsqrt(norm * (1.0 / D) + 1e-06)
    before = same & (iota((rows, rows), 0) < iota((rows, rows), 1))
    repeated = jnp.sum(before.astype(F32), axis=0, keepdims=True)
    target = jnp.where((flat >= 0) & (repeated < 0.5), flat, -1.0)
    hits = (iota((cents, rows), 0).astype(F32) == target).astype(F32)
    updated = pick_rows(hits.astype(BF), scaled)
    hit = jnp.sum(hits, axis=1, keepdims=True)
    new_ref[...] = jnp.where(hit > 0, updated, cent_ref[...])


def shards(
    tokens, doc_ids, ln_gain, w_query, w_key, w_value, w_out, centroids, cluster_mass, assigned
):
    length = tokens.shape[0]
    slots = assigned.shape[0]
    width = w_out.shape[0]
    cents = centroids.shape[0]
    dp = lax.axis_size("dp")
    mp = lax.axis_size("mp")
    capacity = max(2, (slots + dp - 2) // (dp - 1))
    block_rows = round_up(capacity + 3, 8)
    rows = dp * block_rows
    sizes = (length, min(1024, length), slots, capacity, block_rows, dp, mp, width, cents)
    limit = pltpu.CompilerParams(vmem_limit_bytes=48 * 1024 * 1024)

    partial = row_sums(doc_ids, assigned, tokens, ln_gain, w_query, w_key, w_value, w_out, sizes)
    shared = lax.all_to_all(partial, "mp", split_axis=0, concat_axis=0, tiled=True)
    own = jnp.sum(shared, axis=0)
    here = lax.all_to_all(own, "dp", split_axis=0, concat_axis=0, tiled=True)

    pay, docs, near, info, own_sums = pl.pallas_call(
        functools.partial(products_kernel, sizes),
        out_shape=(
            jax.ShapeDtypeStruct((rows, round_up(rows + 4, LANES)), F32),
            jax.ShapeDtypeStruct((rows, width), F32),
            jax.ShapeDtypeStruct((rows, width), F32),
            jax.ShapeDtypeStruct((rows, LANES), F32),
            jax.ShapeDtypeStruct((rows, width), F32),
        ),
        compiler_params=limit,
        name="products",
    )(here, own, centroids, cluster_mass.reshape(1, cents))
    pays = [pay] + [
        lax.ppermute(pay, "mp", [(i, (i + by) % mp) for i in range(mp)]) for by in range(1, mp)
    ]
    return pl.pallas_call(
        functools.partial(update_kernel, sizes),
        out_shape=(
            jax.ShapeDtypeStruct((slots, width), F32),
            jax.ShapeDtypeStruct((cents, width), F32),
        ),
        compiler_params=limit,
        name="update",
    )(*pays, docs, near, info, own_sums, own, centroids)


def solution(mesh):
    placed = (
        P("dp", None),
        P("dp"),
        P(),
        P(None, "mp"),
        P(None, "mp"),
        P(None, "mp"),
        P("mp", None),
        P("dp", "mp"),
        P("dp"),
        P("dp"),
    )
    return jax.shard_map(
        shards,
        mesh=mesh,
        in_specs=placed,
        out_specs=(P("dp", "mp"), P("dp", "mp")),
        check_vma=False,
    )
```

```python
import functools
import math

import jax
import jax.numpy as jnp
from jax import lax
from jax.experimental import pallas as pl
from jax.experimental.pallas import tpu as pltpu
from jax.sharding import PartitionSpec as P

D = 1024
HEAD_DIM = 64
QB = 64
GROUP = 8
EXTENTS = (192, 256, 320, 384, 512, 640)
LANES = 128
BF = jnp.bfloat16
F32 = jnp.float32

NN = (((1,), (0,)), ((), ()))
NT = (((1,), (1,)), ((), ()))
TN = (((0,), (0,)), ((), ()))


def dot(a, b, dims=NN, precision=None):
    return lax.dot_general(a, b, dims, preferred_element_type=F32, precision=precision)


def iota(shape, dim):
    return lax.broadcasted_iota(jnp.int32, shape, dim)


def thirds(x):
    first = x.astype(BF)
    rest = x - first.astype(F32)
    second = rest.astype(BF)
    third = (rest - second.astype(F32)).astype(BF)
    return first, second, third


def pick_rows(one_hot, x, dims=NN):
    first, second, third = thirds(x)
    return dot(one_hot, first, dims) + (dot(one_hot, second, dims) + dot(one_hot, third, dims))


def round_up(n, by):
    return (n + by - 1) // by * by


def row_kernel(
    sizes, ids_hbm, assigned_hbm, gain_hbm, x_hbm, wq_hbm, wk_hbm, wv_hbm, wo_hbm, *refs
):
    mp = sizes[6]
    out_refs = refs[:mp]
    (
        ids_ref, ids_sm, assigned_sm, gain_ref, x_ref, w_ref, wo_ref, normed_ref, q_ref, k_ref, v_ref,
        slot_ref, query_slots_ref, windows_ref, windows_sm, pool_ref, meta_ref, share_ref, scores_ref, raised_ref, small_sems, x_sems, w_sems, sent_ref,
    ) = refs[mp:]
    length, tile, slots, capacity, block_rows, dp, mp, width, cents = sizes
    tiles = length // tile
    lane_blocks = length // LANES
    rows = dp * block_rows
    heads = width // HEAD_DIM
    halves = width // LANES
    row = lax.axis_index("dp")
    column = lax.axis_index("mp")

    small_copies = [
        pltpu.make_async_copy(ids_hbm, ids_ref, small_sems.at[0]),
        pltpu.make_async_copy(ids_hbm, ids_sm, small_sems.at[1]),
        pltpu.make_async_copy(assigned_hbm, assigned_sm, small_sems.at[2]),
        pltpu.make_async_copy(gain_hbm, gain_ref, small_sems.at[3]),
    ]
    part_rows = tile // 4
    x_copies = [
        pltpu.make_async_copy(x_hbm.at[pl.ds(at, part_rows), :], x_ref.at[pl.ds(at, part_rows), :], x_sems.at[i])
        for i, at in enumerate(range(0, length, part_rows))
    ]
    w_copies = [
        pltpu.make_async_copy(w_hbm, w_ref.at[i], w_sems.at[i])
        for i, w_hbm in enumerate((wq_hbm, wk_hbm, wv_hbm))
    ] + [pltpu.make_async_copy(wo_hbm, wo_ref, w_sems.at[3])]
    for copy in small_copies + x_copies[:4]:
        copy.start()
    for copy in w_copies[:3]:
        copy.start(priority=1)
    for copy in x_copies[4:]:
        copy.start()
    w_copies[3].start(priority=1)
    for copy in small_copies:
        copy.wait()

    ids = ids_ref[...]
    local = ids - row * slots
    slot_ids = jnp.where(local < 0, slots, local)
    slot_rows = slot_ids.astype(F32)
    turned = pltpu.roll(slot_rows, QB, 1)
    front = iota(slot_rows.shape, 1) < QB
    query_slots_ref[0] = jnp.where(front, slot_rows, turned)
    query_slots_ref[1] = jnp.where(front, turned, slot_rows)

    lane = iota((1, LANES), 1)
    named = jnp.full((1, LANES), -1, jnp.int32)
    for j in range(slots):
        named = jnp.where(lane == j, assigned_sm[0, j], named)
    owner = named // cents
    wide = jnp.broadcast_to(owner.astype(F32), (LANES, LANES))
    earlier = (wide.T == wide) & (iota((LANES, LANES), 0) < iota((LANES, LANES), 1))
    rank = jnp.sum(earlier.astype(F32), axis=0, keepdims=True)
    goes_to = jnp.where(lane < slots, owner.astype(F32) * block_rows + rank, -1.0)
    goes = jnp.take_along_axis(jnp.broadcast_to(goes_to, slot_rows.shape), slot_ids, axis=1)
    row_of = iota((rows, LANES), 0)
    continued = (row_of % block_rows == capacity).astype(F32)
    row_of = row_of.astype(F32)
    lane_number = iota((8, LANES), 1).astype(F32)
    counts = jnp.zeros((8, LANES), F32)
    for block in range(lane_blocks):
        here = slice(block * LANES, (block + 1) * LANES)
        slot = slot_rows[block:block + 1, :]
        upright = jnp.broadcast_to(slot, (LANES, LANES)).T
        slot_ref[here, :] = upright
        for part in range(0, LANES, 8):
            counts += (upright[part:part + 8] == lane_number).astype(F32)
        mine = jnp.where(row_of == goes[block:block + 1, :], 1.0, 0.0)
        pool_ref[:, here] = jnp.where(slot == slots, continued, mine).astype(BF)
    counts = jnp.broadcast_to(jnp.sum(counts, axis=0, keepdims=True), (8, LANES))

    def order(shape, dim):
        slot = iota(shape, dim)
        return jnp.where(slot == slots, 0, slot + 1)

    before = (order((LANES, LANES), 0) < order((LANES, LANES), 1)) & (iota((LANES, LANES), 0) <= slots)
    before = before.astype(F32).astype(BF)
    upper = counts.astype(BF)
    starts = dot(upper, before) + dot((counts - upper.astype(F32)).astype(BF), before)

    def at_position(values, position):
        mine = iota(slot_rows.shape, 1).astype(F32) == slot_rows[:, position:position + 1]
        return jnp.sum(jnp.where(mine, values[:1], 0.0), axis=1, keepdims=True)

    spot = iota(slot_rows.shape, 1)
    table = jnp.zeros(slot_rows.shape, F32)
    for part in range(LANES // QB):
        table = jnp.where(spot == 2 * part, at_position(starts, part * QB), table)
        table = jnp.where(spot == 2 * part + 1, at_position(starts + counts, (part + 1) * QB - 1), table)
    windows_ref[...] = table.astype(jnp.int32)
    windows_copy = pltpu.make_async_copy(windows_ref, windows_sm, small_sems.at[4])
    windows_copy.start()

    last_slot = ids_sm[lane_blocks - 1, LANES - 1] - row * slots
    speaks = (column == 0).astype(F32)
    meta_ref[0:1, :LANES] = goes_to * speaks
    meta_ref[0:1, LANES:] = counts[:1] * speaks
    meta_ref[1:2, :LANES] = named.astype(F32) * speaks
    meta_ref[1:2, LANES:] = (lane == last_slot).astype(F32) * speaks
    share_ref[...] = jnp.zeros_like(share_ref)

    own = pl.ds(pl.multiple_of(column * width, width), width)
    gain = gain_ref[...]
    piece_rows = 64
    pieces = tile // piece_rows
    lane_slices = [slice(j * LANES, (j + 1) * LANES) for j in range(D // LANES)]

    def piece_of(i, p, lanes):
        at = i * tile + p * piece_rows
        return x_ref[at:at + piece_rows, lanes].astype(F32)

    def normalise(i, group):
        means, inverses = [], []
        for p in group:
            total = functools.reduce(jnp.add, [piece_of(i, p, lanes) for lanes in lane_slices])
            mean = jnp.sum(total, axis=1, keepdims=True) * (1.0 / D)
            means.append(jnp.broadcast_to(mean, (piece_rows, LANES)))
        for p, mean in zip(group, means):
            squares = jnp.zeros((piece_rows, LANES), F32)
            for lanes in lane_slices:
                centered = piece_of(i, p, lanes) - mean
                squares += centered * centered
            variance = jnp.sum(squares, axis=1, keepdims=True) * (1.0 / D)
            inverses.append(jnp.broadcast_to(lax.rsqrt(variance + 1e-05), (piece_rows, LANES)))
        for p, mean, inverse in zip(group, means, inverses):
            here = slice(p * piece_rows, (p + 1) * piece_rows)
            for lanes in lane_slices:
                scaled = (piece_of(i, p, lanes) - mean) * inverse * gain[:, lanes]
                normed_ref[i % 2, here, lanes] = scaled.astype(BF)

    def project(i, which):
        here = slice(i * tile, (i + 1) * tile)
        result = dot(normed_ref[i % 2], w_ref[which])
        if which == 0:
            result = result * (1.0 / math.sqrt(HEAD_DIM))
        (q_ref, k_ref, v_ref)[which][here, :] = result.astype(BF)

    groups = [range(pieces * g // 3, pieces * (g + 1) // 3) for g in range(3)]
    tokens_sum = jnp.zeros((rows, width), F32)
    for quarter in range(4):
        x_copies[quarter].wait()
        normalise(0, range(pieces * quarter // 4, pieces * (quarter + 1) // 4))
    for copy in w_copies[:3]:
        copy.wait()
    for i in range(tiles):
        if i + 1 < tiles:
            for quarter in range(4):
                x_copies[4 * (i + 1) + quarter].wait()
        for which, group in enumerate(groups):
            if i + 1 < tiles:
                normalise(i + 1, group)
            project(i, which)
        here = slice(i * tile, (i + 1) * tile)
        tokens_sum += dot(pool_ref[:, here], x_ref[here, own])
    windows_copy.wait()

    def window(block_pair, part):
        return (windows_sm[block_pair, 2 * part] // 16) * 16, windows_sm[block_pair, 2 * part + 1]

    def all_heads(block):
        at = pl.multiple_of(block * QB, QB)
        zero = jnp.zeros((QB, LANES), BF)
        left = iota((QB, LANES), 1) < HEAD_DIM
        stacked = []
        for half in range(halves):
            piece = q_ref[pl.ds(at, QB), half * LANES:(half + 1) * LANES]
            for kept in (left, jnp.logical_not(left)):
                mine = jnp.where(kept, piece, zero)
                stacked.append(jnp.concatenate([mine if h == half else zero for h in range(halves)], axis=1))
        return jnp.concatenate(stacked, axis=0)

    head_of_lane = (iota((8, width), 1) // HEAD_DIM) == (iota((8, width), 0) % heads)
    upper_rows = iota((8, width), 0) < heads

    def key_shares(raised, inverse):
        upper = inverse.astype(BF).astype(F32)
        parts = jnp.where(upper_rows, upper, inverse - upper)
        return dot(jnp.where(head_of_lane, parts, 0.0).astype(BF), raised, NT)

    def straight(blocks, begins, extent):
        padded = round_up(extent, LANES)
        step = 64
        ats = [pl.multiple_of(jnp.minimum(begin, length - extent), 16) for begin in begins]
        halves_of = [slice(half * LANES, (half + 1) * LANES) for half in range(halves)]
        for i, (block, at) in enumerate(zip(blocks, ats)):
            scores_ref[i, :extent, :] = dot(k_ref[pl.ds(at, extent), :], all_heads(block), NT)
        tops = []
        for i, (block, at) in enumerate(zip(blocks, ats)):
            mine = query_slots_ref[i % 2, pl.ds(block // 2, 1), :]
            top = [jnp.full((8, LANES), -1e30, F32) for _ in range(halves)]
            for key in range(0, extent, step):
                same = slot_ref[pl.ds(at + key, step), :] == mine
                for half, lanes in enumerate(halves_of):
                    masked = jnp.where(same, scores_ref[i, key:key + step, lanes], -1e30)
                    scores_ref[i, key:key + step, lanes] = masked
                    highest = jnp.max(masked.reshape(step // 8, 8, LANES), axis=0)
                    top[half] = jnp.maximum(top[half], highest)
            tops.append([jnp.max(t, axis=0, keepdims=True) for t in top])
        inverses = []
        for i in range(len(blocks)):
            total = [jnp.zeros((8, LANES), F32) for _ in range(halves)]
            for key in range(0, extent, step):
                for half, lanes in enumerate(halves_of):
                    raised = jnp.exp(scores_ref[i, key:key + step, lanes] - tops[i][half])
                    total[half] += jnp.sum(raised.reshape(step // 8, 8, LANES), axis=0)
                    raised_ref[i, key:key + step, lanes] = raised.astype(BF)
            if padded > extent:
                raised_ref[i, extent:padded, :] = jnp.zeros((padded - extent, width), BF)
            inverses.append(
                jnp.concatenate([1.0 / jnp.sum(t, axis=0, keepdims=True) for t in total], axis=1)
            )
        for i, at in enumerate(ats):
            shares = key_shares(raised_ref[i, :padded, :], inverses[i])
            shares = jnp.concatenate([shares, jnp.zeros((8, LANES), F32)], axis=1)
            base = pl.multiple_of((at // LANES) * LANES, LANES)
            share_ref[:, pl.ds(base, padded + LANES)] += pltpu.roll(shares, at % LANES, 1)

    def any_length(block):
        chunk = 256
        begin, end = window(block // 2, block % 2)
        first_chunk = begin // chunk
        end_chunk = (end + chunk - 1) // chunk

        def scores_at(index):
            at = pl.multiple_of(index * chunk, chunk)
            scores = dot(k_ref[pl.ds(at, chunk), :], all_heads(block), NT)
            even = query_slots_ref[0, pl.ds(block // 2, 1), :]
            odd = query_slots_ref[1, pl.ds(block // 2, 1), :]
            query_slots = jnp.where(block % 2 == 0, even, odd)
            same = slot_ref[pl.ds(at, chunk), :] == query_slots
            masked = [
                jnp.where(same, scores[:, half * LANES:(half + 1) * LANES], -1e30) for half in range(halves)
            ]
            return at, jnp.concatenate(masked, axis=1)

        def forward(index, carry):
            top, total = carry
            _, scores = scores_at(index)
            higher = jnp.maximum(top, jnp.max(scores, axis=0, keepdims=True))
            raised = jnp.sum(jnp.exp(scores - higher), axis=0, keepdims=True)
            return higher, total * jnp.exp(top - higher) + raised

        top, total = lax.fori_loop(
            first_chunk, end_chunk, forward,
            (jnp.full((1, width), -1e30, F32), jnp.zeros((1, width), F32)),
        )
        inverse = 1.0 / total

        def again(index, nothing):
            at, scores = scores_at(index)
            share_ref[:, pl.ds(at, chunk)] += key_shares(jnp.exp(scores - top).astype(BF), inverse)
            return nothing

        lax.fori_loop(first_chunk, end_chunk, again, 0)

    def group_step(group, nothing):
        blocks = [group * GROUP + i for i in range(GROUP)]
        spans = [window(group * (GROUP // 2) + i // 2, i % 2) for i in range(GROUP)]
        begins = [begin for begin, _ in spans]
        widest = functools.reduce(jnp.maximum, [end - begin for begin, end in spans])
        done = jnp.int32(0)
        for extent in EXTENTS:
            if extent > length:
                break

            @pl.when((widest > done) & (widest <= extent))
            def run(extent=extent):
                straight(blocks, begins, extent)

            done = jnp.int32(extent)

        @pl.when(widest > done)
        def slow():
            def one(index, nothing):
                any_length(group * GROUP + index)
                return nothing

            lax.fori_loop(0, GROUP, one, 0)

        return nothing

    lax.fori_loop(0, length // QB // GROUP, group_step, 0)

    shares = share_ref[:, :length]
    pool = pool_ref[...]
    weighted = jnp.concatenate(
        [pool * (shares[h:h + 1] + shares[heads + h:heads + h + 1]).astype(BF) for h in range(heads)], axis=0
    )
    every = dot(weighted, v_ref[...])
    lane_head = iota((rows, width), 1) // HEAD_DIM
    context = jnp.zeros((rows, width), F32)
    for h in range(heads):
        context = jnp.where(lane_head == h, every[h * rows:(h + 1) * rows], context)
    upper = context.astype(BF)
    lower = (context - upper.astype(F32)).astype(BF)
    w_copies[3].wait()
    sent = dot(jnp.concatenate([upper, lower], axis=0), wo_ref[...])
    sent = sent[:rows] + sent[rows:]
    for target in range(mp):
        sent_ref[(target - column + mp) % mp] = sent[:, target * width:(target + 1) * width]
    sent_ref[0] += tokens_sum
    for by, out_ref in enumerate(out_refs):
        out_ref[...] = sent_ref[by]
        for block in range(dp):
            at = block * block_rows + capacity + 1
            out_ref[at:at + 2, :] = meta_ref[:2, :]


def row_sums(doc_ids, assigned, tokens, ln_gain, w_query, w_key, w_value, w_out, sizes):
    length, tile, slots, capacity, block_rows, dp, mp, width, cents = sizes
    rows = dp * block_rows
    return pl.pallas_call(
        functools.partial(row_kernel, sizes),
        in_specs=[pl.BlockSpec(memory_space=pltpu.HBM)] * 8,
        out_shape=[jax.ShapeDtypeStruct((rows, width), F32)] * mp,
        scratch_shapes=[
            pltpu.VMEM((length // LANES, LANES), jnp.int32),
            pltpu.SMEM((length // LANES, LANES), jnp.int32),
            pltpu.SMEM((1, slots), jnp.int32),
            pltpu.VMEM((1, D), F32),
            pltpu.VMEM((length, D), BF),
            pltpu.VMEM((3, D, width), BF),
            pltpu.VMEM((width, D), BF),
            pltpu.VMEM((2, tile, D), BF),
            pltpu.VMEM((length, width), BF),
            pltpu.VMEM((length, width), BF),
            pltpu.VMEM((length, width), BF),
            pltpu.VMEM((length, LANES), F32),
            pltpu.VMEM((2, length // LANES, LANES), F32),
            pltpu.VMEM((length // LANES, LANES), jnp.int32),
            pltpu.SMEM((length // LANES, LANES), jnp.int32),
            pltpu.VMEM((rows, length), BF),
            pltpu.VMEM((8, 2 * LANES), F32),
            pltpu.VMEM((8, length + 2 * LANES), F32),
            pltpu.VMEM((GROUP, EXTENTS[-1], width), F32),
            pltpu.VMEM((GROUP, EXTENTS[-1], width), BF),
            pltpu.SemaphoreType.DMA((5,)),
            pltpu.SemaphoreType.DMA((4 * length // tile,)),
            pltpu.SemaphoreType.DMA((4,)),
            pltpu.VMEM((mp, rows, width), F32),
        ],
        compiler_params=pltpu.CompilerParams(vmem_limit_bytes=62 * 1024 * 1024),
        name="row_sums",
    )(
        doc_ids.reshape(length // LANES, LANES), assigned.reshape(1, slots), ln_gain.reshape(1, D),
        tokens, w_query, w_key, w_value, w_out,
    )


def products_kernel(
    sizes, here_ref, own_ref, cent_ref, mass_ref, pay_ref, docs_ref, near_ref, info_ref, own_out_ref
):
    length, tile, slots, capacity, block_rows, dp, mp, width, cents = sizes
    me = lax.axis_index("dp")
    rows = dp * block_rows
    lane = iota((1, LANES), 1)

    def rows_of(meta, first_row, count):
        goes_to, counts = meta[0:1, :LANES], meta[0:1, LANES:]
        named, is_last = meta[1:2, :LANES], meta[1:2, LANES:]
        held = (goes_to == (iota((count, LANES), 0) + first_row).astype(F32)).astype(F32)

        def column(values):
            return jnp.sum(held * values, axis=1, keepdims=True)

        return column(named), column(counts), column(is_last), column(jnp.ones((1, LANES), F32))

    def carry_of(source):
        block = here_ref[pl.ds(pl.multiple_of(source * block_rows, 8), block_rows), :]
        counts = block[capacity + 1:capacity + 2, LANES:]
        count = jnp.sum(jnp.where(lane == slots, counts, 0.0), axis=1, keepdims=True)
        return block[capacity:capacity + 1, :], count

    columns = []
    for source in range(dp):
        base = source * block_rows
        block = here_ref[base:base + block_rows, :]
        meta = block[capacity + 1:capacity + 3, :]
        named, counts, is_last, held = rows_of(meta, me * block_rows, block_rows)
        sums = jnp.where(held > 0, block, 0.0)
        if source < dp - 1:
            carry, carry_count = carry_of(source + 1)
            sums = sums + is_last * carry
            counts = counts + is_last * carry_count
        docs_ref[base:base + block_rows, :] = sums
        columns.append((named - (me * cents).astype(F32), counts, held))
    local = jnp.concatenate([c[0] for c in columns], axis=0)
    counts = jnp.concatenate([c[1] for c in columns], axis=0)
    held = jnp.concatenate([c[2] for c in columns], axis=0)
    valid = ((held > 0) & (counts > 0)).astype(F32)

    docs = docs_ref[...]
    names = (iota((rows, cents), 1).astype(F32) == local) & (valid > 0)
    names = names.astype(F32)
    mass = jnp.sum(names * mass_ref[...], axis=1, keepdims=True)
    near = pick_rows(names.astype(BF), cent_ref[...])
    near_ref[...] = near

    own = own_ref[...]
    _, own_counts, own_last, _ = rows_of(own_ref[capacity + 1:capacity + 3, :], 0, rows)
    following = jnp.minimum(me + 1, dp - 1)
    more = (me < dp - 1).astype(F32)
    carry, carry_count = carry_of(following)
    own = own + own_last * (carry * more)
    own_counts = own_counts + own_last * (carry_count * more)
    own_out_ref[...] = own

    gram = dot(docs, docs, NT, precision=lax.Precision.HIGHEST)
    spot = iota((rows, LANES), 1)
    cross = jnp.sum(near * docs, axis=1, keepdims=True)
    square = jnp.sum(near * near, axis=1, keepdims=True)
    own_square = jnp.sum(own * own, axis=1, keepdims=True)
    doc_square = jnp.sum(docs * docs, axis=1, keepdims=True)
    pay_ref[...] = jnp.zeros_like(pay_ref)
    pay_ref[:, :rows] = gram
    for i, sums in enumerate((cross, square, own_square, doc_square)):
        pay_ref[:, rows + i:rows + i + 1] = sums
    info_ref[...] = jnp.where(
        spot == 0, local, jnp.where(spot == 1, counts, jnp.where(spot == 2, valid, jnp.where(spot == 3, mass, own_counts)))
    )


def update_kernel(sizes, *refs):
    *pay_refs, docs_ref, near_ref, info_ref, own_ref, meta_ref, cent_ref, vec_ref, new_ref = refs
    length, tile, slots, capacity, block_rows, dp, mp, width, cents = sizes
    rows = dp * block_rows
    info = info_ref[...]
    local, counts, valid, mass, own_counts = (info[:, i:i + 1] for i in range(5))
    pay = functools.reduce(jnp.add, [pay_ref[...] for pay_ref in pay_refs])
    cross, square, own_square, doc_square = (pay[:, rows + i:rows + i + 1] for i in range(4))

    def scale(sums, count):
        inverse = 1.0 / jnp.maximum(count, 1.0)
        return inverse * lax.rsqrt(sums * inverse * inverse * (1.0 / D) + 1e-06)

    vectors = own_ref[...] * scale(own_square, own_counts)
    goes_to = meta_ref[capacity + 1:capacity + 2, :LANES]
    place = ((iota((rows, LANES), 0).astype(F32) == goes_to).astype(F32)).T
    vec_ref[...] = pick_rows(place[:slots].astype(BF), vectors)

    share = scale(doc_square, counts) * valid
    across = jnp.where(valid > 0, local, -1.0)
    flat = jnp.broadcast_to(across, (rows, LANES)).T[:1]
    share_flat = jnp.broadcast_to(share, (rows, LANES)).T[:1]
    cross_flat = jnp.broadcast_to(cross, (rows, LANES)).T[:1]
    same = (across == flat) & (valid > 0)
    mixed = jnp.where(same, share_flat, 0.0)
    gained = dot(mixed, docs_ref[...], precision=lax.Precision.HIGHEST)
    twice = dot(mixed, pay[:, :rows], precision=lax.Precision.HIGHEST)
    norm = (
        mass * mass * square
        + 2.0 * mass * jnp.sum(mixed * cross_flat, axis=1, keepdims=True)
        + jnp.sum(twice * mixed, axis=1, keepdims=True)
    )
    blended = mass * near_ref[...] + gained
    scaled = blended * lax.rsqrt(norm * (1.0 / D) + 1e-06)
    before = same & (iota((rows, rows), 0) < iota((rows, rows), 1))
    repeated = jnp.sum(before.astype(F32), axis=0, keepdims=True)
    target = jnp.where((flat >= 0) & (repeated < 0.5), flat, -1.0)
    hits = (iota((cents, rows), 0).astype(F32) == target).astype(F32)
    updated = pick_rows(hits.astype(BF), scaled)
    hit = jnp.sum(hits, axis=1, keepdims=True)
    new_ref[...] = jnp.where(hit > 0, updated, cent_ref[...])


def shards(
    tokens, doc_ids, ln_gain, w_query, w_key, w_value, w_out, centroids, cluster_mass, assigned
):
    length = tokens.shape[0]
    slots = assigned.shape[0]
    width = w_out.shape[0]
    cents = centroids.shape[0]
    dp = lax.axis_size("dp")
    mp = lax.axis_size("mp")
    capacity = max(2, (slots + dp - 2) // (dp - 1))
    block_rows = round_up(capacity + 3, 8)
    rows = dp * block_rows
    sizes = (length, min(1024, length), slots, capacity, block_rows, dp, mp, width, cents)
    limit = pltpu.CompilerParams(vmem_limit_bytes=48 * 1024 * 1024)

    partial = row_sums(doc_ids, assigned, tokens, ln_gain, w_query, w_key, w_value, w_out, sizes)
    own = partial[0]
    for by in range(1, mp):
        own = own + lax.ppermute(partial[by], "mp", [(i, (i + by) % mp) for i in range(mp)])
    here = lax.all_to_all(own, "dp", split_axis=0, concat_axis=0, tiled=True)

    pay, docs, near, info, own_sums = pl.pallas_call(
        functools.partial(products_kernel, sizes),
        out_shape=(
            jax.ShapeDtypeStruct((rows, round_up(rows + 4, LANES)), F32),
            jax.ShapeDtypeStruct((rows, width), F32),
            jax.ShapeDtypeStruct((rows, width), F32),
            jax.ShapeDtypeStruct((rows, LANES), F32),
            jax.ShapeDtypeStruct((rows, width), F32),
        ),
        compiler_params=limit,
        name="products",
    )(here, own, centroids, cluster_mass.reshape(1, cents))
    pays = [pay] + [
        lax.ppermute(pay, "mp", [(i, (i + by) % mp) for i in range(mp)]) for by in range(1, mp)
    ]
    return pl.pallas_call(
        functools.partial(update_kernel, sizes),
        out_shape=(
            jax.ShapeDtypeStruct((slots, width), F32),
            jax.ShapeDtypeStruct((cents, width), F32),
        ),
        compiler_params=limit,
        name="update",
    )(*pays, docs, near, info, own_sums, own, centroids)


def solution(mesh):
    placed = (
        P("dp", None),
        P("dp"),
        P(),
        P(None, "mp"),
        P(None, "mp"),
        P(None, "mp"),
        P("mp", None),
        P("dp", "mp"),
        P("dp"),
        P("dp"),
    )
    return jax.shard_map(
        shards,
        mesh=mesh,
        in_specs=placed,
        out_specs=(P("dp", "mp"), P("dp", "mp")),
        check_vma=False,
    )
```
